128 devices in a mesh: along: 32 (over z, y, core), across: 4 (over x).
Axes of the slice: x: 4, y: 4, z: 4, core: 2. Of those that a mesh axis runs over, the one named last changes fastest.
Arguments:
- elevation: float32 [64, 512, 512], P(None, 'along', 'across'), may hold values from -6 to 6
- velocity_pot: float32 [64, 512, 512], P(None, 'along', 'across'), may hold values from -6 to 6
- surface_coef: float32 [512, 512], P('along', 'across'), may hold values from 0.1 to 1
- panel_slot: int32 [512, 512], P('along', 'across'), may hold values from 0 to 262143, as said below
- near_blocks: bfloat16 [1024, 9, 256, 256], P(('along', 'across')), may hold values from -0.125 to 0.125
- near_cols: int32 [1024, 9], P(('along', 'across')), may hold values from 0 to 1023, as said below
- far_v: bfloat16 [16384, 32, 256], P(('along', 'across')), may hold values from -0.375 to 0.375
- far_u: bfloat16 [16384, 32, 256], P(('along', 'across')), may hold values from -0.25 to 0.25
- far_rows: int32 [16384], P(('along', 'across')), may hold values from 0 to 1023, as said below
- far_cols: int32 [16384], P(('along', 'across')), may hold values from 0 to 1023, as said below
Outputs:
- eta_next: float32 [64, 512, 512], P(None, 'along', 'across')
- potential: bfloat16 [64, 512, 512], P(None, 'along', 'across')
The draws below stay inside these ranges and needn't reach their ends.
Inputs may be any that keep to these rules, and one draw needn't show every extreme that they name: `panel_slot`: A permutation of the positions; cluster c spans positions c * 256 to c * 256 + 255 and belongs to device c // 8 (devices numbered along-major). The panels of each device's tile take exactly 16 positions in each device's range. `near_cols`: entry k = 0 is the row cluster itself; the others are distinct clusters whose index differs from the row's by at most 8 modulo 1024. Pair p's column cluster is owned by the device holding pair p: far_cols[p] // 8 == p // 128. `far_rows`: of the pairs held by one device, at most 2 have row clusters owned by any one device, and in every draw some device receives exactly 2 from every sender; some devices receive none.
All inputs are finite; a program needn't handle non-finite values.
Results may differ from the reference program's by a relative error of at most 0.0058.
Values may be sent and summed in bfloat16 or wider, within the bound.
No kernel may reach another device: no remote copies, remote signals or barrier semaphores. Data moves between devices by JAX's collectives and lax.ppermute only.
A program may use at most 128 MiB of HBM per device.

```python
import math
import jax
import jax.numpy as jnp
from jax import lax

TX = 16
TY = 128
NV = 64
CL = 256
R = 32
NNB = 9
FAR_DEV = 128
NX = 512
NY = 512
CPD = 8
CLUSTERS = 1024
FAR = 16384
FCAP = 2


def draw_panel_slot(key, part):
    key = jax.random.fold_in(key, 11)
    owners = NX // TX * (NY // TY)
    panels = TX * TY
    share = panels // owners
    owner_keys = jax.random.split(jax.random.fold_in(key, 1), owners)
    orders = jax.vmap(lambda k: jax.random.permutation(k, panels))(owner_keys)
    per_source = orders.reshape(owners, owners, share) + (jnp.arange(owners) * panels)[:, None, None]
    per_source = per_source.transpose(1, 0, 2).reshape(owners, panels)
    source_keys = jax.random.split(jax.random.fold_in(key, 2), owners)
    shuffled = jax.vmap(lambda k, row: jax.random.permutation(k, row))(source_keys, per_source)
    grid = shuffled.reshape(NX // TX, NY // TY, TX, TY).transpose(0, 2, 1, 3).reshape(NX, NY)
    return grid.astype(jnp.int32)


def draw_near_cols(key, part):
    key = jax.random.fold_in(key, 12)
    choices_pool = jnp.concatenate([jnp.arange(-CPD, 0), jnp.arange(1, CPD + 1)]).astype(jnp.int32)
    row_keys = jax.random.split(key, CLUSTERS)
    chosen = jax.vmap(lambda k: jax.random.permutation(k, choices_pool)[:NNB - 1])(row_keys)
    offsets = jnp.concatenate([jnp.zeros((CLUSTERS, 1), jnp.int32), chosen], axis=1)
    columns = (jnp.arange(CLUSTERS, dtype=jnp.int32)[:, None] + offsets) % CLUSTERS
    return columns.astype(jnp.int32)


def draw_far_rows(key, part):
    key = jax.random.fold_in(key, 13)
    owners = CLUSTERS // CPD
    slot_count = owners * FCAP
    popular = jax.random.randint(jax.random.fold_in(key, 1), (owners,), 0, 3)
    target_of_slot = jnp.arange(slot_count, dtype=jnp.int32) // FCAP

    def one_source(source_key):
        raw = jax.random.randint(jax.random.fold_in(source_key, 1), (slot_count,), 0, 2 ** 18)
        score = ((2 - popular[target_of_slot]) * 2 ** 18 + raw) * slot_count + jnp.arange(slot_count, dtype=jnp.int32)
        picked = jnp.argsort(score, stable=True)[:FAR_DEV]
        picked = jax.random.permutation(jax.random.fold_in(source_key, 2), picked)
        return picked // FCAP
    source_keys = jax.random.split(jax.random.fold_in(key, 2), owners)
    targets = jax.vmap(one_source)(source_keys)
    within = jax.random.randint(jax.random.fold_in(key, 3), (owners, FAR_DEV), 0, CPD)
    return (targets * CPD + within).reshape(FAR).astype(jnp.int32)


def draw_far_cols(key, part):
    key = jax.random.fold_in(key, 14)
    holder = jnp.arange(FAR, dtype=jnp.int32) // FAR_DEV
    within = jax.random.randint(key, (FAR,), 0, CPD)
    return (holder * CPD + within).astype(jnp.int32)


def level_of(own_key, dims, cuts, low, largest):
    loudness = 1.0
    for dim, parts in cuts:
        draws = jax.random.uniform(jax.random.fold_in(jax.random.fold_in(own_key, 6), dim), (parts,), jnp.float32, low / len(cuts), largest / len(cuts))
        loudness = loudness * jnp.repeat(jnp.exp(draws), dims[dim] // parts).reshape((-1,) + (1,) * (len(dims) - 1 - dim))
    return loudness


def gaussian(rng, extent, deviation, bound, cuts=(), kind=jnp.bfloat16):
    factor_of = level_of(rng, extent, cuts, -0.22, 0.18) if cuts else 1.0
    array = jax.random.normal(rng, extent, jnp.float32) * deviation * factor_of
    return jnp.minimum(jnp.maximum(array, -bound), bound).astype(kind)


def setup_inputs(seed: int = 0) -> dict:
    key_list = jax.random.split(jax.random.key(seed), 11)
    return {
        "elevation": gaussian(key_list[0], (NV, NX, NY), 1.0, 6.0, ((1, 32), (2, 4)), jnp.float32),
        "velocity_pot": gaussian(key_list[1], (NV, NX, NY), 1.0, 6.0, ((1, 32), (2, 4)), jnp.float32),
        "surface_coef": jnp.clip(jnp.exp(math.log(1.0) - 2.3025851 * jax.random.uniform(key_list[2], (NX, NY), jnp.float32) ** level_of(key_list[2], (NX, NY), ((0, 32), (1, 4)), -0.2, 0.2)), 0.1, 1.0),
        "panel_slot": draw_panel_slot(jax.random.fold_in(key_list[10], 71), 0),
        "near_blocks": gaussian(key_list[4], (CLUSTERS, NNB, CL, CL), (NNB * CL) ** -0.5, 0.125, ((0, 128),)),
        "near_cols": draw_near_cols(jax.random.fold_in(key_list[10], 71), 0),
        "far_v": gaussian(key_list[6], (FAR, R, CL), CL ** -0.5, 0.375, ((0, 128),)),
        "far_u": gaussian(key_list[7], (FAR, R, CL), (R * FAR_DEV // CPD) ** -0.5, 0.25, ((0, 128),)),
        "far_rows": draw_far_rows(jax.random.fold_in(key_list[10], 71), 0),
        "far_cols": draw_far_cols(jax.random.fold_in(key_list[10], 71), 0),
    }


def offset_view(field, step_x, step_y):
    return field[:, 2 + step_x: field.shape[1] - 2 + step_x, 2 + step_y: field.shape[2] - 2 + step_y]


def upwind(field):
    return 0.5 * (3.0 * offset_view(field, 0, 0) - 4.0 * offset_view(field, -1, 0) + offset_view(field, -2, 0))


def transverse(field):
    return (offset_view(field, 0, -2) - 8.0 * offset_view(field, 0, -1) + 8.0 * offset_view(field, 0, 1) - offset_view(field, 0, 2)) / 12.0


def curvature(field):
    return offset_view(field, 1, 0) + offset_view(field, -1, 0) + offset_view(field, 0, 1) + offset_view(field, 0, -1) - 4.0 * offset_view(field, 0, 0)


def surface_step(padded, surface_coef):
    eta_pad = padded[0]
    phi_pad = padded[1]
    eta_next = offset_view(eta_pad, 0, 0) - 0.4 * upwind(eta_pad) + 0.3 * transverse(eta_pad) + surface_coef * curvature(phi_pad)
    source = offset_view(phi_pad, 0, 0) - 0.4 * upwind(phi_pad) + 0.3 * transverse(phi_pad) - 0.5 * eta_next
    return eta_next, source


def reference(elevation, velocity_pot, surface_coef, panel_slot, near_blocks, near_cols, far_v, far_u, far_rows, far_cols):
    padded = jnp.pad(jnp.stack([elevation, velocity_pot]), ((0, 0), (0, 0), (2, 2), (2, 2)))
    eta_next, source = surface_step(padded, surface_coef)
    flat_source = source.astype(jnp.bfloat16).reshape(NV, NX * NY)
    slots = panel_slot.reshape(NX * NY)
    ordered = jnp.zeros_like(flat_source).at[:, slots].set(flat_source)
    clustered = ordered.reshape(NV, CLUSTERS, CL).transpose(1, 0, 2)

    def near_one(index):
        columns = near_cols[index]
        block = near_blocks[index].astype(jnp.float32)
        sources = clustered[columns].astype(jnp.float32)
        return jnp.einsum('kij,kvj->vi', block, sources)

    near_pot = lax.map(near_one, jnp.arange(CLUSTERS))
    blocks = FAR // FAR_DEV

    def far_block(total, pieces):
        rows, columns, basis_v, basis_u = pieces
        sources = clustered[columns].astype(jnp.float32)
        coeff = jnp.einsum('fvj,frj->fvr', sources, basis_v.astype(jnp.float32)).astype(jnp.bfloat16)
        term = jnp.einsum('fvr,frj->fvj', coeff.astype(jnp.float32), basis_u.astype(jnp.float32)).astype(jnp.bfloat16)
        return total.at[rows].add(term.astype(jnp.float32)), None

    start = jnp.zeros((CLUSTERS, NV, CL), jnp.float32)
    far_pot, unused = lax.scan(far_block, start, (far_rows.reshape(blocks, FAR_DEV), far_cols.reshape(blocks, FAR_DEV), far_v.reshape(blocks, FAR_DEV, R, CL), far_u.reshape(blocks, FAR_DEV, R, CL)))
    total = (near_pot + far_pot).astype(jnp.bfloat16)
    flat_total = total.transpose(1, 0, 2).reshape(NV, NX * NY)
    potential = flat_total[:, slots].reshape(NV, NX, NY)
    return eta_next, potential
```

```python
import jax
import jax.numpy as jnp
from jax import lax
from jax.sharding import PartitionSpec as P

CL = 256
BOTH = ("along", "across")


def halo(elevation, velocity_pot):
    n, m = lax.axis_size("along"), lax.axis_size("across")
    down = [(i, i + 1) for i in range(n - 1)]
    up = [(i + 1, i) for i in range(n - 1)]
    right = [(i, i + 1) for i in range(m - 1)]
    left = [(i + 1, i) for i in range(m - 1)]
    both = jnp.stack([elevation, velocity_pot])
    above = lax.ppermute(both[:, :, -2:, :], "along", down)
    below = lax.ppermute(velocity_pot[:, :1, :], "along", up)
    west = lax.ppermute(both[:, :, :, -2:], "across", right)
    east = lax.ppermute(both[:, :, :, :2], "across", left)
    return above, below, west, east


def surface_step(elevation, velocity_pot, coef, above, below, west, east):
    def up_x(f, a):
        g = jnp.concatenate([a, f], axis=1)
        return 0.5 * (3.0 * f - 4.0 * g[:, 1:-1] + g[:, :-2])

    def trans(f, w, e):
        g = jnp.concatenate([w, f, e], axis=2)
        return (g[:, :, :-4] - 8.0 * g[:, :, 1:-3] + 8.0 * g[:, :, 3:-1] - g[:, :, 4:]) / 12.0

    gx = jnp.concatenate([above[1][:, 1:], velocity_pot, below], axis=1)
    gy = jnp.concatenate([west[1][:, :, 1:], velocity_pot, east[1][:, :, :1]], axis=2)
    curv = gx[:, 2:] + gx[:, :-2] + gy[:, :, 2:] + gy[:, :, :-2] - 4.0 * velocity_pot
    eta = (
        elevation
        - 0.4 * up_x(elevation, above[0])
        + 0.3 * trans(elevation, west[0], east[0])
        + coef * curv
    )
    source = (
        velocity_pot
        - 0.4 * up_x(velocity_pot, above[1])
        + 0.3 * trans(velocity_pot, west[1], east[1])
        - 0.5 * eta
    )
    return eta, source.astype(jnp.bfloat16)


def rank_within(keys, count, block):
    hits = (keys.reshape(-1, block)[:, :, None] == jnp.arange(count)).astype(jnp.bfloat16)
    strict = jnp.tril(jnp.ones((block, block), jnp.bfloat16), -1)
    within = jnp.einsum("ij,bjd->bid", strict, hits, preferred_element_type=jnp.float32)
    sums = jnp.sum(hits.astype(jnp.float32), axis=1)
    blocks = hits.shape[0]
    before = jnp.tril(jnp.ones((blocks, blocks), jnp.float32), -1)
    offset = jnp.sum(before[:, :, None] * sums[None], axis=1)
    rank = jnp.sum(hits.astype(jnp.float32) * (within + offset[:, None, :]), axis=2)
    return rank.reshape(-1).astype(jnp.int32)


def one_hot(index, count):
    return (index[..., None] == jnp.arange(count, dtype=jnp.int32)).astype(jnp.bfloat16)


def dot(spec, a, b):
    return jnp.einsum(spec, a, b, preferred_element_type=jnp.float32)


def body(
    elevation,
    velocity_pot,
    surface_coef,
    panel_slot,
    near_blocks,
    near_cols,
    far_v,
    far_u,
    far_rows,
    far_cols,
):
    waves, tile_x, tile_y = elevation.shape
    panels = tile_x * tile_y
    owners = lax.axis_size(BOTH)
    per_owner = panels // CL
    clusters = per_owner * owners
    me = lax.axis_index(BOTH)
    pairs, rank_r = far_rows.shape[0], far_u.shape[1]
    bf16 = jnp.bfloat16

    all_rows = lax.all_gather(far_rows, BOTH).reshape(owners, pairs)
    above, below, west, east = halo(elevation, velocity_pot)

    target = far_rows // per_owner
    slot = 2 * target + rank_within(target, owners, pairs)
    place = one_hot(slot, 2 * owners).T
    u_out = dot("sp,prj->srj", place, far_u).astype(bf16).reshape(owners, 2, rank_r, CL)
    u_in = lax.all_to_all(u_out, BOTH, split_axis=0, concat_axis=0, tiled=True)

    flat_slot = panel_slot.reshape(panels)
    dest = flat_slot // panels
    local = flat_slot % panels
    rank = rank_within(dest, owners, 256)
    half, row = rank // 8, dest * 8 + rank % 8
    sender = one_hot(row, owners * 8).T

    eta, source = surface_step(elevation, velocity_pot, surface_coef, above, below, west, east)
    flat = source.reshape(waves, panels)
    zero = jnp.zeros((), bf16)
    info = jnp.stack([local // 128, local % 128]).astype(bf16)
    first = half == 0
    stacked = jnp.concatenate(
        [
            jnp.where(first, flat, zero),
            jnp.where(first, zero, flat),
            jnp.where(first, info, zero),
            jnp.where(first, zero, info),
            jnp.zeros((124, panels), bf16),
        ]
    )
    payload = dot("rp,vp->rv", sender, stacked).astype(bf16).reshape(owners, 8, 256)
    arrived = lax.all_to_all(payload, BOTH, split_axis=0, concat_axis=0, tiled=True)
    arrived = arrived.reshape(owners * 8, 256)
    notes = arrived[:, 128:132].astype(jnp.int32)
    slot_a = notes[:, 0] * 128 + notes[:, 1]
    slot_b = notes[:, 2] * 128 + notes[:, 3]
    hot_a, hot_b = one_hot(slot_a, panels), one_hot(slot_b, panels)
    clustered = (
        dot("av,as->vs", arrived[:, :64], hot_a) + dot("av,as->vs", arrived[:, 64:128], hot_b)
    ).astype(bf16)
    clustered = clustered.reshape(waves, per_owner, CL).transpose(1, 0, 2)

    col = far_cols - me * per_owner
    pair_sources = dot("pc,cvj->pvj", one_hot(col, per_owner), clustered).astype(bf16)
    coeff = dot("prj,pvj->prv", far_v, pair_sources).astype(bf16)
    c_out = dot("sp,prv->srv", place, coeff).astype(bf16)
    c_out = c_out.reshape(owners, 2, rank_r, waves).transpose(0, 2, 1, 3)
    c_out = c_out.reshape(owners, rank_r, 2 * waves)
    c_in = lax.all_to_all(c_out, BOTH, split_axis=0, concat_axis=0, tiled=True)

    ring = [(i, (i + 1) % owners) for i in range(owners)]
    back = [(j, i) for i, j in ring]
    before = lax.ppermute(clustered, BOTH, ring)
    after = lax.ppermute(clustered, BOTH, back)
    widened = jnp.concatenate([before, clustered, after])
    relative = (near_cols - (me * per_owner - per_owner)) % clusters
    near_sources = widened[relative]
    near_pot = dot("cnij,cnvj->cvi", near_blocks, near_sources)

    hits = (all_rows // per_owner) == me
    order = jnp.arange(pairs, dtype=jnp.int32) * per_owner + all_rows % per_owner
    lowest = jnp.min(jnp.where(hits, order, pairs * per_owner), axis=1)
    highest = jnp.max(jnp.where(hits, order, -1), axis=1)
    row_a = jnp.where(lowest < pairs * per_owner, lowest % per_owner, -1)
    row_b = jnp.where(highest > lowest, highest % per_owner, -1)
    rows = jnp.stack([row_a, row_b], axis=1)
    mask = one_hot(rows, per_owner)
    c_in = c_in.reshape(owners, rank_r, 2, waves)
    masked = c_in[:, :, :, None, :] * mask[:, None, :, :, None]
    far_pot = dot("srkcv,skrj->cvj", masked, u_in)

    total = (near_pot + far_pot).astype(bf16)
    flat_total = total.transpose(1, 0, 2).reshape(waves, panels)
    home_a = dot("as,vs->av", hot_a, flat_total)
    home_b = dot("as,vs->av", hot_b, flat_total)
    home = jnp.concatenate([home_a, home_b], axis=1).astype(bf16).reshape(owners, 8, 2 * waves)
    returned = lax.all_to_all(home, BOTH, split_axis=0, concat_axis=0, tiled=True)
    returned = returned.reshape(owners * 8, 2 * waves)
    picked = dot("rv,rp->vp", returned, sender)
    potential = jnp.where(first, picked[:waves], picked[waves:]).astype(bf16)
    return (eta, potential.reshape(waves, tile_x, tile_y))


def solution(mesh):
    in_specs = (
        P(None, "along", "across"),
        P(None, "along", "across"),
        P("along", "across"),
        P("along", "across"),
        P(BOTH, None, None, None),
        P(BOTH, None),
        P(BOTH, None, None),
        P(BOTH, None, None),
        P(BOTH),
        P(BOTH),
    )
    out_specs = (P(None, "along", "across"), P(None, "along", "across"))
    return jax.shard_map(body, mesh=mesh, in_specs=in_specs, out_specs=out_specs, check_vma=False)
```

```python
import functools

import jax
import jax.numpy as jnp
from jax import lax
from jax.experimental import pallas as pl
from jax.experimental.pallas import tpu as pltpu
from jax.sharding import PartitionSpec as P

CL = 256
BOTH = ("along", "across")
OWNERS = 128
PAIRS = 128
RANK = 32
WAVES = 64
ROWS = 1024
PANELS = 2048
BF16 = jnp.bfloat16
F32 = jnp.float32
VMEM = pl.BlockSpec(memory_space=pltpu.VMEM)
SMEM = pl.BlockSpec(memory_space=pltpu.SMEM)


def call(kernel, out_shape, in_specs, out_specs, scratch=(), limit=48, cost=0):
    return pl.pallas_call(
        kernel,
        out_shape=out_shape,
        in_specs=in_specs,
        out_specs=out_specs,
        scratch_shapes=list(scratch),
        compiler_params=pltpu.CompilerParams(vmem_limit_bytes=limit * 2**20),
        cost_estimate=pl.CostEstimate(flops=0, bytes_accessed=cost, transcendentals=0),
    )


def iota(shape, dim):
    return lax.broadcasted_iota(jnp.int32, shape, dim)


def dot(a, b):
    return jnp.dot(a, b, preferred_element_type=F32)


def dot_nt(a, b):
    return lax.dot_general(a, b, (((1,), (1,)), ((), ())), preferred_element_type=F32)


def bucket_kernel(rows_ref, u_ref, out_ref, pick_ref, count):
    def clear(i, c):
        pick_ref[i] = PAIRS
        pick_ref[OWNERS + i] = PAIRS
        count[i] = 0
        return c

    lax.fori_loop(0, OWNERS, clear, 0, unroll=8)
    out_ref[...] = jnp.zeros_like(out_ref)

    def put(p, c):
        target = rows_ref[p] // 8
        slot = count[target]
        count[target] = slot + 1
        pick_ref[slot * OWNERS + target] = p
        out_ref[target, slot] = u_ref[p]
        return c

    lax.fori_loop(0, PAIRS, put, 0, unroll=4)


def far_bucket(far_rows, far_u):
    return call(
        bucket_kernel,
        (
            jax.ShapeDtypeStruct((OWNERS, 2, RANK, CL), BF16),
            jax.ShapeDtypeStruct((2 * OWNERS,), jnp.int32),
        ),
        [SMEM, VMEM],
        (VMEM, SMEM),
        [pltpu.SMEM((OWNERS,), jnp.int32)],
    )(far_rows, far_u)


def order_kernel(slot_ref, hot_ref, place_ref):
    strict = (iota((128, 128), 0) < iota((128, 128), 1)).astype(BF16)
    weights = jnp.concatenate([strict, jnp.ones((128, 128), BF16)], axis=1)
    seen = jnp.zeros((128, 128), F32)
    for x in range(16):
        slot = slot_ref[x : x + 1, :]
        dest, local = slot >> 11, slot & (PANELS - 1)
        hits = iota((128, 128), 0) == dest
        sums = dot(hits.astype(BF16), weights)
        rank = jnp.sum(jnp.where(hits, sums[:, :128] + seen, 0.0), axis=0, keepdims=True)
        seen = seen + sums[:, 128:]
        rank = rank.astype(jnp.int32)
        row = dest * 8 + (rank & 7)
        lanes = pl.ds(x * 128, 128)
        hot_ref[:, lanes] = (iota((ROWS, 128), 0) == row).astype(F32).astype(BF16)
        place_ref[0:1, lanes] = rank >> 3
        place_ref[1:2, lanes] = local >> 7
        place_ref[2:3, lanes] = local & 127
        place_ref[3:8, lanes] = jnp.zeros((5, 128), jnp.int32)


def sender_order(panel_slot):
    return call(
        order_kernel,
        (
            jax.ShapeDtypeStruct((ROWS, PANELS), BF16),
            jax.ShapeDtypeStruct((8, PANELS), jnp.int32),
        ),
        [VMEM],
        (VMEM, VMEM),
    )(panel_slot)


def payload_kernel(source_ref, hot_ref, place_ref, rows_ref, out_ref, stack):
    stack[...] = jnp.zeros_like(stack)
    for x in range(16):
        lanes = pl.ds(x * 128, 128)
        place = place_ref[:, lanes]
        second = place[0:1] == 1
        values = source_ref[:, x, :]
        stack[0:64, lanes] = jnp.where(second, 0.0, values).astype(BF16)
        stack[64:128, lanes] = jnp.where(second, values, 0.0).astype(BF16)
        high, low = place[1:2].astype(F32), place[2:3].astype(F32)
        notes = [
            jnp.where(second, 0.0, high),
            jnp.where(second, 0.0, low),
            jnp.where(second, high, 0.0),
            jnp.where(second, low, 0.0),
            jnp.zeros((12, 128), F32),
        ]
        stack[128:144, lanes] = jnp.concatenate(notes, axis=0).astype(BF16)
    rows = rows_ref[...].astype(F32)
    own = jnp.concatenate([jnp.zeros((4, 128), F32), rows, jnp.zeros((10, 128), F32)], axis=0)
    stack[128:144, pl.ds(PANELS, 128)] = own.astype(BF16)
    for m in range(0, ROWS, 256):
        left = hot_ref[pl.ds(m, 256), :]
        owner = ((iota((256, 128), 0) + m) >> 3) == iota((256, 128), 1)
        values = dot_nt(left, stack[:, pl.ds(0, PANELS)])
        values += dot_nt(owner.astype(F32).astype(BF16), stack[:, pl.ds(PANELS, 128)])
        out_ref[pl.ds(m, 256), :] = values.astype(BF16)


def source_payload(source, hot, place, rows):
    return call(
        payload_kernel,
        jax.ShapeDtypeStruct((ROWS, 256), BF16),
        [VMEM] * 4,
        VMEM,
        [pltpu.VMEM((256, PANELS + 128), BF16)],
    )(source, hot, place, rows)


def cluster_kernel(
    pick_ref, col_ref, arrived_ref, v_ref, clustered_ref, hot_ref, info_ref, c_ref, left, coeff
):
    for m in range(0, ROWS, 128):
        lanes = pl.ds(m, 128)
        values = arrived_ref[lanes, 0:128].astype(F32).T
        notes = arrived_ref[lanes, 128:256].astype(F32).T
        for half in range(2):
            slot = (notes[2 * half : 2 * half + 1] * 128.0 + notes[2 * half + 1 : 2 * half + 2])
            slot = slot.astype(jnp.int32)
            upper = slot >= 1024
            mine = values[half * 64 : half * 64 + 64]
            at = pl.ds(half * ROWS + m, 128)
            left[0:64, at] = jnp.where(upper, 0.0, mine).astype(BF16)
            left[64:128, at] = jnp.where(upper, mine, 0.0).astype(BF16)
            hot = iota((1024, 128), 0) == (slot & 1023)
            hot_ref[:, at] = hot.astype(F32).astype(BF16)
            info_ref[half : half + 1, lanes] = upper.astype(F32)
        info_ref[2:4, lanes] = notes[4:6]
        info_ref[4:8, lanes] = jnp.zeros((4, 128), F32)
    for q in range(4):
        got = dot_nt(left[...], hot_ref[pl.ds(q * 256, 256), :]).astype(BF16)
        clustered_ref[q] = got[0:64]
        clustered_ref[4 + q] = got[64:128]
    for q in range(4):
        pair = jnp.concatenate([clustered_ref[2 * q], clustered_ref[2 * q + 1]], axis=0)
        for m in range(0, PAIRS, 16):
            rows = v_ref[pl.ds(m, 16)].reshape(16 * RANK, CL)
            coeff[q, pl.ds(m * RANK, 16 * RANK), :] = dot_nt(rows, pair)
    lane = iota((RANK, 128), 1)

    def put(t, c):
        both = []
        for s in range(2):
            p = pick_ref[s * OWNERS + t]
            held = p < PAIRS
            p = jnp.minimum(p, PAIRS - 1)
            col = col_ref[p] & 7
            tile = coeff[col >> 1, pl.ds(pl.multiple_of(p * RANK, RANK), RANK), :]
            tile = jnp.where((col & 1) == s, tile, pltpu.roll(tile, 64, 1))
            both.append(jnp.where(held, tile, 0.0))
        c_ref[t] = jnp.where(lane < 64, both[0], both[1]).astype(BF16)
        return c

    lax.fori_loop(0, OWNERS, put, 0, unroll=4)


def cluster_and_coeff(pick, cols, arrived, far_v):
    return call(
        cluster_kernel,
        (
            jax.ShapeDtypeStruct((8, WAVES, CL), BF16),
            jax.ShapeDtypeStruct((1024, PANELS), BF16),
            jax.ShapeDtypeStruct((8, ROWS), F32),
            jax.ShapeDtypeStruct((OWNERS, RANK, 2 * WAVES), BF16),
        ),
        [SMEM, SMEM, VMEM, VMEM],
        (VMEM,) * 4,
        [pltpu.VMEM((128, PANELS), BF16), pltpu.VMEM((4, PAIRS * RANK, 128), F32)],
    )(pick, cols, arrived, far_v)


def near_kernel(rel_ref, before_ref, own_ref, after_ref, blocks_ref, out_ref, wide):
    c = pl.program_id(0)

    @pl.when(c == 0)
    def _():
        wide[0:8] = before_ref[...]
        wide[8:16] = own_ref[...]
        wide[16:24] = after_ref[...]

    total = jnp.zeros((WAVES, CL), F32)
    for k in range(9):
        total += dot_nt(wide[rel_ref[c * 9 + k]], blocks_ref[0, k])
    out_ref[0] = total


def near_product(relative, before, own, after, near_blocks):
    whole = pl.BlockSpec((8, WAVES, CL), lambda c, r: (0, 0, 0))
    return pl.pallas_call(
        near_kernel,
        out_shape=jax.ShapeDtypeStruct((8, WAVES, CL), F32),
        grid_spec=pltpu.PrefetchScalarGridSpec(
            num_scalar_prefetch=1,
            grid=(8,),
            in_specs=[
                whole,
                whole,
                whole,
                pl.BlockSpec((1, 9, CL, CL), lambda c, r: (c, 0, 0, 0)),
            ],
            out_specs=pl.BlockSpec((1, WAVES, CL), lambda c, r: (c, 0, 0)),
            scratch_shapes=[pltpu.VMEM((24, WAVES, CL), BF16)],
        ),
        compiler_params=pltpu.CompilerParams(vmem_limit_bytes=32 * 2**20),
        cost_estimate=pl.CostEstimate(flops=0, bytes_accessed=0, transcendentals=0),
    )(relative, before, own, after, near_blocks)


def total_kernel(c_ref, u_ref, near_ref, hot_ref, info_ref, out_ref, acc, masked, grid):
    acc[...] = jnp.zeros_like(acc)
    spread = ((iota((128, 512), 0) >> 3) == (iota((128, 512), 1) >> 5)) & (
        (iota((128, 512), 0) & 7) == 0
    )
    spread = spread.astype(F32).astype(BF16)

    def chunk(m, c):
        src = pl.ds(m * 16, 16)
        rows = dot(info_ref[:, pl.ds(pl.multiple_of(m * 128, 128), 128)].astype(BF16), spread)
        turned = c_ref[src].reshape(512, 128).astype(F32).T
        for s in range(2):
            row = rows[2 + s : 3 + s]
            mine = turned[s * 64 : s * 64 + 64]
            for cluster in range(8):
                masked[pl.ds(cluster * 64, 64), :] = jnp.where(
                    row == float(cluster), mine, 0.0
                ).astype(BF16)
            acc[...] += dot(masked[...], u_ref[src, s].reshape(512, CL))
        return c

    lax.fori_loop(0, 8, chunk, 0)
    for cluster in range(8):
        total = near_ref[cluster] + acc[pl.ds(cluster * 64, 64), :]
        grid[pl.ds((cluster >> 2) * 64, 64), pl.ds((cluster & 3) * 256, 256)] = total.astype(BF16)
    for m in range(0, ROWS, 256):
        halves = []
        for half in range(2):
            got = dot(grid[...], hot_ref[:, pl.ds(half * ROWS + m, 256)])
            upper = info_ref[half : half + 1, pl.ds(m, 256)] == 1.0
            halves.append(jnp.where(upper, got[64:128], got[0:64]))
        out_ref[pl.ds(m, 256), :] = jnp.concatenate(halves, axis=0).T.astype(BF16)


def total_home(c_in, u_in, near, hot, info):
    return call(
        total_kernel,
        jax.ShapeDtypeStruct((ROWS, 128), BF16),
        [VMEM] * 5,
        VMEM,
        [
            pltpu.VMEM((512, CL), F32),
            pltpu.VMEM((512, 512), BF16),
            pltpu.VMEM((128, 1024), BF16),
        ],
    )(c_in, u_in, near, hot, info)


def potential_kernel(returned_ref, hot_ref, place_ref, out_ref, turned, wide):
    for m in range(0, ROWS, 128):
        turned[:, pl.ds(m, 128)] = returned_ref[pl.ds(m, 128), :].astype(F32).T.astype(BF16)
    for x in range(0, 16, 2):
        lanes = pl.ds(x * 128, 256)
        got = dot(turned[...], hot_ref[:, lanes])
        got = jnp.where(place_ref[0:1, lanes] == 1, got[64:128], got[0:64])
        wide[:, x, :] = got[:, :128]
        wide[:, x + 1, :] = got[:, 128:]
    out_ref[...] = wide[...].astype(BF16)


def panel_potential(returned, hot, place):
    return call(
        potential_kernel,
        jax.ShapeDtypeStruct((WAVES, 16, 128), BF16),
        [VMEM] * 3,
        VMEM,
        [pltpu.VMEM((128, ROWS), BF16), pltpu.VMEM((WAVES, 16, 128), F32)],
    )(returned, hot, place)


def halo(elevation, velocity_pot):
    n, m = lax.axis_size("along"), lax.axis_size("across")
    down = [(i, i + 1) for i in range(n - 1)]
    up = [(i + 1, i) for i in range(n - 1)]
    right = [(i, i + 1) for i in range(m - 1)]
    left = [(i + 1, i) for i in range(m - 1)]
    both = jnp.stack([elevation, velocity_pot])
    above = lax.ppermute(both[:, :, -2:, :], "along", down)
    below = lax.ppermute(velocity_pot[:, :1, :], "along", up)
    west = lax.ppermute(both[:, :, :, -2:], "across", right)
    east = lax.ppermute(both[:, :, :, :2], "across", left)
    return above, below, west, east


def surface_step(elevation, velocity_pot, coef, above, below, west, east):
    def up_x(f, a):
        g = jnp.concatenate([a, f], axis=1)
        return 0.5 * (3.0 * f - 4.0 * g[:, 1:-1] + g[:, :-2])

    def trans(f, w, e):
        g = jnp.concatenate([w, f, e], axis=2)
        return (g[:, :, :-4] - 8.0 * g[:, :, 1:-3] + 8.0 * g[:, :, 3:-1] - g[:, :, 4:]) / 12.0

    gx = jnp.concatenate([above[1][:, 1:], velocity_pot, below], axis=1)
    gy = jnp.concatenate([west[1][:, :, 1:], velocity_pot, east[1][:, :, :1]], axis=2)
    curv = gx[:, 2:] + gx[:, :-2] + gy[:, :, 2:] + gy[:, :, :-2] - 4.0 * velocity_pot
    eta = (
        elevation
        - 0.4 * up_x(elevation, above[0])
        + 0.3 * trans(elevation, west[0], east[0])
        + coef * curv
    )
    source = (
        velocity_pot
        - 0.4 * up_x(velocity_pot, above[1])
        + 0.3 * trans(velocity_pot, west[1], east[1])
        - 0.5 * eta
    )
    return eta, source


def exchange(x):
    return lax.all_to_all(x, BOTH, split_axis=0, concat_axis=0, tiled=True)


def body(
    elevation,
    velocity_pot,
    surface_coef,
    panel_slot,
    near_blocks,
    near_cols,
    far_v,
    far_u,
    far_rows,
    far_cols,
):
    per_owner, clusters = 8, 1024
    me = lax.axis_index(BOTH)

    u_out, pick = far_bucket(far_rows, far_u)
    u_in = exchange(u_out)

    padded_rows = jnp.concatenate([far_rows % 8, jnp.full((1,), 8, jnp.int32)])
    slot_rows = padded_rows[pick].reshape(2, OWNERS)
    above, below, west, east = halo(elevation, velocity_pot)
    hot, place = sender_order(panel_slot)
    eta, source = surface_step(elevation, velocity_pot, surface_coef, above, below, west, east)
    payload = source_payload(source, hot, place, slot_rows).reshape(OWNERS, 8, 256)
    payload, u_in = lax.optimization_barrier((payload, u_in))
    arrived = exchange(payload).reshape(ROWS, 256)

    clustered, unhot, info, c_out = cluster_and_coeff(pick, far_cols, arrived, far_v)
    c_in = exchange(c_out)

    ring = [(i, (i + 1) % OWNERS) for i in range(OWNERS)]
    back = [(j, i) for i, j in ring]
    before = lax.ppermute(clustered, BOTH, ring)
    after = lax.ppermute(clustered, BOTH, back)
    relative = (near_cols - (me * per_owner - per_owner)) % clusters
    near = near_product(relative.reshape(72), before, clustered, after, near_blocks)

    home = total_home(c_in, u_in, near, unhot, info).reshape(OWNERS, 8, 128)
    returned = exchange(home).reshape(ROWS, 128)
    potential = panel_potential(returned, hot, place)
    return (eta, potential)


def solution(mesh):
    in_specs = (
        P(None, "along", "across"),
        P(None, "along", "across"),
        P("along", "across"),
        P("along", "across"),
        P(BOTH, None, None, None),
        P(BOTH, None),
        P(BOTH, None, None),
        P(BOTH, None, None),
        P(BOTH),
        P(BOTH),
    )
    out_specs = (P(None, "along", "across"), P(None, "along", "across"))
    return jax.shard_map(body, mesh=mesh, in_specs=in_specs, out_specs=out_specs, check_vma=False)
```

```python
import jax
import jax.numpy as jnp
from jax import lax
from jax.experimental import pallas as pl
from jax.experimental.pallas import tpu as pltpu
from jax.sharding import PartitionSpec as P

CL = 256
BOTH = ("along", "across")
OWNERS = 128
PAIRS = 128
RANK = 32
WAVES = 64
ROWS = 1024
PANELS = 2048
BF16 = jnp.bfloat16
F32 = jnp.float32
WIDE = 56
VMEM = pl.BlockSpec(memory_space=pltpu.VMEM)
SMEM = pl.BlockSpec(memory_space=pltpu.SMEM)
HBM = pl.BlockSpec(memory_space=pltpu.HBM)


def call(kernel, out_shape, in_specs, out_specs, scratch=(), limit=4, cost=0):
    return pl.pallas_call(
        kernel,
        out_shape=out_shape,
        in_specs=in_specs,
        out_specs=out_specs,
        scratch_shapes=list(scratch),
        compiler_params=pltpu.CompilerParams(vmem_limit_bytes=limit * 2**20),
        cost_estimate=pl.CostEstimate(flops=0, bytes_accessed=cost, transcendentals=0),
    )


def hot_block(count, row):
    index = iota((count, row.shape[1]), 0).astype(jnp.int16)
    hit = index == row.astype(jnp.int16)
    return jnp.where(hit, jnp.ones((), BF16), jnp.zeros((), BF16))


def iota(shape, dim):
    return lax.broadcasted_iota(jnp.int32, shape, dim)


def dot(a, b):
    return jnp.dot(a, b, preferred_element_type=F32)


def dot_nt(a, b):
    return lax.dot_general(a, b, (((1,), (1,)), ((), ())), preferred_element_type=F32)


def bucket_kernel(table_ref, u_hbm, out_hbm, values, packed, sems):
    load([(u_hbm, values)], sems)

    def put(t, c):
        for s in range(2):
            p = table_ref[s * OWNERS + t]
            mine = values[jnp.minimum(p, PAIRS - 1)]
            packed[t, pl.ds(s * RANK, RANK), :] = jnp.where(p < PAIRS, mine, jnp.zeros_like(mine))
        return c

    lax.fori_loop(0, OWNERS, put, 0, unroll=4)
    load([(packed, out_hbm.at[:, 0:64, :])], sems)


def far_bucket(table, far_u):
    return call(
        bucket_kernel,
        jax.ShapeDtypeStruct((OWNERS, 80, CL), BF16),
        [SMEM, HBM],
        HBM,
        [
            pltpu.VMEM((PAIRS, RANK, CL), BF16),
            pltpu.VMEM((OWNERS, 2 * RANK, CL), BF16),
            pltpu.SemaphoreType.DMA((1,)),
        ],
        limit=WIDE,
        cost=9 * 2**20,
    )(table, far_u)


def load(pairs, sems):
    copies = [pltpu.make_async_copy(a, b, sems.at[i]) for i, (a, b) in enumerate(pairs)]
    for copy in copies:
        copy.start()
    for copy in copies:
        copy.wait()


def tracks(hbm, ref):
    return [(hbm.at[:, x, :], ref.at[x]) for x in range(16)]


def pack_kernel(
    elevation_hbm, phi_hbm, down_ref, up_ref, right_ref, left_ref, elevation, phi, sems
):
    load(tracks(elevation_hbm, elevation) + tracks(phi_hbm, phi), sems)
    lane = iota((WAVES, 128), 1)
    right = jnp.zeros((WAVES, 128), F32)
    left = jnp.zeros((WAVES, 128), F32)
    for k, ref in enumerate((elevation, phi)):
        for x in range(16):
            values = ref[x]
            if x >= 14:
                down_ref[2 * k + x - 14] = values
            if x == 0 and k == 1:
                up_ref[...] = values
            at = 64 * k + 2 * x
            here = (lane >> 1) == at // 2
            right = jnp.where(here, pltpu.roll(values, (at + 2) % 128, 1), right)
            left = jnp.where(here, pltpu.roll(values, at, 1) if at else values, left)
    right_ref[...] = right
    left_ref[...] = left


def pack_edges(elevation, velocity_pot):
    side = jax.ShapeDtypeStruct((WAVES, 128), F32)
    track = pltpu.VMEM((16, WAVES, 128), F32)
    return call(
        pack_kernel,
        (jax.ShapeDtypeStruct((4, WAVES, 128), F32), side, side, side),
        [HBM, HBM],
        (VMEM,) * 4,
        [track, track, pltpu.SemaphoreType.DMA((32,))],
        limit=WIDE,
    )(elevation, velocity_pot)


def surface_kernel(
    keep_ref,
    elevation_hbm,
    phi_hbm,
    coef_hbm,
    slot_hbm,
    rows_hbm,
    cols_hbm,
    above_ref,
    below_ref,
    west_ref,
    east_ref,
    eta_hbm,
    out_hbm,
    place_ref,
    table_ref,
    elevation,
    phi,
    coef,
    slots,
    far,
    hot,
    eta_tracks,
    stack,
    out,
    sems,
    field_sems,
    eta_sems,
    out_sems,
):
    fields = tracks(elevation_hbm, elevation) + tracks(phi_hbm, phi)
    fields = [pltpu.make_async_copy(a, b, field_sems.at[i]) for i, (a, b) in enumerate(fields)]
    small = [
        (slot_hbm, slots),
        (rows_hbm, far.at[0:1]),
        (cols_hbm, far.at[1:2]),
        (coef_hbm, coef),
    ]
    small = [pltpu.make_async_copy(a, b, sems.at[i]) for i, (a, b) in enumerate(small)]
    for copy in small + fields:
        copy.start()
    for copy in small:
        copy.wait()

    up = iota((128, 128), 0) < iota((128, 128), 1)
    weights = jnp.concatenate([up.astype(F32), jnp.ones((128, 128), F32)], axis=1).astype(BF16)
    seen = jnp.zeros((128, 128), F32)
    for x in range(16):
        slot = slots[x : x + 1, :]
        dest, local = slot >> 11, slot & (PANELS - 1)
        hits = iota((128, 128), 0) == dest
        sums = dot(hits.astype(F32).astype(BF16), weights)
        rank = jnp.sum(jnp.where(hits, sums[:, :128] + seen, 0.0), axis=0, keepdims=True)
        seen = seen + sums[:, 128:]
        rank = rank.astype(jnp.int32)
        row = dest * 8 + (rank & 7)
        lanes = pl.ds(x * 128, 128)
        hot[:, lanes] = hot_block(ROWS, row)
        place_ref[0:1, lanes] = rank >> 3
        place_ref[1:2, lanes] = local >> 7
        place_ref[2:3, lanes] = local & 127
        place_ref[3:4, lanes] = row
        place_ref[4:8, lanes] = jnp.zeros((4, 128), jnp.int32)

    turned = [
        jnp.broadcast_to(far[k : k + 1, :].astype(F32), (128, 128)).T.astype(jnp.int32)
        for k in range(2)
    ]
    hits = (turned[0] >> 3) == iota((128, 128), 1)
    down = (iota((128, 128), 0) > iota((128, 128), 1)).astype(F32).astype(BF16)
    rank = dot(down, hits.astype(F32).astype(BF16))
    values = (iota((128, 128), 0) - PAIRS, (turned[0] & 7) - 8, turned[1] & 7)
    for k, (value, base) in enumerate(zip(values, (PAIRS, 8, 0))):
        for s in range(2):
            chosen = hits & (rank == float(s))
            found = jnp.sum(jnp.where(chosen, value.astype(F32), 0.0), axis=0, keepdims=True)
            table_ref[2 * k + s : 2 * k + s + 1, :] = found.astype(jnp.int32) + base
    table_ref[6:8, :] = jnp.zeros((2, 128), jnp.int32)

    for copy in fields:
        copy.wait()
    lane = iota((WAVES, 128), 1)
    west, east = west_ref[...] * keep_ref[2], east_ref[...] * keep_ref[3]
    above = [above_ref[k] * keep_ref[0] for k in range(4)]
    below = below_ref[...] * keep_ref[1]

    def views(f, x, k, ref):
        x1 = ref[x - 1] if x >= 1 else above[2 * k + 1]
        x2 = ref[x - 2] if x >= 2 else above[2 * k + x]
        at = 64 * k + 2 * x
        left = pltpu.roll(west, 128 - at, 1) if at else west
        right = pltpu.roll(east, 126 - at, 1)
        w2 = jnp.where(lane < 2, left, pltpu.roll(f, 2, 1))
        w1 = jnp.where(lane < 1, pltpu.roll(left, 127, 1), pltpu.roll(f, 1, 1))
        e2 = jnp.where(lane >= 126, right, pltpu.roll(f, 126, 1))
        e1 = jnp.where(lane >= 127, pltpu.roll(right, 1, 1), pltpu.roll(f, 127, 1))
        up = 0.5 * (3.0 * f - 4.0 * x1 + x2)
        across = (w2 - 8.0 * w1 + 8.0 * e1 - e2) * (1.0 / 12.0)
        return x1, w1, e1, up, across

    stack[128:256, :] = jnp.zeros((128, PANELS + 128), BF16)
    stack[0:128, pl.ds(PANELS, 128)] = jnp.zeros((128, 128), BF16)
    stores = []
    for x in range(16):
        e, p = elevation[x], phi[x]
        _, _, _, up, across = views(e, x, 0, elevation)
        p1, pw, pe, phi_up, phi_across = views(p, x, 1, phi)
        next_row = phi[x + 1] if x < 15 else below
        curvature = next_row + p1 + pe + pw - 4.0 * p
        eta = e - 0.4 * up + 0.3 * across + coef[x : x + 1, :] * curvature
        eta_tracks[x] = eta
        stores.append(pltpu.make_async_copy(eta_tracks.at[x], eta_hbm.at[:, x, :], eta_sems.at[x]))
        stores[x].start()
        values = p - 0.4 * phi_up + 0.3 * phi_across - 0.5 * eta
        lanes = pl.ds(x * 128, 128)
        place = place_ref[:, lanes]
        second = place[0:1] == 1
        stack[0:64, lanes] = jnp.where(second, 0.0, values).astype(BF16)
        stack[64:128, lanes] = jnp.where(second, values, 0.0).astype(BF16)
        high, low = place[1:2].astype(F32), place[2:3].astype(F32)
        notes = [
            jnp.where(second, 0.0, high),
            jnp.where(second, 0.0, low),
            jnp.where(second, high, 0.0),
            jnp.where(second, low, 0.0),
            jnp.zeros((12, 128), F32),
        ]
        stack[128:144, lanes] = jnp.concatenate(notes, axis=0).astype(BF16)
    rows = table_ref[2:4, :].astype(F32)
    own = jnp.concatenate([jnp.zeros((4, 128), F32), rows, jnp.zeros((10, 128), F32)], axis=0)
    stack[128:144, pl.ds(PANELS, 128)] = own.astype(BF16)
    for m in range(0, ROWS, 256):
        at = pl.ds(m, 256)
        owner = ((iota((256, 128), 0) + m) >> 3) == iota((256, 128), 1)
        values = dot_nt(hot[at, :], stack[:, pl.ds(0, PANELS)])
        values += dot_nt(owner.astype(F32).astype(BF16), stack[:, pl.ds(PANELS, 128)])
        out[at, :] = values.astype(BF16)
        stores.append(pltpu.make_async_copy(out.at[at], out_hbm.at[at], out_sems.at[m // 256]))
        stores[-1].start()
    for copy in stores:
        copy.wait()


def surface_payload(keep, elevation, velocity_pot, coef, slots, rows, cols, halo):
    track = pltpu.VMEM((16, WAVES, 128), F32)
    return call(
        surface_kernel,
        (
            jax.ShapeDtypeStruct((WAVES, 16, 128), F32),
            jax.ShapeDtypeStruct((ROWS, 256), BF16),
            jax.ShapeDtypeStruct((8, PANELS), jnp.int32),
            jax.ShapeDtypeStruct((8, 128), jnp.int32),
        ),
        [SMEM] + [HBM] * 6 + [VMEM] * 4,
        (HBM, HBM, VMEM, VMEM),
        [
            track,
            track,
            pltpu.VMEM((16, 128), F32),
            pltpu.VMEM((16, 128), jnp.int32),
            pltpu.VMEM((2, 128), jnp.int32),
            pltpu.VMEM((ROWS, PANELS), BF16),
            track,
            pltpu.VMEM((256, PANELS + 128), BF16),
            pltpu.VMEM((ROWS, 256), BF16),
            pltpu.SemaphoreType.DMA((4,)),
            pltpu.SemaphoreType.DMA((32,)),
            pltpu.SemaphoreType.DMA((16,)),
            pltpu.SemaphoreType.DMA((4,)),
        ],
        limit=WIDE,
    )(
        keep,
        elevation,
        velocity_pot,
        coef,
        slots,
        rows.reshape(1, PAIRS),
        cols.reshape(1, PAIRS),
        *halo,
    )


def cluster_kernel(arrived_ref, clustered_ref, info_ref, hot, right):
    lane = iota((128, 128), 1)
    for m in range(0, ROWS, 128):
        lanes = pl.ds(m, 128)
        values = arrived_ref[lanes, 0:128].astype(F32)
        tail = arrived_ref[lanes, 128:256].astype(F32)
        notes = tail.T
        swapped = pltpu.roll(values, 64, 1)
        for half in range(2):
            slot = notes[2 * half : 2 * half + 1] * 128.0 + notes[2 * half + 1 : 2 * half + 2]
            info_ref[half : half + 1, lanes] = slot
            at = half * ROWS + m
            place = slot.astype(jnp.int32) & 1023
            hot[:, pl.ds(at, 128)] = hot_block(1024, place)
            both = jnp.where((lane < 64) == (half == 0), values, swapped)
            upper = tail[:, 2 * half : 2 * half + 1] >= 8.0
            right[pl.ds(at, 128), :] = jnp.where(upper == (lane >= 64), both, 0.0).astype(BF16)
        info_ref[2:4, lanes] = notes[4:6]
        info_ref[4:8, lanes] = jnp.zeros((4, 128), F32)
    for m in range(0, 1024, 256):
        clustered_ref[pl.ds(m, 256), :] = dot(hot[pl.ds(m, 256), :], right[...]).astype(BF16)


def to_clusters(arrived):
    return call(
        cluster_kernel,
        (
            jax.ShapeDtypeStruct((1024, 128), BF16),
            jax.ShapeDtypeStruct((8, ROWS), F32),
        ),
        [VMEM],
        (VMEM,) * 2,
        [pltpu.VMEM((1024, PANELS), BF16), pltpu.VMEM((PANELS, 128), BF16)],
        limit=8,
    )(arrived)


def coeff_kernel(table_ref, clustered_ref, v_hbm, big_hbm, out_hbm, basis, coeff, packed, sems):
    del big_hbm
    parts = [
        pltpu.make_async_copy(v_hbm.at[pl.ds(m, 32)], basis.at[pl.ds(m, 32)], sems.at[m // 32])
        for m in range(0, PAIRS, 32)
    ]
    for copy in parts:
        copy.start()
    weights = [clustered_ref[pl.ds(q * 256, 256), :] for q in range(4)]
    weights = [jnp.concatenate(weights[q : q + 2], axis=1) for q in (0, 2)]
    for q in range(4):
        coeff[q, pl.ds(PAIRS * RANK, RANK), :] = jnp.zeros((RANK, 128), F32)
    for m in range(0, PAIRS, 16):
        if m % 32 == 0:
            parts[m // 32].wait()
        rows = basis[pl.ds(m, 16)].reshape(16 * RANK, CL)
        at = pl.ds(m * RANK, 16 * RANK)
        for q in range(2):
            got = dot(rows, weights[q])
            coeff[2 * q, at, :] = got[:, :128]
            coeff[2 * q + 1, at, :] = got[:, 128:]
    lane = iota((RANK, 128), 1)

    def put(t, c):
        both = []
        for s in range(2):
            p = table_ref[s * OWNERS + t]
            col = table_ref[(4 + s) * OWNERS + t]
            tile = coeff[col & 3, pl.ds(pl.multiple_of(p * RANK, RANK), RANK), :]
            both.append(pltpu.roll(tile, ((col >> 2) ^ s) * 64, 1))
        both = jnp.where(lane < 64, both[0], both[1])
        packed[t, :, 0:128] = both[0:16].astype(BF16)
        packed[t, :, 128:256] = both[16:32].astype(BF16)
        return c

    lax.fori_loop(0, OWNERS, put, 0, unroll=8)
    load([(packed, out_hbm.at[:, 64:80, :])], sems)


def add_coeff(table, clustered, far_v, big):
    return pl.pallas_call(
        coeff_kernel,
        out_shape=jax.ShapeDtypeStruct((OWNERS, 80, CL), BF16),
        in_specs=[SMEM, VMEM, HBM, HBM],
        out_specs=HBM,
        scratch_shapes=[
            pltpu.VMEM((PAIRS, RANK, CL), BF16),
            pltpu.VMEM((4, PAIRS * RANK + RANK, 128), F32),
            pltpu.VMEM((OWNERS, 16, CL), BF16),
            pltpu.SemaphoreType.DMA((4,)),
        ],
        input_output_aliases={3: 0},
        compiler_params=pltpu.CompilerParams(vmem_limit_bytes=WIDE * 2**20),
        cost_estimate=pl.CostEstimate(flops=0, bytes_accessed=0, transcendentals=0),
    )(table, clustered, far_v, big)


def near_kernel(
    rel_ref,
    before_ref,
    own_ref,
    after_ref,
    info_ref,
    place_ref,
    blocks_ref,
    out_ref,
    unhot_hbm,
    hot_hbm,
    wide,
    unhot,
    hot,
    sems,
):
    c = pl.program_id(0)

    @pl.when(c == 0)
    def _():
        for k, ref in enumerate((before_ref, own_ref, after_ref)):
            for q in range(4):
                turned = ref[pl.ds(q * 256, 256), :].astype(F32).T.astype(BF16)
                wide[8 * k + q] = turned[0:64]
                wide[8 * k + 4 + q] = turned[64:128]

    lanes = pl.ds(pl.multiple_of(c * 256, 256), 256)
    info = info_ref[:, pl.ds(pl.multiple_of(lax.rem(c, 4) * 256, 256), 256)]
    slot = jnp.where(c < 4, info[0:1], info[1:2]).astype(jnp.int32)
    unhot[:, lanes] = hot_block(1024, slot & 1023)
    hot[:, lanes] = hot_block(ROWS, place_ref[3:4, lanes])
    total = jnp.zeros((WAVES, CL), F32)
    for k in range(9):
        total += dot_nt(wide[rel_ref[c * 9 + k]], blocks_ref[0, k])
    out_ref[0] = total

    @pl.when(c == 7)
    def _():
        load([(unhot, unhot_hbm), (hot, hot_hbm)], sems)


def near_product(relative, before, own, after, info, place, near_blocks):
    matrix = jax.ShapeDtypeStruct((1024, PANELS), BF16)
    return pl.pallas_call(
        near_kernel,
        out_shape=(jax.ShapeDtypeStruct((8, WAVES, CL), F32), matrix, matrix),
        grid_spec=pltpu.PrefetchScalarGridSpec(
            num_scalar_prefetch=1,
            grid=(8,),
            in_specs=[VMEM] * 5 + [pl.BlockSpec((1, 9, CL, CL), lambda c, r: (c, 0, 0, 0))],
            out_specs=(pl.BlockSpec((1, WAVES, CL), lambda c, r: (c, 0, 0)), HBM, HBM),
            scratch_shapes=[
                pltpu.VMEM((24, WAVES, CL), BF16),
                pltpu.VMEM((1024, PANELS), BF16),
                pltpu.VMEM((1024, PANELS), BF16),
                pltpu.SemaphoreType.DMA((2,)),
            ],
        ),
        compiler_params=pltpu.CompilerParams(vmem_limit_bytes=WIDE * 2**20),
        cost_estimate=pl.CostEstimate(flops=0, bytes_accessed=12 * 2**20, transcendentals=0),
    )(relative, before, own, after, info, place, near_blocks)


def total_kernel(
    big_hbm, near_ref, hot_hbm, info_ref, out_hbm, big, hot, acc, masked, grid, out, sems, hot_sems, out_sems
):
    pieces = [
        pltpu.make_async_copy(big_hbm.at[pl.ds(m * 16, 16)], big.at[pl.ds(m * 16, 16)], sems.at[m])
        for m in range(8)
    ]
    for piece in pieces:
        piece.start()
    hot_copy = pltpu.make_async_copy(hot_hbm, hot, hot_sems.at[0])
    hot_copy.start()
    spread = ((iota((128, 256), 0) >> 3) == (iota((128, 256), 1) >> 4)) & (
        (iota((128, 256), 0) & 7) == 0
    )
    spread = spread.astype(F32).astype(BF16)
    for m in range(8):
        pieces[m].wait()
        src = pl.ds(m * 16, 16)
        slot = m % 2
        rows = dot(info_ref[:, pl.ds(m * 128, 128)].astype(BF16), spread)
        bases = []
        for part in range(2):
            mine = big[src, 64:80, pl.ds(part * 128, 128)].reshape(256, 128)
            turned = mine.astype(F32).T.astype(BF16)
            for s in range(2):
                at = pl.ds((2 * part + s) * 256, 256)
                for cluster in range(8):
                    hit = (rows[2 + s : 3 + s] == float(cluster)).astype(F32).astype(BF16)
                    masked[slot, pl.ds(cluster * 64, 64), at] = turned[s * 64 : s * 64 + 64] * hit
                bases.append(big[src, pl.ds(s * RANK + part * 16, 16), :].reshape(256, CL))
        product = dot(masked[slot], jnp.concatenate(bases, axis=0))
        if m == 0:
            acc[...] = product
        else:
            acc[...] += product
    for cluster in range(8):
        total = near_ref[cluster] + acc[pl.ds(cluster * 64, 64), :]
        grid[pl.ds((cluster >> 2) * 64, 64), pl.ds((cluster & 3) * 256, 256)] = total.astype(BF16)
    hot_copy.wait()
    stores = []
    for m in range(0, ROWS, 256):
        at = pl.ds(m, 256)
        halves = []
        for half in range(2):
            got = dot(grid[...], hot[:, pl.ds(half * ROWS + m, 256)])
            upper = info_ref[half : half + 1, at] >= 1024.0
            halves.append(jnp.where(upper, got[64:128], got[0:64]))
        out[at, :] = jnp.concatenate(halves, axis=0).T.astype(BF16)
        stores.append(pltpu.make_async_copy(out.at[at], out_hbm.at[at], out_sems.at[m // 256]))
        stores[-1].start()
    for copy in stores:
        copy.wait()


def total_home(big, near, hot, info):
    return call(
        total_kernel,
        jax.ShapeDtypeStruct((ROWS, 128), BF16),
        [HBM, VMEM, HBM, VMEM],
        HBM,
        [
            pltpu.VMEM((OWNERS, 80, CL), BF16),
            pltpu.VMEM((1024, PANELS), BF16),
            pltpu.VMEM((512, CL), F32),
            pltpu.VMEM((2, 512, 1024), BF16),
            pltpu.VMEM((128, 1024), BF16),
            pltpu.VMEM((ROWS, 128), BF16),
            pltpu.SemaphoreType.DMA((8,)),
            pltpu.SemaphoreType.DMA((1,)),
            pltpu.SemaphoreType.DMA((4,)),
        ],
        limit=WIDE,
    )(big, near, hot, info)


def potential_kernel(returned_ref, hot_ref, place_ref, out_ref, turned, wide):
    for m in range(0, ROWS, 128):
        turned[:, pl.ds(m, 128)] = returned_ref[pl.ds(m, 128), :].astype(F32).T.astype(BF16)
    for x in range(0, 16, 2):
        lanes = pl.ds(x * 128, 256)
        got = dot(turned[...], hot_ref[:, lanes])
        got = jnp.where(place_ref[0:1, lanes] == 1, got[64:128], got[0:64])
        wide[:, x, :] = got[:, :128]
        wide[:, x + 1, :] = got[:, 128:]
    out_ref[...] = wide[...].astype(BF16)


def panel_potential(returned, hot, place):
    return call(
        potential_kernel,
        jax.ShapeDtypeStruct((WAVES, 16, 128), BF16),
        [VMEM] * 3,
        VMEM,
        [pltpu.VMEM((128, ROWS), BF16), pltpu.VMEM((WAVES, 16, 128), F32)],
    )(returned, hot, place)


def exchange(x):
    return lax.all_to_all(x, BOTH, split_axis=0, concat_axis=0, tiled=True)


def ring(axis, step):
    size = lax.axis_size(axis)
    return [(i, (i + step) % size) for i in range(size)]


def body(
    elevation,
    velocity_pot,
    surface_coef,
    panel_slot,
    near_blocks,
    near_cols,
    far_v,
    far_u,
    far_rows,
    far_cols,
):
    per_owner, clusters = 8, 1024
    me = lax.axis_index(BOTH)
    row, col = lax.axis_index("along"), lax.axis_index("across")
    keep = jnp.stack(
        [row > 0, row < lax.axis_size("along") - 1, col > 0, col < lax.axis_size("across") - 1]
    ).astype(F32)

    down, up, right, left = pack_edges(elevation, velocity_pot)
    above = lax.ppermute(down, "along", ring("along", 1))
    below = lax.ppermute(up, "along", ring("along", -1))
    west = lax.ppermute(right, "across", ring("across", 1))
    east = lax.ppermute(left, "across", ring("across", -1))
    eta, payload, place, table = surface_payload(
        keep,
        elevation,
        velocity_pot,
        surface_coef,
        panel_slot,
        far_rows,
        far_cols,
        (above, below, west, east),
    )
    table = table.reshape(8 * 128)
    arrived = exchange(payload.reshape(OWNERS, 8, 256)).reshape(ROWS, 256)
    big = far_bucket(table, far_u)
    arrived, big = lax.optimization_barrier((arrived, big))

    clustered, info = to_clusters(arrived)
    before = lax.ppermute(clustered, BOTH, ring(BOTH, 1))
    after = lax.ppermute(clustered, BOTH, ring(BOTH, -1))
    big = add_coeff(table, clustered, far_v, big)
    before, after, big = lax.optimization_barrier((before, after, big))
    big = exchange(big)

    relative = (near_cols - (me * per_owner - per_owner)) % clusters
    near, unhot, hot = near_product(
        relative.reshape(72), before, clustered, after, info, place, near_blocks
    )

    home = total_home(big, near, unhot, info).reshape(OWNERS, 8, 128)
    returned = exchange(home).reshape(ROWS, 128)
    potential = panel_potential(returned, hot, place)
    return (eta, potential)


def solution(mesh):
    in_specs = (
        P(None, "along", "across"),
        P(None, "along", "across"),
        P("along", "across"),
        P("along", "across"),
        P(BOTH, None, None, None),
        P(BOTH, None),
        P(BOTH, None, None),
        P(BOTH, None, None),
        P(BOTH),
        P(BOTH),
    )
    out_specs = (P(None, "along", "across"), P(None, "along", "across"))
    return jax.shard_map(body, mesh=mesh, in_specs=in_specs, out_specs=out_specs, check_vma=False)
```

```python
import jax
import jax.numpy as jnp
from jax import lax
from jax.experimental import pallas as pl
from jax.experimental.pallas import tpu as pltpu
from jax.sharding import PartitionSpec as P

CL = 256
BOTH = ("along", "across")
OWNERS = 128
PAIRS = 128
RANK = 32
WAVES = 64
ROWS = 1024
PANELS = 2048
BF16 = jnp.bfloat16
F32 = jnp.float32
WIDE = 56
PACK = 56
TIGHT = 52
VMEM = pl.BlockSpec(memory_space=pltpu.VMEM)
SMEM = pl.BlockSpec(memory_space=pltpu.SMEM)
HBM = pl.BlockSpec(memory_space=pltpu.HBM)


def call(kernel, out_shape, in_specs, out_specs, scratch=(), limit=4, cost=0):
    return pl.pallas_call(
        kernel,
        out_shape=out_shape,
        in_specs=in_specs,
        out_specs=out_specs,
        scratch_shapes=list(scratch),
        compiler_params=pltpu.CompilerParams(vmem_limit_bytes=limit * 2**20),
        cost_estimate=pl.CostEstimate(flops=0, bytes_accessed=cost, transcendentals=0),
    )


def hot_block(count, row):
    index = iota((count, row.shape[1]), 0).astype(jnp.int16)
    hit = index == row.astype(jnp.int16)
    return jnp.where(hit, jnp.ones((), BF16), jnp.zeros((), BF16))


def iota(shape, dim):
    return lax.broadcasted_iota(jnp.int32, shape, dim)


def dot(a, b):
    return jnp.dot(a, b, preferred_element_type=F32)


def dot_nt(a, b):
    return lax.dot_general(a, b, (((1,), (1,)), ((), ())), preferred_element_type=F32)


def bucket_kernel(table_ref, u_hbm, out_hbm, values, packed, sems):
    load([(u_hbm, values)], sems)

    def put(t, c):
        for s in range(2):
            p = table_ref[s * OWNERS + t]
            mine = values[jnp.minimum(p, PAIRS - 1)]
            packed[t, pl.ds(s * RANK, RANK), :] = jnp.where(p < PAIRS, mine, jnp.zeros_like(mine))
        return c

    lax.fori_loop(0, OWNERS, put, 0, unroll=4)
    load([(packed, out_hbm.at[:, 0:64, :])], sems)


def far_bucket(table, far_u):
    return call(
        bucket_kernel,
        jax.ShapeDtypeStruct((OWNERS, 80, CL), BF16),
        [SMEM, HBM],
        HBM,
        [
            pltpu.VMEM((PAIRS, RANK, CL), BF16),
            pltpu.VMEM((OWNERS, 2 * RANK, CL), BF16),
            pltpu.SemaphoreType.DMA((1,)),
        ],
        limit=TIGHT,
        cost=9 * 2**20,
    )(table, far_u)


def load(pairs, sems):
    copies = [pltpu.make_async_copy(a, b, sems.at[i]) for i, (a, b) in enumerate(pairs)]
    for copy in copies:
        copy.start()
    for copy in copies:
        copy.wait()


def pack_kernel(
    elevation_hbm,
    phi_hbm,
    slot_hbm,
    rows_hbm,
    cols_hbm,
    coef_hbm,
    elevation_ref,
    phi_ref,
    plan_ref,
    along_a,
    along_b,
    across_a,
    across_b,
    ints,
    sems,
    field_sems,
):
    small = [
        (slot_hbm, ints.at[0:16]),
        (rows_hbm, ints.at[16:17]),
        (cols_hbm, ints.at[17:18]),
        (coef_hbm, plan_ref.at[24:40]),
    ]
    small = [pltpu.make_async_copy(a, b, sems.at[i]) for i, (a, b) in enumerate(small)]
    fields = []
    for x in range(16):
        fields.append((elevation_hbm.at[:, x, :], elevation_ref.at[x]))
        fields.append((phi_hbm.at[:, x, :], phi_ref.at[x]))
    fields = [pltpu.make_async_copy(a, b, field_sems.at[i]) for i, (a, b) in enumerate(fields)]
    for copy in fields + small:
        copy.start()
    for copy in small:
        copy.wait()
    plan_ref[0:24, :] = ints[...].astype(F32)
    even_row = lax.rem(lax.axis_index("along"), 2) == 0
    even_col = lax.rem(lax.axis_index("across"), 2) == 0
    for copy in fields:
        copy.wait()
    lane = iota((WAVES, 128), 1)
    right = jnp.zeros((WAVES, 128), F32)
    left = jnp.zeros((WAVES, 128), F32)
    for k, ref in enumerate((elevation_ref, phi_ref)):
        for x in range(16):
            values = ref[x]
            at = 64 * k + 2 * x
            here = (lane >> 1) == at // 2
            right = jnp.where(here, pltpu.roll(values, (at + 2) % 128, 1), right)
            left = jnp.where(here, pltpu.roll(values, at, 1) if at else values, left)
    across_a[...] = jnp.where(even_col, right, left)
    across_b[...] = jnp.where(even_col, left, right)
    upward = phi_ref[0]
    for k, downward in enumerate((elevation_ref[14], elevation_ref[15], phi_ref[14], phi_ref[15])):
        along_a[k] = jnp.where(even_row, downward, upward)
        along_b[k] = jnp.where(even_row, upward, downward)


def pack_edges(elevation, velocity_pot, panel_slot, far_rows, far_cols, coef):
    side = jax.ShapeDtypeStruct((WAVES, 128), F32)
    rows = jax.ShapeDtypeStruct((4, WAVES, 128), F32)
    track = jax.ShapeDtypeStruct((16, WAVES, 128), F32)
    return call(
        pack_kernel,
        (track, track, jax.ShapeDtypeStruct((40, 128), F32), rows, rows, side, side),
        [HBM] * 6,
        (VMEM,) * 7,
        [
            pltpu.VMEM((24, 128), jnp.int32),
            pltpu.SemaphoreType.DMA((4,)),
            pltpu.SemaphoreType.DMA((32,)),
        ],
        limit=PACK,
    )(
        elevation,
        velocity_pot,
        panel_slot,
        far_rows.reshape(1, PAIRS),
        far_cols.reshape(1, PAIRS),
        coef,
    )


def order_kernel(plan_ref, hot_ref, place_ref, table_ref):
    up = iota((128, 128), 0) < iota((128, 128), 1)
    weights = jnp.concatenate([up.astype(F32), jnp.ones((128, 128), F32)], axis=1).astype(BF16)
    seen = jnp.zeros((128, 128), F32)
    for x in range(16):
        slot = plan_ref[x : x + 1, :].astype(jnp.int32)
        dest, local = slot >> 11, slot & (PANELS - 1)
        hits = iota((128, 128), 0) == dest
        sums = dot(hits.astype(F32).astype(BF16), weights)
        rank = jnp.sum(jnp.where(hits, sums[:, :128] + seen, 0.0), axis=0, keepdims=True)
        seen = seen + sums[:, 128:]
        rank = rank.astype(jnp.int32)
        row = dest * 8 + (rank & 7)
        lanes = pl.ds(x * 128, 128)
        hot_ref[:, lanes] = hot_block(ROWS, row)
        place_ref[0:1, lanes] = rank >> 3
        place_ref[1:2, lanes] = local >> 7
        place_ref[2:3, lanes] = local & 127
        place_ref[3:4, lanes] = row
        place_ref[4:8, lanes] = jnp.zeros((4, 128), jnp.int32)

    turned = [
        jnp.broadcast_to(plan_ref[k : k + 1, :], (128, 128)).T.astype(jnp.int32)
        for k in range(16, 18)
    ]
    hits = (turned[0] >> 3) == iota((128, 128), 1)
    down = (iota((128, 128), 0) > iota((128, 128), 1)).astype(F32).astype(BF16)
    rank = dot(down, hits.astype(F32).astype(BF16))
    values = (iota((128, 128), 0) - PAIRS, (turned[0] & 7) - 8, turned[1] & 7)
    for k, (value, base) in enumerate(zip(values, (PAIRS, 8, 0))):
        for s in range(2):
            chosen = hits & (rank == float(s))
            found = jnp.sum(jnp.where(chosen, value.astype(F32), 0.0), axis=0, keepdims=True)
            table_ref[2 * k + s : 2 * k + s + 1, :] = found.astype(jnp.int32) + base
    table_ref[6:8, :] = jnp.zeros((2, 128), jnp.int32)


def sender_order(plan):
    return call(
        order_kernel,
        (
            jax.ShapeDtypeStruct((ROWS, PANELS), BF16),
            jax.ShapeDtypeStruct((8, PANELS), jnp.int32),
            jax.ShapeDtypeStruct((8, 128), jnp.int32),
        ),
        [VMEM],
        (VMEM,) * 3,
        limit=8,
    )(plan)


def surface_kernel(
    plan_ref,
    elevation_ref,
    phi_ref,
    along_a,
    along_b,
    across_a,
    across_b,
    hot_ref,
    place_ref,
    table_ref,
    eta_hbm,
    out_hbm,
    eta_tracks,
    stack,
    out,
    eta_sems,
    out_sems,
):
    row, col = lax.axis_index("along"), lax.axis_index("across")
    first_row, last_row = row == 0, row == lax.axis_size("along") - 1
    first_col, last_col = col == 0, col == lax.axis_size("across") - 1
    lane = iota((WAVES, 128), 1)
    even_row, even_col = lax.rem(row, 2) == 0, lax.rem(col, 2) == 0
    west = jnp.where(even_col, across_b[...], across_a[...])
    east = jnp.where(even_col, across_a[...], across_b[...])
    west, east = jnp.where(first_col, 0.0, west), jnp.where(last_col, 0.0, east)
    above = [jnp.where(even_row, along_b[k], along_a[k]) for k in range(4)]
    above = [jnp.where(first_row, 0.0, values) for values in above]
    below = jnp.where(last_row, 0.0, jnp.where(even_row, along_a[0], along_b[0]))

    def views(f, x, k, ref):
        x1 = ref[x - 1] if x >= 1 else above[2 * k + 1]
        x2 = ref[x - 2] if x >= 2 else above[2 * k + x]
        at = 64 * k + 2 * x
        left = pltpu.roll(west, 128 - at, 1) if at else west
        right = pltpu.roll(east, 126 - at, 1)
        w2 = jnp.where(lane < 2, left, pltpu.roll(f, 2, 1))
        w1 = jnp.where(lane < 1, pltpu.roll(left, 127, 1), pltpu.roll(f, 1, 1))
        e2 = jnp.where(lane >= 126, right, pltpu.roll(f, 126, 1))
        e1 = jnp.where(lane >= 127, pltpu.roll(right, 1, 1), pltpu.roll(f, 127, 1))
        up = 0.5 * (3.0 * f - 4.0 * x1 + x2)
        across = (w2 - 8.0 * w1 + 8.0 * e1 - e2) * (1.0 / 12.0)
        return x1, w1, e1, up, across

    stack[128:256, :] = jnp.zeros((128, PANELS + 128), BF16)
    stack[0:128, pl.ds(PANELS, 128)] = jnp.zeros((128, 128), BF16)
    stores = []
    for x in range(16):
        e, p = elevation_ref[x], phi_ref[x]
        _, _, _, up, across = views(e, x, 0, elevation_ref)
        p1, pw, pe, phi_up, phi_across = views(p, x, 1, phi_ref)
        next_row = phi_ref[x + 1] if x < 15 else below
        curvature = next_row + p1 + pe + pw - 4.0 * p
        eta = e - 0.4 * up + 0.3 * across + plan_ref[24 + x : 25 + x, :] * curvature
        eta_tracks[x] = eta
        stores.append(pltpu.make_async_copy(eta_tracks.at[x], eta_hbm.at[:, x, :], eta_sems.at[x]))
        stores[x].start()
        values = p - 0.4 * phi_up + 0.3 * phi_across - 0.5 * eta
        lanes = pl.ds(x * 128, 128)
        place = place_ref[:, lanes]
        second = place[0:1] == 1
        stack[0:64, lanes] = jnp.where(second, 0.0, values).astype(BF16)
        stack[64:128, lanes] = jnp.where(second, values, 0.0).astype(BF16)
        high, low = place[1:2].astype(F32), place[2:3].astype(F32)
        notes = [
            jnp.where(second, 0.0, high),
            jnp.where(second, 0.0, low),
            jnp.where(second, high, 0.0),
            jnp.where(second, low, 0.0),
            jnp.zeros((12, 128), F32),
        ]
        stack[128:144, lanes] = jnp.concatenate(notes, axis=0).astype(BF16)
    rows = table_ref[2:4, :].astype(F32)
    own = jnp.concatenate([jnp.zeros((4, 128), F32), rows, jnp.zeros((10, 128), F32)], axis=0)
    stack[128:144, pl.ds(PANELS, 128)] = own.astype(BF16)
    for m in range(0, ROWS, 256):
        at = pl.ds(m, 256)
        owner = ((iota((256, 128), 0) + m) >> 3) == iota((256, 128), 1)
        values = dot_nt(hot_ref[at, :], stack[:, pl.ds(0, PANELS)])
        values += dot_nt(owner.astype(F32).astype(BF16), stack[:, pl.ds(PANELS, 128)])
        out[at, :] = values.astype(BF16)
        stores.append(pltpu.make_async_copy(out.at[at], out_hbm.at[at], out_sems.at[m // 256]))
        stores[-1].start()
    for copy in stores:
        copy.wait()


def surface_payload(plan, fields, halo, hot, place, table):
    return call(
        surface_kernel,
        (
            jax.ShapeDtypeStruct((WAVES, 16, 128), F32),
            jax.ShapeDtypeStruct((ROWS, 256), BF16),
        ),
        [VMEM] * 10,
        (HBM, HBM),
        [
            pltpu.VMEM((16, WAVES, 128), F32),
            pltpu.VMEM((256, PANELS + 128), BF16),
            pltpu.VMEM((ROWS, 256), BF16),
            pltpu.SemaphoreType.DMA((16,)),
            pltpu.SemaphoreType.DMA((4,)),
        ],
        limit=12,
    )(plan, *fields, *halo, hot, place, table)


def cluster_kernel(arrived_ref, clustered_ref, info_ref, hot, right):
    lane = iota((128, 128), 1)
    for m in range(0, ROWS, 128):
        lanes = pl.ds(m, 128)
        values = arrived_ref[lanes, 0:128].astype(F32)
        tail = arrived_ref[lanes, 128:256].astype(F32)
        notes = tail.T
        swapped = pltpu.roll(values, 64, 1)
        for half in range(2):
            slot = notes[2 * half : 2 * half + 1] * 128.0 + notes[2 * half + 1 : 2 * half + 2]
            info_ref[half : half + 1, lanes] = slot
            at = half * ROWS + m
            place = slot.astype(jnp.int32) & 1023
            hot[:, pl.ds(at, 128)] = hot_block(1024, place)
            both = jnp.where((lane < 64) == (half == 0), values, swapped)
            upper = tail[:, 2 * half : 2 * half + 1] >= 8.0
            right[pl.ds(at, 128), :] = jnp.where(upper == (lane >= 64), both, 0.0).astype(BF16)
        info_ref[2:4, lanes] = notes[4:6]
        info_ref[4:8, lanes] = jnp.zeros((4, 128), F32)
    for m in range(0, 1024, 256):
        clustered_ref[pl.ds(m, 256), :] = dot(hot[pl.ds(m, 256), :], right[...]).astype(BF16)


def to_clusters(arrived):
    return call(
        cluster_kernel,
        (
            jax.ShapeDtypeStruct((1024, 128), BF16),
            jax.ShapeDtypeStruct((8, ROWS), F32),
        ),
        [VMEM],
        (VMEM,) * 2,
        [pltpu.VMEM((1024, PANELS), BF16), pltpu.VMEM((PANELS, 128), BF16)],
        limit=8,
    )(arrived)


def coeff_kernel(table_ref, clustered_ref, v_hbm, big_hbm, out_hbm, basis, coeff, packed, sems):
    del big_hbm
    parts = [
        pltpu.make_async_copy(v_hbm.at[pl.ds(m, 32)], basis.at[pl.ds(m, 32)], sems.at[m // 32])
        for m in range(0, PAIRS, 32)
    ]
    for copy in parts:
        copy.start()
    weights = [clustered_ref[pl.ds(q * 256, 256), :] for q in range(4)]
    weights = [jnp.concatenate(weights[q : q + 2], axis=1) for q in (0, 2)]
    for q in range(4):
        coeff[q, pl.ds(PAIRS * RANK, RANK), :] = jnp.zeros((RANK, 128), F32)
    for m in range(0, PAIRS, 16):
        if m % 32 == 0:
            parts[m // 32].wait()
        rows = basis[pl.ds(m, 16)].reshape(16 * RANK, CL)
        at = pl.ds(m * RANK, 16 * RANK)
        for q in range(2):
            got = dot(rows, weights[q])
            coeff[2 * q, at, :] = got[:, :128]
            coeff[2 * q + 1, at, :] = got[:, 128:]
    lane = iota((RANK, 128), 1)

    def put(t, c):
        both = []
        for s in range(2):
            p = table_ref[s * OWNERS + t]
            col = table_ref[(4 + s) * OWNERS + t]
            tile = coeff[col & 3, pl.ds(pl.multiple_of(p * RANK, RANK), RANK), :]
            both.append(pltpu.roll(tile, ((col >> 2) ^ s) * 64, 1))
        both = jnp.where(lane < 64, both[0], both[1])
        packed[t, :, 0:128] = both[0:16].astype(BF16)
        packed[t, :, 128:256] = both[16:32].astype(BF16)
        return c

    lax.fori_loop(0, OWNERS, put, 0, unroll=8)
    load([(packed, out_hbm.at[:, 64:80, :])], sems)


def add_coeff(table, clustered, far_v, big):
    return pl.pallas_call(
        coeff_kernel,
        out_shape=jax.ShapeDtypeStruct((OWNERS, 80, CL), BF16),
        in_specs=[SMEM, VMEM, HBM, HBM],
        out_specs=HBM,
        scratch_shapes=[
            pltpu.VMEM((PAIRS, RANK, CL), BF16),
            pltpu.VMEM((4, PAIRS * RANK + RANK, 128), F32),
            pltpu.VMEM((OWNERS, 16, CL), BF16),
            pltpu.SemaphoreType.DMA((4,)),
        ],
        input_output_aliases={3: 0},
        compiler_params=pltpu.CompilerParams(vmem_limit_bytes=TIGHT * 2**20),
        cost_estimate=pl.CostEstimate(flops=0, bytes_accessed=32 * 2**20, transcendentals=0),
    )(table, clustered, far_v, big)


def near_kernel(
    rel_ref,
    before_ref,
    own_ref,
    after_ref,
    info_ref,
    place_ref,
    blocks_ref,
    out_ref,
    unhot_hbm,
    hot_hbm,
    wide,
    unhot,
    hot,
    sems,
):
    c = pl.program_id(0)

    @pl.when(c == 0)
    def _():
        for k, ref in enumerate((before_ref, own_ref, after_ref)):
            for q in range(4):
                turned = ref[pl.ds(q * 256, 256), :].astype(F32).T.astype(BF16)
                wide[8 * k + q] = turned[0:64]
                wide[8 * k + 4 + q] = turned[64:128]

    lanes = pl.ds(pl.multiple_of(c * 256, 256), 256)
    info = info_ref[:, pl.ds(pl.multiple_of(lax.rem(c, 4) * 256, 256), 256)]
    slot = jnp.where(c < 4, info[0:1], info[1:2]).astype(jnp.int32)
    unhot[:, lanes] = hot_block(1024, slot & 1023)
    hot[:, lanes] = hot_block(ROWS, place_ref[3:4, lanes])
    total = jnp.zeros((WAVES, CL), F32)
    for k in range(9):
        total += dot_nt(wide[rel_ref[c * 9 + k]], blocks_ref[0, k])
    out_ref[0] = total

    @pl.when(c == 7)
    def _():
        load([(unhot, unhot_hbm), (hot, hot_hbm)], sems)


def near_product(relative, before, own, after, info, place, near_blocks):
    matrix = jax.ShapeDtypeStruct((1024, PANELS), BF16)
    return pl.pallas_call(
        near_kernel,
        out_shape=(jax.ShapeDtypeStruct((8, WAVES, CL), F32), matrix, matrix),
        grid_spec=pltpu.PrefetchScalarGridSpec(
            num_scalar_prefetch=1,
            grid=(8,),
            in_specs=[VMEM] * 5 + [pl.BlockSpec((1, 9, CL, CL), lambda c, r: (c, 0, 0, 0))],
            out_specs=(pl.BlockSpec((1, WAVES, CL), lambda c, r: (c, 0, 0)), HBM, HBM),
            scratch_shapes=[
                pltpu.VMEM((24, WAVES, CL), BF16),
                pltpu.VMEM((1024, PANELS), BF16),
                pltpu.VMEM((1024, PANELS), BF16),
                pltpu.SemaphoreType.DMA((2,)),
            ],
        ),
        compiler_params=pltpu.CompilerParams(vmem_limit_bytes=TIGHT * 2**20),
        cost_estimate=pl.CostEstimate(flops=0, bytes_accessed=512 * 2**20, transcendentals=0),
    )(relative, before, own, after, info, place, near_blocks)


def total_kernel(
    big_hbm,
    near_ref,
    hot_hbm,
    info_ref,
    out_hbm,
    coeffs,
    basis,
    hot,
    acc,
    masked,
    grid,
    out,
    sems,
    out_sems,
):
    copies = [pltpu.make_async_copy(big_hbm.at[:, 64:80, :], coeffs, sems.at[4])]
    for n in range(4):
        part = big_hbm.at[:, pl.ds(16 * n, 16), :]
        copies.append(pltpu.make_async_copy(part, basis.at[n], sems.at[n]))
    copies.append(pltpu.make_async_copy(hot_hbm, hot, sems.at[5]))
    for copy in copies:
        copy.start()
    spread = ((iota((128, 256), 0) >> 3) == (iota((128, 256), 1) >> 4)) & (
        (iota((128, 256), 0) & 7) == 0
    )
    spread = spread.astype(F32).astype(BF16)
    identity = (iota((128, 128), 0) == iota((128, 128), 1)).astype(F32).astype(BF16)
    copies[0].wait()
    for m in range(8):
        src = pl.ds(m * 16, 16)
        at = pl.ds(m * 256, 256)
        rows = dot(info_ref[:, pl.ds(m * 128, 128)].astype(BF16), spread)
        for part in range(2):
            mine = coeffs[src, :, pl.ds(part * 128, 128)].reshape(256, 128)
            turned = dot_nt(identity, mine).astype(BF16)
            for s in range(2):
                for cluster in range(8):
                    hit = (rows[2 + s : 3 + s] == float(cluster)).astype(F32).astype(BF16)
                    values = turned[s * 64 : s * 64 + 64] * hit
                    masked[2 * s + part, pl.ds(cluster * 64, 64), at] = values
    for n in range(4):
        copies[1 + n].wait()
        product = dot(masked[n], basis[n].reshape(2048, CL))
        if n == 0:
            acc[...] = product
        else:
            acc[...] += product
    for cluster in range(8):
        total = near_ref[cluster] + acc[pl.ds(cluster * 64, 64), :]
        grid[pl.ds((cluster >> 2) * 64, 64), pl.ds((cluster & 3) * 256, 256)] = total.astype(BF16)
    copies[5].wait()
    stores = []
    for m in range(0, ROWS, 256):
        at = pl.ds(m, 256)
        halves = []
        for half in range(2):
            got = dot(grid[...], hot[:, pl.ds(half * ROWS + m, 256)])
            upper = info_ref[half : half + 1, at] >= 1024.0
            halves.append(jnp.where(upper, got[64:128], got[0:64]))
        out[at, :] = jnp.concatenate(halves, axis=0).T.astype(BF16)
        stores.append(pltpu.make_async_copy(out.at[at], out_hbm.at[at], out_sems.at[m // 256]))
        stores[-1].start()
    for copy in stores:
        copy.wait()


def total_home(big, near, hot, info):
    return call(
        total_kernel,
        jax.ShapeDtypeStruct((ROWS, 128), BF16),
        [HBM, VMEM, HBM, VMEM],
        HBM,
        [
            pltpu.VMEM((OWNERS, 16, CL), BF16),
            pltpu.VMEM((4, OWNERS, 16, CL), BF16),
            pltpu.VMEM((1024, PANELS), BF16),
            pltpu.VMEM((512, CL), F32),
            pltpu.VMEM((4, 512, 2048), BF16),
            pltpu.VMEM((128, 1024), BF16),
            pltpu.VMEM((ROWS, 128), BF16),
            pltpu.SemaphoreType.DMA((6,)),
            pltpu.SemaphoreType.DMA((4,)),
        ],
        limit=TIGHT,
    )(big, near, hot, info)


def potential_kernel(returned_ref, hot_ref, place_ref, out_ref, turned, wide):
    for m in range(0, ROWS, 128):
        turned[:, pl.ds(m, 128)] = returned_ref[pl.ds(m, 128), :].astype(F32).T.astype(BF16)
    for x in range(0, 16, 2):
        lanes = pl.ds(x * 128, 256)
        got = dot(turned[...], hot_ref[:, lanes])
        got = jnp.where(place_ref[0:1, lanes] == 1, got[64:128], got[0:64])
        wide[:, x, :] = got[:, :128]
        wide[:, x + 1, :] = got[:, 128:]
    out_ref[...] = wide[...].astype(BF16)


def panel_potential(returned, hot, place):
    return call(
        potential_kernel,
        jax.ShapeDtypeStruct((WAVES, 16, 128), BF16),
        [VMEM] * 3,
        VMEM,
        [pltpu.VMEM((128, ROWS), BF16), pltpu.VMEM((WAVES, 16, 128), F32)],
    )(returned, hot, place)


def exchange(x):
    return lax.all_to_all(x, BOTH, split_axis=0, concat_axis=0, tiled=True)


def ring(axis, step):
    size = lax.axis_size(axis)
    return [(i, (i + step) % size) for i in range(size)]


def swap(axis, first):
    size = lax.axis_size(axis)
    pairs = [(i, (i + 1) % size) for i in range(first, size, 2)]
    return pairs + [(j, i) for i, j in pairs]


def body(
    elevation,
    velocity_pot,
    surface_coef,
    panel_slot,
    near_blocks,
    near_cols,
    far_v,
    far_u,
    far_rows,
    far_cols,
):
    per_owner, clusters = 8, 1024
    me = lax.axis_index(BOTH)
    *fields, plan, along_a, along_b, across_a, across_b = pack_edges(
        elevation, velocity_pot, panel_slot, far_rows, far_cols, surface_coef
    )
    along_a = lax.ppermute(along_a, "along", swap("along", 0))
    along_b = lax.ppermute(along_b, "along", swap("along", 1))
    across_a = lax.ppermute(across_a, "across", swap("across", 0))
    across_b = lax.ppermute(across_b, "across", swap("across", 1))
    hot, place, table = sender_order(plan)
    halo = (along_a, along_b, across_a, across_b)
    eta, payload = surface_payload(plan, fields, halo, hot, place, table)
    table = table.reshape(8 * 128)
    arrived = exchange(payload.reshape(OWNERS, 8, 256)).reshape(ROWS, 256)
    big = far_bucket(table, far_u)
    arrived, big = lax.optimization_barrier((arrived, big))

    clustered, info = to_clusters(arrived)
    before = lax.ppermute(clustered, BOTH, ring(BOTH, 1))
    after = lax.ppermute(clustered, BOTH, ring(BOTH, -1))
    big = add_coeff(table, clustered, far_v, big)
    before, after, big = lax.optimization_barrier((before, after, big))
    big = exchange(big)

    relative = (near_cols - (me * per_owner - per_owner)) % clusters
    near, unhot, hot = near_product(
        relative.reshape(72), before, clustered, after, info, place, near_blocks
    )

    home = total_home(big, near, unhot, info).reshape(OWNERS, 8, 128)
    returned = exchange(home).reshape(ROWS, 128)
    potential = panel_potential(returned, hot, place)
    return (eta, potential)


def solution(mesh):
    in_specs = (
        P(None, "along", "across"),
        P(None, "along", "across"),
        P("along", "across"),
        P("along", "across"),
        P(BOTH, None, None, None),
        P(BOTH, None),
        P(BOTH, None, None),
        P(BOTH, None, None),
        P(BOTH),
        P(BOTH),
    )
    out_specs = (P(None, "along", "across"), P(None, "along", "across"))
    return jax.shard_map(body, mesh=mesh, in_specs=in_specs, out_specs=out_specs, check_vma=False)
```

```python
import jax
import jax.numpy as jnp
from jax import lax
from jax.experimental import pallas as pl
from jax.experimental.pallas import tpu as pltpu
from jax.sharding import PartitionSpec as P

CL = 256
BOTH = ("along", "across")
OWNERS = 128
PAIRS = 128
RANK = 32
WAVES = 64
ROWS = 1024
PANELS = 2048
BF16 = jnp.bfloat16
F32 = jnp.float32
WIDE = 56
PACK = 56
TIGHT = 52
VMEM = pl.BlockSpec(memory_space=pltpu.VMEM)
SMEM = pl.BlockSpec(memory_space=pltpu.SMEM)
HBM = pl.BlockSpec(memory_space=pltpu.HBM)


def call(kernel, out_shape, in_specs, out_specs, scratch=(), limit=4, cost=0):
    return pl.pallas_call(
        kernel,
        out_shape=out_shape,
        in_specs=in_specs,
        out_specs=out_specs,
        scratch_shapes=list(scratch),
        compiler_params=pltpu.CompilerParams(vmem_limit_bytes=limit * 2**20),
        cost_estimate=pl.CostEstimate(flops=0, bytes_accessed=cost, transcendentals=0),
    )


def hot_block(count, row):
    index = iota((count, row.shape[1]), 0).astype(jnp.int16)
    hit = index == row.astype(jnp.int16)
    return jnp.where(hit, jnp.ones((), BF16), jnp.zeros((), BF16))


def iota(shape, dim):
    return lax.broadcasted_iota(jnp.int32, shape, dim)


def dot(a, b):
    return jnp.dot(a, b, preferred_element_type=F32)


def dot_nt(a, b):
    return lax.dot_general(a, b, (((1,), (1,)), ((), ())), preferred_element_type=F32)


def bucket_kernel(table_ref, u_hbm, out_hbm, values, packed, sems):
    load([(u_hbm, values)], sems)

    def put(t, c):
        for s in range(2):
            p = table_ref[s * OWNERS + t]
            mine = values[jnp.minimum(p, PAIRS - 1)]
            packed[t, pl.ds(s * RANK, RANK), :] = jnp.where(p < PAIRS, mine, jnp.zeros_like(mine))
        return c

    lax.fori_loop(0, OWNERS, put, 0, unroll=4)
    load([(packed, out_hbm.at[:, 0:64, :])], sems)


def far_bucket(table, far_u):
    return call(
        bucket_kernel,
        jax.ShapeDtypeStruct((OWNERS, 80, CL), BF16),
        [SMEM, HBM],
        HBM,
        [
            pltpu.VMEM((PAIRS, RANK, CL), BF16),
            pltpu.VMEM((OWNERS, 2 * RANK, CL), BF16),
            pltpu.SemaphoreType.DMA((1,)),
        ],
        limit=TIGHT,
        cost=9 * 2**20,
    )(table, far_u)


def load(pairs, sems):
    copies = [pltpu.make_async_copy(a, b, sems.at[i]) for i, (a, b) in enumerate(pairs)]
    for copy in copies:
        copy.start()
    for copy in copies:
        copy.wait()


def pack_kernel(
    elevation_hbm,
    phi_hbm,
    slot_hbm,
    rows_hbm,
    cols_hbm,
    coef_hbm,
    fields_ref,
    plan_ref,
    along_a,
    along_b,
    across_a,
    across_b,
    ints,
    sems,
    field_sems,
):
    small = [
        (slot_hbm, ints.at[0:16]),
        (rows_hbm, ints.at[16:17]),
        (cols_hbm, ints.at[17:18]),
        (coef_hbm, plan_ref.at[24:40]),
    ]
    small = [pltpu.make_async_copy(a, b, sems.at[i]) for i, (a, b) in enumerate(small)]
    fields = []
    for x in range(16):
        fields.append((elevation_hbm.at[:, x, :], fields_ref.at[x]))
        fields.append((phi_hbm.at[:, x, :], fields_ref.at[16 + x]))
    fields = [pltpu.make_async_copy(a, b, field_sems.at[i]) for i, (a, b) in enumerate(fields)]
    for copy in fields + small:
        copy.start()
    for copy in small:
        copy.wait()
    plan_ref[0:24, :] = ints[...].astype(F32)
    even_row = lax.rem(lax.axis_index("along"), 2) == 0
    even_col = lax.rem(lax.axis_index("across"), 2) == 0
    for copy in fields:
        copy.wait()
    lane = iota((WAVES, 128), 1)
    right = jnp.zeros((WAVES, 128), F32)
    left = jnp.zeros((WAVES, 128), F32)
    for k in range(2):
        for x in range(16):
            values = fields_ref[16 * k + x]
            at = 64 * k + 2 * x
            here = (lane >> 1) == at // 2
            right = jnp.where(here, pltpu.roll(values, (at + 2) % 128, 1), right)
            left = jnp.where(here, pltpu.roll(values, at, 1) if at else values, left)
    across_a[...] = jnp.where(even_col, right, left)
    across_b[...] = jnp.where(even_col, left, right)
    upward = fields_ref[16]
    for k, downward in enumerate([fields_ref[n] for n in (14, 15, 30, 31)]):
        along_a[k] = jnp.where(even_row, downward, upward)
        along_b[k] = jnp.where(even_row, upward, downward)


def pack_edges(elevation, velocity_pot, panel_slot, far_rows, far_cols, coef):
    side = jax.ShapeDtypeStruct((WAVES, 128), F32)
    rows = jax.ShapeDtypeStruct((4, WAVES, 128), F32)
    tracks = jax.ShapeDtypeStruct((32, WAVES, 128), F32)
    return call(
        pack_kernel,
        (tracks, jax.ShapeDtypeStruct((40, 128), F32), rows, rows, side, side),
        [HBM] * 6,
        (VMEM,) * 6,
        [
            pltpu.VMEM((24, 128), jnp.int32),
            pltpu.SemaphoreType.DMA((4,)),
            pltpu.SemaphoreType.DMA((32,)),
        ],
        limit=PACK,
    )(
        elevation,
        velocity_pot,
        panel_slot,
        far_rows.reshape(1, PAIRS),
        far_cols.reshape(1, PAIRS),
        coef,
    )


def order_kernel(plan_ref, hot_ref, place_ref, table_ref):
    up = iota((128, 128), 0) < iota((128, 128), 1)
    weights = jnp.concatenate([up.astype(F32), jnp.ones((128, 128), F32)], axis=1).astype(BF16)
    seen = jnp.zeros((128, 128), F32)
    for x in range(16):
        slot = plan_ref[x : x + 1, :].astype(jnp.int32)
        dest, local = slot >> 11, slot & (PANELS - 1)
        hits = iota((128, 128), 0) == dest
        sums = dot(hits.astype(F32).astype(BF16), weights)
        rank = jnp.sum(jnp.where(hits, sums[:, :128] + seen, 0.0), axis=0, keepdims=True)
        seen = seen + sums[:, 128:]
        rank = rank.astype(jnp.int32)
        row = dest * 8 + (rank & 7)
        lanes = pl.ds(x * 128, 128)
        hot_ref[:, lanes] = hot_block(ROWS, row)
        place_ref[0:1, lanes] = rank >> 3
        place_ref[1:2, lanes] = local >> 7
        place_ref[2:3, lanes] = local & 127
        place_ref[3:4, lanes] = row
        place_ref[4:8, lanes] = jnp.zeros((4, 128), jnp.int32)

    turned = [
        jnp.broadcast_to(plan_ref[k : k + 1, :], (128, 128)).T.astype(jnp.int32)
        for k in range(16, 18)
    ]
    hits = (turned[0] >> 3) == iota((128, 128), 1)
    down = (iota((128, 128), 0) > iota((128, 128), 1)).astype(F32).astype(BF16)
    rank = dot(down, hits.astype(F32).astype(BF16))
    values = (iota((128, 128), 0) - PAIRS, (turned[0] & 7) - 8, turned[1] & 7)
    for k, (value, base) in enumerate(zip(values, (PAIRS, 8, 0))):
        for s in range(2):
            chosen = hits & (rank == float(s))
            found = jnp.sum(jnp.where(chosen, value.astype(F32), 0.0), axis=0, keepdims=True)
            table_ref[2 * k + s : 2 * k + s + 1, :] = found.astype(jnp.int32) + base
    table_ref[6:8, :] = jnp.zeros((2, 128), jnp.int32)


def sender_order(plan):
    return call(
        order_kernel,
        (
            jax.ShapeDtypeStruct((ROWS, PANELS), BF16),
            jax.ShapeDtypeStruct((8, PANELS), jnp.int32),
            jax.ShapeDtypeStruct((8, 128), jnp.int32),
        ),
        [VMEM],
        (VMEM,) * 3,
        limit=8,
    )(plan)


def surface_kernel(
    plan_ref,
    fields,
    along_a,
    along_b,
    across_a,
    across_b,
    hot_ref,
    place_ref,
    table_ref,
    eta_hbm,
    out_hbm,
    eta_tracks,
    stack,
    out,
    eta_sems,
    out_sems,
):
    row, col = lax.axis_index("along"), lax.axis_index("across")
    first_row, last_row = row == 0, row == lax.axis_size("along") - 1
    first_col, last_col = col == 0, col == lax.axis_size("across") - 1
    lane = iota((WAVES, 128), 1)
    even_row, even_col = lax.rem(row, 2) == 0, lax.rem(col, 2) == 0
    west = jnp.where(even_col, across_b[...], across_a[...])
    east = jnp.where(even_col, across_a[...], across_b[...])
    west, east = jnp.where(first_col, 0.0, west), jnp.where(last_col, 0.0, east)
    above = [jnp.where(even_row, along_b[k], along_a[k]) for k in range(4)]
    above = [jnp.where(first_row, 0.0, values) for values in above]
    below = jnp.where(last_row, 0.0, jnp.where(even_row, along_a[0], along_b[0]))

    def views(f, x, k):
        x1 = fields[16 * k + x - 1] if x >= 1 else above[2 * k + 1]
        x2 = fields[16 * k + x - 2] if x >= 2 else above[2 * k + x]
        at = 64 * k + 2 * x
        left = pltpu.roll(west, 128 - at, 1) if at else west
        right = pltpu.roll(east, 126 - at, 1)
        w2 = jnp.where(lane < 2, left, pltpu.roll(f, 2, 1))
        w1 = jnp.where(lane < 1, pltpu.roll(left, 127, 1), pltpu.roll(f, 1, 1))
        e2 = jnp.where(lane >= 126, right, pltpu.roll(f, 126, 1))
        e1 = jnp.where(lane >= 127, pltpu.roll(right, 1, 1), pltpu.roll(f, 127, 1))
        up = 0.5 * (3.0 * f - 4.0 * x1 + x2)
        across = (w2 - 8.0 * w1 + 8.0 * e1 - e2) * (1.0 / 12.0)
        return x1, w1, e1, up, across

    stack[128:256, :] = jnp.zeros((128, PANELS + 128), BF16)
    stack[0:128, pl.ds(PANELS, 128)] = jnp.zeros((128, 128), BF16)
    stores = []
    for x in range(16):
        e, p = fields[x], fields[16 + x]
        _, _, _, up, across = views(e, x, 0)
        p1, pw, pe, phi_up, phi_across = views(p, x, 1)
        next_row = fields[17 + x] if x < 15 else below
        curvature = next_row + p1 + pe + pw - 4.0 * p
        eta = e - 0.4 * up + 0.3 * across + plan_ref[24 + x : 25 + x, :] * curvature
        eta_tracks[x] = eta
        stores.append(pltpu.make_async_copy(eta_tracks.at[x], eta_hbm.at[:, x, :], eta_sems.at[x]))
        stores[x].start()
        values = p - 0.4 * phi_up + 0.3 * phi_across - 0.5 * eta
        lanes = pl.ds(x * 128, 128)
        place = place_ref[:, lanes]
        second = place[0:1] == 1
        stack[0:64, lanes] = jnp.where(second, 0.0, values).astype(BF16)
        stack[64:128, lanes] = jnp.where(second, values, 0.0).astype(BF16)
        high, low = place[1:2].astype(F32), place[2:3].astype(F32)
        notes = [
            jnp.where(second, 0.0, high),
            jnp.where(second, 0.0, low),
            jnp.where(second, high, 0.0),
            jnp.where(second, low, 0.0),
            jnp.zeros((12, 128), F32),
        ]
        stack[128:144, lanes] = jnp.concatenate(notes, axis=0).astype(BF16)
    rows = table_ref[2:4, :].astype(F32)
    own = jnp.concatenate([jnp.zeros((4, 128), F32), rows, jnp.zeros((10, 128), F32)], axis=0)
    stack[128:144, pl.ds(PANELS, 128)] = own.astype(BF16)
    for m in range(0, ROWS, 256):
        at = pl.ds(m, 256)
        owner = ((iota((256, 128), 0) + m) >> 3) == iota((256, 128), 1)
        values = dot_nt(hot_ref[at, :], stack[:, pl.ds(0, PANELS)])
        values += dot_nt(owner.astype(F32).astype(BF16), stack[:, pl.ds(PANELS, 128)])
        out[at, :] = values.astype(BF16)
        stores.append(pltpu.make_async_copy(out.at[at], out_hbm.at[at], out_sems.at[m // 256]))
        stores[-1].start()
    for copy in stores:
        copy.wait()


def surface_payload(plan, fields, halo, hot, place, table):
    return call(
        surface_kernel,
        (
            jax.ShapeDtypeStruct((WAVES, 16, 128), F32),
            jax.ShapeDtypeStruct((ROWS, 256), BF16),
        ),
        [VMEM] * 9,
        (HBM, HBM),
        [
            pltpu.VMEM((16, WAVES, 128), F32),
            pltpu.VMEM((256, PANELS + 128), BF16),
            pltpu.VMEM((ROWS, 256), BF16),
            pltpu.SemaphoreType.DMA((16,)),
            pltpu.SemaphoreType.DMA((4,)),
        ],
        limit=12,
    )(plan, fields, *halo, hot, place, table)


def cluster_kernel(arrived_ref, clustered_ref, info_ref, hot, right):
    lane = iota((128, 128), 1)
    for m in range(0, ROWS, 128):
        lanes = pl.ds(m, 128)
        values = arrived_ref[lanes, 0:128].astype(F32)
        tail = arrived_ref[lanes, 128:256].astype(F32)
        notes = tail.T
        swapped = pltpu.roll(values, 64, 1)
        for half in range(2):
            slot = notes[2 * half : 2 * half + 1] * 128.0 + notes[2 * half + 1 : 2 * half + 2]
            info_ref[half : half + 1, lanes] = slot
            at = half * ROWS + m
            place = slot.astype(jnp.int32) & 1023
            hot[:, pl.ds(at, 128)] = hot_block(1024, place)
            both = jnp.where((lane < 64) == (half == 0), values, swapped)
            upper = tail[:, 2 * half : 2 * half + 1] >= 8.0
            right[pl.ds(at, 128), :] = jnp.where(upper == (lane >= 64), both, 0.0).astype(BF16)
        info_ref[2:4, lanes] = notes[4:6]
        info_ref[4:8, lanes] = jnp.zeros((4, 128), F32)
    for m in range(0, 1024, 256):
        clustered_ref[pl.ds(m, 256), :] = dot(hot[pl.ds(m, 256), :], right[...]).astype(BF16)


def to_clusters(arrived):
    return call(
        cluster_kernel,
        (
            jax.ShapeDtypeStruct((1024, 128), BF16),
            jax.ShapeDtypeStruct((8, ROWS), F32),
        ),
        [VMEM],
        (VMEM,) * 2,
        [pltpu.VMEM((1024, PANELS), BF16), pltpu.VMEM((PANELS, 128), BF16)],
        limit=8,
    )(arrived)


def coeff_kernel(table_ref, clustered_ref, v_hbm, big_hbm, out_hbm, basis, coeff, packed, sems):
    del big_hbm
    parts = [
        pltpu.make_async_copy(v_hbm.at[pl.ds(m, 32)], basis.at[pl.ds(m, 32)], sems.at[m // 32])
        for m in range(0, PAIRS, 32)
    ]
    for copy in parts:
        copy.start()
    weights = [clustered_ref[pl.ds(q * 256, 256), :] for q in range(4)]
    weights = [jnp.concatenate(weights[q : q + 2], axis=1) for q in (0, 2)]
    for q in range(4):
        coeff[q, pl.ds(PAIRS * RANK, RANK), :] = jnp.zeros((RANK, 128), F32)
    for m in range(0, PAIRS, 16):
        if m % 32 == 0:
            parts[m // 32].wait()
        rows = basis[pl.ds(m, 16)].reshape(16 * RANK, CL)
        at = pl.ds(m * RANK, 16 * RANK)
        for q in range(2):
            got = dot(rows, weights[q])
            coeff[2 * q, at, :] = got[:, :128]
            coeff[2 * q + 1, at, :] = got[:, 128:]
    lane = iota((RANK, 128), 1)

    def put(t, c):
        both = []
        for s in range(2):
            p = table_ref[s * OWNERS + t]
            col = table_ref[(4 + s) * OWNERS + t]
            tile = coeff[col & 3, pl.ds(pl.multiple_of(p * RANK, RANK), RANK), :]
            both.append(pltpu.roll(tile, ((col >> 2) ^ s) * 64, 1))
        both = jnp.where(lane < 64, both[0], both[1])
        packed[t, :, 0:128] = both[0:16].astype(BF16)
        packed[t, :, 128:256] = both[16:32].astype(BF16)
        return c

    lax.fori_loop(0, OWNERS, put, 0, unroll=8)
    load([(packed, out_hbm.at[:, 64:80, :])], sems)


def add_coeff(table, clustered, far_v, big):
    return pl.pallas_call(
        coeff_kernel,
        out_shape=jax.ShapeDtypeStruct((OWNERS, 80, CL), BF16),
        in_specs=[SMEM, VMEM, HBM, HBM],
        out_specs=HBM,
        scratch_shapes=[
            pltpu.VMEM((PAIRS, RANK, CL), BF16),
            pltpu.VMEM((4, PAIRS * RANK + RANK, 128), F32),
            pltpu.VMEM((OWNERS, 16, CL), BF16),
            pltpu.SemaphoreType.DMA((4,)),
        ],
        input_output_aliases={3: 0},
        compiler_params=pltpu.CompilerParams(vmem_limit_bytes=TIGHT * 2**20),
        cost_estimate=pl.CostEstimate(flops=0, bytes_accessed=32 * 2**20, transcendentals=0),
    )(table, clustered, far_v, big)


def near_kernel(
    rel_ref,
    before_ref,
    own_ref,
    after_ref,
    info_ref,
    place_ref,
    blocks_ref,
    out_ref,
    unhot_hbm,
    hot_hbm,
    wide,
    unhot,
    hot,
    sems,
):
    c = pl.program_id(0)

    @pl.when(c == 0)
    def _():
        for k, ref in enumerate((before_ref, own_ref, after_ref)):
            for q in range(4):
                turned = ref[pl.ds(q * 256, 256), :].astype(F32).T.astype(BF16)
                wide[8 * k + q] = turned[0:64]
                wide[8 * k + 4 + q] = turned[64:128]

    lanes = pl.ds(pl.multiple_of(c * 256, 256), 256)
    info = info_ref[:, pl.ds(pl.multiple_of(lax.rem(c, 4) * 256, 256), 256)]
    slot = jnp.where(c < 4, info[0:1], info[1:2]).astype(jnp.int32)
    unhot[:, lanes] = hot_block(1024, slot & 1023)
    hot[:, lanes] = hot_block(ROWS, place_ref[3:4, lanes])
    total = jnp.zeros((WAVES, CL), F32)
    for k in range(9):
        total += dot_nt(wide[rel_ref[c * 9 + k]], blocks_ref[0, k])
    out_ref[0] = total

    @pl.when(c == 7)
    def _():
        load([(unhot, unhot_hbm), (hot, hot_hbm)], sems)


def near_product(relative, before, own, after, info, place, near_blocks):
    matrix = jax.ShapeDtypeStruct((1024, PANELS), BF16)
    return pl.pallas_call(
        near_kernel,
        out_shape=(jax.ShapeDtypeStruct((8, WAVES, CL), F32), matrix, matrix),
        grid_spec=pltpu.PrefetchScalarGridSpec(
            num_scalar_prefetch=1,
            grid=(8,),
            in_specs=[VMEM] * 5 + [pl.BlockSpec((1, 9, CL, CL), lambda c, r: (c, 0, 0, 0))],
            out_specs=(pl.BlockSpec((1, WAVES, CL), lambda c, r: (c, 0, 0)), HBM, HBM),
            scratch_shapes=[
                pltpu.VMEM((24, WAVES, CL), BF16),
                pltpu.VMEM((1024, PANELS), BF16),
                pltpu.VMEM((1024, PANELS), BF16),
                pltpu.SemaphoreType.DMA((2,)),
            ],
        ),
        compiler_params=pltpu.CompilerParams(vmem_limit_bytes=TIGHT * 2**20),
        cost_estimate=pl.CostEstimate(flops=0, bytes_accessed=512 * 2**20, transcendentals=0),
    )(relative, before, own, after, info, place, near_blocks)


def total_kernel(
    big_hbm,
    near_ref,
    hot_hbm,
    info_ref,
    out_hbm,
    coeffs,
    basis,
    hot,
    acc,
    masked,
    grid,
    out,
    sems,
    out_sems,
):
    copies = [pltpu.make_async_copy(big_hbm.at[:, 64:80, :], coeffs, sems.at[4])]
    for n in range(4):
        part = big_hbm.at[:, pl.ds(16 * n, 16), :]
        copies.append(pltpu.make_async_copy(part, basis.at[n], sems.at[n]))
    copies.append(pltpu.make_async_copy(hot_hbm, hot, sems.at[5]))
    for copy in copies:
        copy.start()
    spread = ((iota((128, 256), 0) >> 3) == (iota((128, 256), 1) >> 4)) & (
        (iota((128, 256), 0) & 7) == 0
    )
    spread = spread.astype(F32).astype(BF16)
    copies[0].wait()
    for m in range(8):
        src = pl.ds(m * 16, 16)
        at = pl.ds(m * 256, 256)
        rows = dot(info_ref[:, pl.ds(m * 128, 128)].astype(BF16), spread)
        for part in range(2):
            mine = coeffs[src, :, pl.ds(part * 128, 128)].reshape(256, 128)
            turned = mine.astype(F32).T.astype(BF16)
            for s in range(2):
                for cluster in range(8):
                    hit = (rows[2 + s : 3 + s] == float(cluster)).astype(F32).astype(BF16)
                    values = turned[s * 64 : s * 64 + 64] * hit
                    masked[2 * s + part, pl.ds(cluster * 64, 64), at] = values
    for copy in copies[1:]:
        copy.wait()
    for r in range(0, 512, 128):
        at = pl.ds(r, 128)
        product = dot(masked[0, at, :], basis[0].reshape(2048, CL))
        for n in range(1, 4):
            product += dot(masked[n, at, :], basis[n].reshape(2048, CL))
        acc[at, :] = product
    for cluster in range(8):
        total = near_ref[cluster] + acc[pl.ds(cluster * 64, 64), :]
        grid[pl.ds((cluster >> 2) * 64, 64), pl.ds((cluster & 3) * 256, 256)] = total.astype(BF16)
    stores = []
    for m in range(0, ROWS, 256):
        at = pl.ds(m, 256)
        halves = []
        for half in range(2):
            got = dot(grid[...], hot[:, pl.ds(half * ROWS + m, 256)])
            upper = info_ref[half : half + 1, at] >= 1024.0
            halves.append(jnp.where(upper, got[64:128], got[0:64]))
        out[at, :] = jnp.concatenate(halves, axis=0).T.astype(BF16)
        stores.append(pltpu.make_async_copy(out.at[at], out_hbm.at[at], out_sems.at[m // 256]))
        stores[-1].start()
    for copy in stores:
        copy.wait()


def total_home(big, near, hot, info):
    return call(
        total_kernel,
        jax.ShapeDtypeStruct((ROWS, 128), BF16),
        [HBM, VMEM, HBM, VMEM],
        HBM,
        [
            pltpu.VMEM((OWNERS, 16, CL), BF16),
            pltpu.VMEM((4, OWNERS, 16, CL), BF16),
            pltpu.VMEM((1024, PANELS), BF16),
            pltpu.VMEM((512, CL), F32),
            pltpu.VMEM((4, 512, 2048), BF16),
            pltpu.VMEM((128, 1024), BF16),
            pltpu.VMEM((ROWS, 128), BF16),
            pltpu.SemaphoreType.DMA((6,)),
            pltpu.SemaphoreType.DMA((4,)),
        ],
        limit=TIGHT,
    )(big, near, hot, info)


def potential_kernel(returned_ref, hot_ref, place_ref, out_ref, turned, wide):
    for m in range(0, ROWS, 128):
        turned[:, pl.ds(m, 128)] = returned_ref[pl.ds(m, 128), :].astype(F32).T.astype(BF16)
    for x in range(0, 16, 2):
        lanes = pl.ds(x * 128, 256)
        got = dot(turned[...], hot_ref[:, lanes])
        got = jnp.where(place_ref[0:1, lanes] == 1, got[64:128], got[0:64])
        wide[:, x, :] = got[:, :128]
        wide[:, x + 1, :] = got[:, 128:]
    out_ref[...] = wide[...].astype(BF16)


def panel_potential(returned, hot, place):
    return call(
        potential_kernel,
        jax.ShapeDtypeStruct((WAVES, 16, 128), BF16),
        [VMEM] * 3,
        VMEM,
        [pltpu.VMEM((128, ROWS), BF16), pltpu.VMEM((WAVES, 16, 128), F32)],
    )(returned, hot, place)


def exchange(x):
    return lax.all_to_all(x, BOTH, split_axis=0, concat_axis=0, tiled=True)


def ring(axis, step):
    size = lax.axis_size(axis)
    return [(i, (i + step) % size) for i in range(size)]


def swap(axis, first):
    size = lax.axis_size(axis)
    pairs = [(i, (i + 1) % size) for i in range(first, size, 2)]
    return pairs + [(j, i) for i, j in pairs]


def body(
    elevation,
    velocity_pot,
    surface_coef,
    panel_slot,
    near_blocks,
    near_cols,
    far_v,
    far_u,
    far_rows,
    far_cols,
):
    per_owner, clusters = 8, 1024
    me = lax.axis_index(BOTH)
    fields, plan, along_a, along_b, across_a, across_b = pack_edges(
        elevation, velocity_pot, panel_slot, far_rows, far_cols, surface_coef
    )
    along_a = lax.ppermute(along_a, "along", swap("along", 0))
    along_b = lax.ppermute(along_b, "along", swap("along", 1))
    across_a = lax.ppermute(across_a, "across", swap("across", 0))
    across_b = lax.ppermute(across_b, "across", swap("across", 1))
    hot, place, table = sender_order(plan)
    halo = (along_a, along_b, across_a, across_b)
    eta, payload = surface_payload(plan, fields, halo, hot, place, table)
    table = table.reshape(8 * 128)
    arrived = exchange(payload.reshape(OWNERS, 8, 256)).reshape(ROWS, 256)
    big = far_bucket(table, far_u)
    arrived, big = lax.optimization_barrier((arrived, big))

    clustered, info = to_clusters(arrived)
    before = lax.ppermute(clustered, BOTH, ring(BOTH, 1))
    after = lax.ppermute(clustered, BOTH, ring(BOTH, -1))
    big = add_coeff(table, clustered, far_v, big)
    before, after, big = lax.optimization_barrier((before, after, big))
    big = exchange(big)

    relative = (near_cols - (me * per_owner - per_owner)) % clusters
    near, unhot, hot = near_product(
        relative.reshape(72), before, clustered, after, info, place, near_blocks
    )

    home = total_home(big, near, unhot, info).reshape(OWNERS, 8, 128)
    returned = exchange(home).reshape(ROWS, 128)
    potential = panel_potential(returned, hot, place)
    return (eta, potential)


def solution(mesh):
    in_specs = (
        P(None, "along", "across"),
        P(None, "along", "across"),
        P("along", "across"),
        P("along", "across"),
        P(BOTH, None, None, None),
        P(BOTH, None),
        P(BOTH, None, None),
        P(BOTH, None, None),
        P(BOTH),
        P(BOTH),
    )
    out_specs = (P(None, "along", "across"), P(None, "along", "across"))
    return jax.shard_map(body, mesh=mesh, in_specs=in_specs, out_specs=out_specs, check_vma=False)
```

```python
import jax
import jax.numpy as jnp
from jax import lax
from jax.experimental import pallas as pl
from jax.experimental.pallas import tpu as pltpu
from jax.sharding import PartitionSpec as P

CL = 256
BOTH = ("along", "across")
OWNERS = 128
PAIRS = 128
RANK = 32
WAVES = 64
ROWS = 1024
PANELS = 2048
BF16 = jnp.bfloat16
F32 = jnp.float32
WIDE = 56
PACK = 56
TIGHT = 52
VMEM = pl.BlockSpec(memory_space=pltpu.VMEM)
SMEM = pl.BlockSpec(memory_space=pltpu.SMEM)
HBM = pl.BlockSpec(memory_space=pltpu.HBM)


def call(kernel, out_shape, in_specs, out_specs, scratch=(), limit=4, cost=0):
    return pl.pallas_call(
        kernel,
        out_shape=out_shape,
        in_specs=in_specs,
        out_specs=out_specs,
        scratch_shapes=list(scratch),
        compiler_params=pltpu.CompilerParams(vmem_limit_bytes=limit * 2**20),
        cost_estimate=pl.CostEstimate(flops=0, bytes_accessed=cost, transcendentals=0),
    )


def hot_block(count, row):
    index = iota((count, row.shape[1]), 0).astype(jnp.int16)
    hit = index == row.astype(jnp.int16)
    return jnp.where(hit, jnp.ones((), BF16), jnp.zeros((), BF16))


def iota(shape, dim):
    return lax.broadcasted_iota(jnp.int32, shape, dim)


def dot(a, b):
    return jnp.dot(a, b, preferred_element_type=F32)


def dot_nt(a, b):
    return lax.dot_general(a, b, (((1,), (1,)), ((), ())), preferred_element_type=F32)


def bucket_kernel(table_ref, u_hbm, out_hbm, values, packed, sems):
    load([(u_hbm, values)], sems)

    def put(t, c):
        for s in range(2):
            p = table_ref[s * OWNERS + t]
            mine = values[jnp.minimum(p, PAIRS - 1)]
            packed[t, pl.ds(s * RANK, RANK), :] = jnp.where(p < PAIRS, mine, jnp.zeros_like(mine))
        return c

    lax.fori_loop(0, OWNERS, put, 0, unroll=4)
    load([(packed, out_hbm.at[:, 0:64, :])], sems)


def far_bucket(table, far_u):
    return call(
        bucket_kernel,
        jax.ShapeDtypeStruct((OWNERS, 80, CL), BF16),
        [SMEM, HBM],
        HBM,
        [
            pltpu.VMEM((PAIRS, RANK, CL), BF16),
            pltpu.VMEM((OWNERS, 2 * RANK, CL), BF16),
            pltpu.SemaphoreType.DMA((1,)),
        ],
        limit=TIGHT,
        cost=9 * 2**20,
    )(table, far_u)


def load(pairs, sems):
    copies = [pltpu.make_async_copy(a, b, sems.at[i]) for i, (a, b) in enumerate(pairs)]
    for copy in copies:
        copy.start()
    for copy in copies:
        copy.wait()


def pack_kernel(
    elevation_hbm,
    phi_hbm,
    slot_hbm,
    rows_hbm,
    cols_hbm,
    coef_hbm,
    fields_ref,
    plan_ref,
    along_a,
    along_b,
    across_a,
    across_b,
    ints,
    sems,
    field_sems,
):
    small = [
        (slot_hbm, ints.at[0:16]),
        (rows_hbm, ints.at[16:17]),
        (cols_hbm, ints.at[17:18]),
        (coef_hbm, plan_ref.at[24:40]),
    ]
    small = [pltpu.make_async_copy(a, b, sems.at[i]) for i, (a, b) in enumerate(small)]
    fields = []
    for x in range(16):
        fields.append((elevation_hbm.at[:, x, :], fields_ref.at[x]))
        fields.append((phi_hbm.at[:, x, :], fields_ref.at[16 + x]))
    fields = [pltpu.make_async_copy(a, b, field_sems.at[i]) for i, (a, b) in enumerate(fields)]
    for copy in fields + small:
        copy.start()
    for copy in small:
        copy.wait()
    plan_ref[0:24, :] = ints[...].astype(F32)
    even_row = lax.rem(lax.axis_index("along"), 2) == 0
    even_col = lax.rem(lax.axis_index("across"), 2) == 0
    for copy in fields:
        copy.wait()
    lane = iota((WAVES, 128), 1)
    right = jnp.zeros((WAVES, 128), F32)
    left = jnp.zeros((WAVES, 128), F32)
    for k in range(2):
        for x in range(16):
            values = fields_ref[16 * k + x]
            at = 64 * k + 2 * x
            here = (lane >> 1) == at // 2
            right = jnp.where(here, pltpu.roll(values, (at + 2) % 128, 1), right)
            left = jnp.where(here, pltpu.roll(values, at, 1) if at else values, left)
    across_a[...] = jnp.where(even_col, right, left)
    across_b[...] = jnp.where(even_col, left, right)
    upward = fields_ref[16]
    for k, downward in enumerate([fields_ref[n] for n in (14, 15, 30, 31)]):
        along_a[k] = jnp.where(even_row, downward, upward)
        along_b[k] = jnp.where(even_row, upward, downward)


def pack_edges(elevation, velocity_pot, panel_slot, far_rows, far_cols, coef):
    side = jax.ShapeDtypeStruct((WAVES, 128), F32)
    rows = jax.ShapeDtypeStruct((4, WAVES, 128), F32)
    tracks = jax.ShapeDtypeStruct((32, WAVES, 128), F32)
    return call(
        pack_kernel,
        (tracks, jax.ShapeDtypeStruct((40, 128), F32), rows, rows, side, side),
        [HBM] * 6,
        (VMEM,) * 6,
        [
            pltpu.VMEM((24, 128), jnp.int32),
            pltpu.SemaphoreType.DMA((4,)),
            pltpu.SemaphoreType.DMA((32,)),
        ],
        limit=PACK,
    )(
        elevation,
        velocity_pot,
        panel_slot,
        far_rows.reshape(1, PAIRS),
        far_cols.reshape(1, PAIRS),
        coef,
    )


def order_kernel(plan_ref, hot_ref, place_ref, table_ref):
    up = iota((128, 128), 0) < iota((128, 128), 1)
    weights = jnp.concatenate([up.astype(F32), jnp.ones((128, 128), F32)], axis=1).astype(BF16)
    seen = jnp.zeros((128, 128), F32)
    for x in range(16):
        slot = plan_ref[x : x + 1, :].astype(jnp.int32)
        dest, local = slot >> 11, slot & (PANELS - 1)
        hits = iota((128, 128), 0) == dest
        sums = dot(hits.astype(F32).astype(BF16), weights)
        rank = jnp.sum(jnp.where(hits, sums[:, :128] + seen, 0.0), axis=0, keepdims=True)
        seen = seen + sums[:, 128:]
        rank = rank.astype(jnp.int32)
        row = dest * 8 + (rank & 7)
        lanes = pl.ds(x * 128, 128)
        hot_ref[:, lanes] = hot_block(ROWS, row)
        place_ref[0:1, lanes] = rank >> 3
        place_ref[1:2, lanes] = local >> 7
        place_ref[2:3, lanes] = local & 127
        place_ref[3:4, lanes] = row
        place_ref[4:8, lanes] = jnp.zeros((4, 128), jnp.int32)

    turned = [
        jnp.broadcast_to(plan_ref[k : k + 1, :], (128, 128)).T.astype(jnp.int32)
        for k in range(16, 18)
    ]
    hits = (turned[0] >> 3) == iota((128, 128), 1)
    down = (iota((128, 128), 0) > iota((128, 128), 1)).astype(F32).astype(BF16)
    rank = dot(down, hits.astype(F32).astype(BF16))
    values = (iota((128, 128), 0) - PAIRS, (turned[0] & 7) - 8, turned[1] & 7)
    for k, (value, base) in enumerate(zip(values, (PAIRS, 8, 0))):
        for s in range(2):
            chosen = hits & (rank == float(s))
            found = jnp.sum(jnp.where(chosen, value.astype(F32), 0.0), axis=0, keepdims=True)
            table_ref[2 * k + s : 2 * k + s + 1, :] = found.astype(jnp.int32) + base
    table_ref[6:8, :] = jnp.zeros((2, 128), jnp.int32)


def sender_order(plan):
    return call(
        order_kernel,
        (
            jax.ShapeDtypeStruct((ROWS, PANELS), BF16),
            jax.ShapeDtypeStruct((8, PANELS), jnp.int32),
            jax.ShapeDtypeStruct((8, 128), jnp.int32),
        ),
        [VMEM],
        (VMEM,) * 3,
        limit=8,
    )(plan)


def surface_kernel(
    plan_ref,
    fields,
    along_a,
    along_b,
    across_a,
    across_b,
    hot_ref,
    place_ref,
    table_ref,
    eta_hbm,
    out_hbm,
    eta_tracks,
    stack,
    out,
    eta_sems,
    out_sems,
):
    row, col = lax.axis_index("along"), lax.axis_index("across")
    first_row, last_row = row == 0, row == lax.axis_size("along") - 1
    first_col, last_col = col == 0, col == lax.axis_size("across") - 1
    lane = iota((WAVES, 128), 1)
    even_row, even_col = lax.rem(row, 2) == 0, lax.rem(col, 2) == 0
    west = jnp.where(even_col, across_b[...], across_a[...])
    east = jnp.where(even_col, across_a[...], across_b[...])
    west, east = jnp.where(first_col, 0.0, west), jnp.where(last_col, 0.0, east)
    above = [jnp.where(even_row, along_b[k], along_a[k]) for k in range(4)]
    above = [jnp.where(first_row, 0.0, values) for values in above]
    below = jnp.where(last_row, 0.0, jnp.where(even_row, along_a[0], along_b[0]))

    def views(f, x, k):
        x1 = fields[16 * k + x - 1] if x >= 1 else above[2 * k + 1]
        x2 = fields[16 * k + x - 2] if x >= 2 else above[2 * k + x]
        at = 64 * k + 2 * x
        left = pltpu.roll(west, 128 - at, 1) if at else west
        right = pltpu.roll(east, 126 - at, 1)
        w2 = jnp.where(lane < 2, left, pltpu.roll(f, 2, 1))
        w1 = jnp.where(lane < 1, pltpu.roll(left, 127, 1), pltpu.roll(f, 1, 1))
        e2 = jnp.where(lane >= 126, right, pltpu.roll(f, 126, 1))
        e1 = jnp.where(lane >= 127, pltpu.roll(right, 1, 1), pltpu.roll(f, 127, 1))
        up = 0.5 * (3.0 * f - 4.0 * x1 + x2)
        across = (w2 - 8.0 * w1 + 8.0 * e1 - e2) * (1.0 / 12.0)
        return x1, w1, e1, up, across

    stack[128:256, :] = jnp.zeros((128, PANELS + 128), BF16)
    stack[0:128, pl.ds(PANELS, 128)] = jnp.zeros((128, 128), BF16)
    stores = []
    for x in range(16):
        e, p = fields[x], fields[16 + x]
        _, _, _, up, across = views(e, x, 0)
        p1, pw, pe, phi_up, phi_across = views(p, x, 1)
        next_row = fields[17 + x] if x < 15 else below
        curvature = next_row + p1 + pe + pw - 4.0 * p
        eta = e - 0.4 * up + 0.3 * across + plan_ref[24 + x : 25 + x, :] * curvature
        eta_tracks[x] = eta
        stores.append(pltpu.make_async_copy(eta_tracks.at[x], eta_hbm.at[:, x, :], eta_sems.at[x]))
        stores[x].start()
        values = p - 0.4 * phi_up + 0.3 * phi_across - 0.5 * eta
        lanes = pl.ds(x * 128, 128)
        place = place_ref[:, lanes]
        second = place[0:1] == 1
        stack[0:64, lanes] = jnp.where(second, 0.0, values).astype(BF16)
        stack[64:128, lanes] = jnp.where(second, values, 0.0).astype(BF16)
        high, low = place[1:2].astype(F32), place[2:3].astype(F32)
        notes = [
            jnp.where(second, 0.0, high),
            jnp.where(second, 0.0, low),
            jnp.where(second, high, 0.0),
            jnp.where(second, low, 0.0),
            jnp.zeros((12, 128), F32),
        ]
        stack[128:144, lanes] = jnp.concatenate(notes, axis=0).astype(BF16)
    rows = table_ref[2:4, :].astype(F32)
    own = jnp.concatenate([jnp.zeros((4, 128), F32), rows, jnp.zeros((10, 128), F32)], axis=0)
    stack[128:144, pl.ds(PANELS, 128)] = own.astype(BF16)
    for m in range(0, ROWS, 256):
        at = pl.ds(m, 256)
        owner = ((iota((256, 128), 0) + m) >> 3) == iota((256, 128), 1)
        values = dot_nt(hot_ref[at, :], stack[:, pl.ds(0, PANELS)])
        values += dot_nt(owner.astype(F32).astype(BF16), stack[:, pl.ds(PANELS, 128)])
        out[at, :] = values.astype(BF16)
        stores.append(pltpu.make_async_copy(out.at[at], out_hbm.at[at], out_sems.at[m // 256]))
        stores[-1].start()
    for copy in stores:
        copy.wait()


def surface_payload(plan, fields, halo, hot, place, table):
    return call(
        surface_kernel,
        (
            jax.ShapeDtypeStruct((WAVES, 16, 128), F32),
            jax.ShapeDtypeStruct((ROWS, 256), BF16),
        ),
        [VMEM] * 9,
        (HBM, HBM),
        [
            pltpu.VMEM((16, WAVES, 128), F32),
            pltpu.VMEM((256, PANELS + 128), BF16),
            pltpu.VMEM((ROWS, 256), BF16),
            pltpu.SemaphoreType.DMA((16,)),
            pltpu.SemaphoreType.DMA((4,)),
        ],
        limit=12,
    )(plan, fields, *halo, hot, place, table)


def cluster_kernel(arrived_ref, clustered_ref, info_ref, hot, right):
    lane = iota((128, 128), 1)
    for m in range(0, ROWS, 128):
        lanes = pl.ds(m, 128)
        values = arrived_ref[lanes, 0:128].astype(F32)
        tail = arrived_ref[lanes, 128:256].astype(F32)
        notes = tail.T
        swapped = pltpu.roll(values, 64, 1)
        for half in range(2):
            slot = notes[2 * half : 2 * half + 1] * 128.0 + notes[2 * half + 1 : 2 * half + 2]
            info_ref[half : half + 1, lanes] = slot
            at = half * ROWS + m
            place = slot.astype(jnp.int32) & 1023
            hot[:, pl.ds(at, 128)] = hot_block(1024, place)
            both = jnp.where((lane < 64) == (half == 0), values, swapped)
            upper = tail[:, 2 * half : 2 * half + 1] >= 8.0
            right[pl.ds(at, 128), :] = jnp.where(upper == (lane >= 64), both, 0.0).astype(BF16)
        info_ref[2:4, lanes] = notes[4:6]
        info_ref[4:8, lanes] = jnp.zeros((4, 128), F32)
    for m in range(0, 1024, 256):
        clustered_ref[pl.ds(m, 256), :] = dot(hot[pl.ds(m, 256), :], right[...]).astype(BF16)


def to_clusters(arrived):
    return call(
        cluster_kernel,
        (
            jax.ShapeDtypeStruct((1024, 128), BF16),
            jax.ShapeDtypeStruct((8, ROWS), F32),
        ),
        [VMEM],
        (VMEM,) * 2,
        [pltpu.VMEM((1024, PANELS), BF16), pltpu.VMEM((PANELS, 128), BF16)],
        limit=8,
    )(arrived)


def coeff_kernel(table_ref, clustered_ref, v_hbm, big_hbm, out_hbm, basis, coeff, packed, sems):
    del big_hbm
    parts = [
        pltpu.make_async_copy(v_hbm.at[pl.ds(m, 32)], basis.at[pl.ds(m, 32)], sems.at[m // 32])
        for m in range(0, PAIRS, 32)
    ]
    for copy in parts:
        copy.start()
    weights = [clustered_ref[pl.ds(q * 256, 256), :] for q in range(4)]
    weights = [jnp.concatenate(weights[q : q + 2], axis=1) for q in (0, 2)]
    for q in range(4):
        coeff[q, pl.ds(PAIRS * RANK, RANK), :] = jnp.zeros((RANK, 128), F32)
    for m in range(0, PAIRS, 16):
        if m % 32 == 0:
            parts[m // 32].wait()
        rows = basis[pl.ds(m, 16)].reshape(16 * RANK, CL)
        at = pl.ds(m * RANK, 16 * RANK)
        for q in range(2):
            got = dot(rows, weights[q])
            coeff[2 * q, at, :] = got[:, :128]
            coeff[2 * q + 1, at, :] = got[:, 128:]
    lane = iota((RANK, 128), 1)

    def put(t, c):
        both = []
        for s in range(2):
            p = table_ref[s * OWNERS + t]
            col = table_ref[(4 + s) * OWNERS + t]
            tile = coeff[col & 3, pl.ds(pl.multiple_of(p * RANK, RANK), RANK), :]
            both.append(pltpu.roll(tile, ((col >> 2) ^ s) * 64, 1))
        both = jnp.where(lane < 64, both[0], both[1])
        packed[t, :, 0:128] = both[0:16].astype(BF16)
        packed[t, :, 128:256] = both[16:32].astype(BF16)
        return c

    lax.fori_loop(0, OWNERS, put, 0, unroll=8)
    load([(packed, out_hbm.at[:, 64:80, :])], sems)


def add_coeff(table, clustered, far_v, big):
    return pl.pallas_call(
        coeff_kernel,
        out_shape=jax.ShapeDtypeStruct((OWNERS, 80, CL), BF16),
        in_specs=[SMEM, VMEM, HBM, HBM],
        out_specs=HBM,
        scratch_shapes=[
            pltpu.VMEM((PAIRS, RANK, CL), BF16),
            pltpu.VMEM((4, PAIRS * RANK + RANK, 128), F32),
            pltpu.VMEM((OWNERS, 16, CL), BF16),
            pltpu.SemaphoreType.DMA((4,)),
        ],
        input_output_aliases={3: 0},
        compiler_params=pltpu.CompilerParams(vmem_limit_bytes=TIGHT * 2**20),
        cost_estimate=pl.CostEstimate(flops=0, bytes_accessed=32 * 2**20, transcendentals=0),
    )(table, clustered, far_v, big)


def near_kernel(
    rel_ref,
    before_ref,
    own_ref,
    after_ref,
    place_ref,
    blocks_ref,
    out_ref,
    hot_hbm,
    wide,
    hot,
    sems,
):
    c = pl.program_id(0)

    @pl.when(c == 0)
    def _():
        for k, ref in enumerate((before_ref, own_ref, after_ref)):
            for q in range(4):
                turned = ref[pl.ds(q * 256, 256), :].astype(F32).T.astype(BF16)
                wide[8 * k + q] = turned[0:64]
                wide[8 * k + 4 + q] = turned[64:128]

    lanes = pl.ds(pl.multiple_of(c * 256, 256), 256)
    hot[:, lanes] = hot_block(ROWS, place_ref[3:4, lanes])
    total = jnp.zeros((WAVES, CL), F32)
    for k in range(9):
        total += dot_nt(wide[rel_ref[c * 9 + k]], blocks_ref[0, k])
    out_ref[0] = total

    @pl.when(c == 7)
    def _():
        load([(hot, hot_hbm)], sems)


def near_product(relative, before, own, after, place, near_blocks):
    matrix = jax.ShapeDtypeStruct((1024, PANELS), BF16)
    return pl.pallas_call(
        near_kernel,
        out_shape=(jax.ShapeDtypeStruct((8, WAVES, CL), F32), matrix),
        grid_spec=pltpu.PrefetchScalarGridSpec(
            num_scalar_prefetch=1,
            grid=(8,),
            in_specs=[VMEM] * 4 + [pl.BlockSpec((1, 9, CL, CL), lambda c, r: (c, 0, 0, 0))],
            out_specs=(pl.BlockSpec((1, WAVES, CL), lambda c, r: (c, 0, 0)), HBM),
            scratch_shapes=[
                pltpu.VMEM((24, WAVES, CL), BF16),
                pltpu.VMEM((1024, PANELS), BF16),
                pltpu.SemaphoreType.DMA((1,)),
            ],
        ),
        compiler_params=pltpu.CompilerParams(vmem_limit_bytes=TIGHT * 2**20),
        cost_estimate=pl.CostEstimate(flops=0, bytes_accessed=512 * 2**20, transcendentals=0),
    )(relative, before, own, after, place, near_blocks)


def total_kernel(big_ref, near_ref, info_ref, out_hbm, hot, acc, masked, grid, out, out_sems):
    spread = ((iota((128, 256), 0) >> 3) == (iota((128, 256), 1) >> 4)) & (
        (iota((128, 256), 0) & 7) == 0
    )
    spread = spread.astype(F32).astype(BF16)
    for m in range(8):
        src = pl.ds(m * 16, 16)
        at = pl.ds(m * 256, 256)
        rows = dot(info_ref[:, pl.ds(m * 128, 128)].astype(BF16), spread)
        for part in range(2):
            mine = big_ref[src, 64:80, pl.ds(part * 128, 128)].reshape(256, 128)
            turned = mine.astype(F32).T.astype(BF16)
            for s in range(2):
                for cluster in range(8):
                    hit = (rows[2 + s : 3 + s] == float(cluster)).astype(F32).astype(BF16)
                    values = turned[s * 64 : s * 64 + 64] * hit
                    masked[2 * s + part, pl.ds(cluster * 64, 64), at] = values
    basis = [big_ref[:, pl.ds(16 * n, 16), :].reshape(2048, CL) for n in range(4)]
    for r in range(0, 512, 128):
        at = pl.ds(r, 128)
        product = dot(masked[0, at, :], basis[0])
        for n in range(1, 4):
            product += dot(masked[n, at, :], basis[n])
        acc[at, :] = product
    for half in range(2):
        for m in range(0, ROWS, 128):
            slot = info_ref[half : half + 1, pl.ds(m, 128)].astype(jnp.int32)
            hot[:, pl.ds(half * ROWS + m, 128)] = hot_block(1024, slot & 1023)
    for cluster in range(8):
        total = near_ref[cluster] + acc[pl.ds(cluster * 64, 64), :]
        grid[pl.ds((cluster >> 2) * 64, 64), pl.ds((cluster & 3) * 256, 256)] = total.astype(BF16)
    stores = []
    for m in range(0, ROWS, 256):
        at = pl.ds(m, 256)
        halves = []
        for half in range(2):
            got = dot(grid[...], hot[:, pl.ds(half * ROWS + m, 256)])
            upper = info_ref[half : half + 1, at] >= 1024.0
            halves.append(jnp.where(upper, got[64:128], got[0:64]))
        out[at, :] = jnp.concatenate(halves, axis=0).T.astype(BF16)
        stores.append(pltpu.make_async_copy(out.at[at], out_hbm.at[at], out_sems.at[m // 256]))
        stores[-1].start()
    for copy in stores:
        copy.wait()


def total_home(big, near, info):
    return call(
        total_kernel,
        jax.ShapeDtypeStruct((ROWS, 128), BF16),
        [VMEM, VMEM, VMEM],
        HBM,
        [
            pltpu.VMEM((1024, PANELS), BF16),
            pltpu.VMEM((512, CL), F32),
            pltpu.VMEM((4, 512, 2048), BF16),
            pltpu.VMEM((128, 1024), BF16),
            pltpu.VMEM((ROWS, 128), BF16),
            pltpu.SemaphoreType.DMA((4,)),
        ],
        limit=24,
    )(big, near, info)


def potential_kernel(returned_ref, hot_ref, place_ref, out_ref, turned, wide):
    for m in range(0, ROWS, 128):
        turned[:, pl.ds(m, 128)] = returned_ref[pl.ds(m, 128), :].astype(F32).T.astype(BF16)
    for x in range(0, 16, 2):
        lanes = pl.ds(x * 128, 256)
        got = dot(turned[...], hot_ref[:, lanes])
        got = jnp.where(place_ref[0:1, lanes] == 1, got[64:128], got[0:64])
        wide[:, x, :] = got[:, :128]
        wide[:, x + 1, :] = got[:, 128:]
    out_ref[...] = wide[...].astype(BF16)


def panel_potential(returned, hot, place):
    return call(
        potential_kernel,
        jax.ShapeDtypeStruct((WAVES, 16, 128), BF16),
        [VMEM] * 3,
        VMEM,
        [pltpu.VMEM((128, ROWS), BF16), pltpu.VMEM((WAVES, 16, 128), F32)],
    )(returned, hot, place)


def exchange(x):
    return lax.all_to_all(x, BOTH, split_axis=0, concat_axis=0, tiled=True)


def ring(axis, step):
    size = lax.axis_size(axis)
    return [(i, (i + step) % size) for i in range(size)]


def swap(axis, first):
    size = lax.axis_size(axis)
    pairs = [(i, (i + 1) % size) for i in range(first, size, 2)]
    return pairs + [(j, i) for i, j in pairs]


def body(
    elevation,
    velocity_pot,
    surface_coef,
    panel_slot,
    near_blocks,
    near_cols,
    far_v,
    far_u,
    far_rows,
    far_cols,
):
    per_owner, clusters = 8, 1024
    me = lax.axis_index(BOTH)
    fields, plan, along_a, along_b, across_a, across_b = pack_edges(
        elevation, velocity_pot, panel_slot, far_rows, far_cols, surface_coef
    )
    along_a = lax.ppermute(along_a, "along", swap("along", 0))
    along_b = lax.ppermute(along_b, "along", swap("along", 1))
    across_a = lax.ppermute(across_a, "across", swap("across", 0))
    across_b = lax.ppermute(across_b, "across", swap("across", 1))
    hot, place, table = sender_order(plan)
    halo = (along_a, along_b, across_a, across_b)
    eta, payload = surface_payload(plan, fields, halo, hot, place, table)
    table = table.reshape(8 * 128)
    arrived = exchange(payload.reshape(OWNERS, 8, 256)).reshape(ROWS, 256)
    big = far_bucket(table, far_u)
    arrived, big = lax.optimization_barrier((arrived, big))

    clustered, info = to_clusters(arrived)
    before = lax.ppermute(clustered, BOTH, ring(BOTH, 1))
    after = lax.ppermute(clustered, BOTH, ring(BOTH, -1))
    big = add_coeff(table, clustered, far_v, big)
    after, before, big = lax.optimization_barrier((after, before, big))
    big = exchange(big)

    relative = (near_cols - (me * per_owner - per_owner)) % clusters
    near, hot = near_product(
        relative.reshape(72), before, clustered, after, place, near_blocks
    )

    home = total_home(big, near, info).reshape(OWNERS, 8, 128)
    returned = exchange(home).reshape(ROWS, 128)
    potential = panel_potential(returned, hot, place)
    return (eta, potential)


def solution(mesh):
    in_specs = (
        P(None, "along", "across"),
        P(None, "along", "across"),
        P("along", "across"),
        P("along", "across"),
        P(BOTH, None, None, None),
        P(BOTH, None),
        P(BOTH, None, None),
        P(BOTH, None, None),
        P(BOTH),
        P(BOTH),
    )
    out_specs = (P(None, "along", "across"), P(None, "along", "across"))
    return jax.shard_map(body, mesh=mesh, in_specs=in_specs, out_specs=out_specs, check_vma=False)
```

```python
import jax
import jax.numpy as jnp
from jax import lax
from jax.experimental import pallas as pl
from jax.experimental.pallas import tpu as pltpu
from jax.sharding import PartitionSpec as P

CL = 256
BOTH = ("along", "across")
OWNERS = 128
PAIRS = 128
RANK = 32
WAVES = 64
ROWS = 1024
PANELS = 2048
BF16 = jnp.bfloat16
F32 = jnp.float32
WIDE = 56
PACK = 56
TIGHT = 52
VMEM = pl.BlockSpec(memory_space=pltpu.VMEM)
SMEM = pl.BlockSpec(memory_space=pltpu.SMEM)
HBM = pl.BlockSpec(memory_space=pltpu.HBM)


def call(kernel, out_shape, in_specs, out_specs, scratch=(), limit=4, cost=0):
    return pl.pallas_call(
        kernel,
        out_shape=out_shape,
        in_specs=in_specs,
        out_specs=out_specs,
        scratch_shapes=list(scratch),
        compiler_params=pltpu.CompilerParams(vmem_limit_bytes=limit * 2**20),
        cost_estimate=pl.CostEstimate(flops=0, bytes_accessed=cost, transcendentals=0),
    )


def hot_block(count, row):
    index = iota((count, row.shape[1]), 0).astype(jnp.int16)
    hit = index == row.astype(jnp.int16)
    return jnp.where(hit, jnp.ones((), BF16), jnp.zeros((), BF16))


def iota(shape, dim):
    return lax.broadcasted_iota(jnp.int32, shape, dim)


def dot(a, b):
    return jnp.dot(a, b, preferred_element_type=F32)


def dot_nt(a, b):
    return lax.dot_general(a, b, (((1,), (1,)), ((), ())), preferred_element_type=F32)


def bucket_kernel(table_ref, u_hbm, out_hbm, values, packed, sems):
    load([(u_hbm, values)], sems)

    def put(t, c):
        for s in range(2):
            p = table_ref[s * OWNERS + t]
            mine = values[jnp.minimum(p, PAIRS - 1)]
            packed[t, pl.ds(s * RANK, RANK), :] = jnp.where(p < PAIRS, mine, jnp.zeros_like(mine))
        return c

    lax.fori_loop(0, OWNERS, put, 0, unroll=4)
    load([(packed, out_hbm.at[:, 0:64, :])], sems)


def far_bucket(table, far_u):
    return call(
        bucket_kernel,
        jax.ShapeDtypeStruct((OWNERS, 80, CL), BF16),
        [SMEM, HBM],
        HBM,
        [
            pltpu.VMEM((PAIRS, RANK, CL), BF16),
            pltpu.VMEM((OWNERS, 2 * RANK, CL), BF16),
            pltpu.SemaphoreType.DMA((1,)),
        ],
        limit=TIGHT,
        cost=9 * 2**20,
    )(table, far_u)


def load(pairs, sems):
    copies = [pltpu.make_async_copy(a, b, sems.at[i]) for i, (a, b) in enumerate(pairs)]
    for copy in copies:
        copy.start()
    for copy in copies:
        copy.wait()


def pack_kernel(
    elevation_hbm,
    phi_hbm,
    slot_hbm,
    rows_hbm,
    cols_hbm,
    coef_hbm,
    fields_ref,
    plan_ref,
    along_a,
    along_b,
    across_a,
    across_b,
    ints,
    sems,
    field_sems,
):
    small = [
        (slot_hbm, ints.at[0:16]),
        (rows_hbm, ints.at[16:17]),
        (cols_hbm, ints.at[17:18]),
        (coef_hbm, plan_ref.at[24:40]),
    ]
    small = [pltpu.make_async_copy(a, b, sems.at[i]) for i, (a, b) in enumerate(small)]
    fields = []
    for x in range(16):
        fields.append((elevation_hbm.at[:, x, :], fields_ref.at[x]))
        fields.append((phi_hbm.at[:, x, :], fields_ref.at[16 + x]))
    fields = [pltpu.make_async_copy(a, b, field_sems.at[i]) for i, (a, b) in enumerate(fields)]
    for copy in fields + small:
        copy.start()
    for copy in small:
        copy.wait()
    plan_ref[0:24, :] = ints[...].astype(F32)
    even_row = lax.rem(lax.axis_index("along"), 2) == 0
    even_col = lax.rem(lax.axis_index("across"), 2) == 0
    for copy in fields:
        copy.wait()
    lane = iota((WAVES, 128), 1)
    right = jnp.zeros((WAVES, 128), F32)
    left = jnp.zeros((WAVES, 128), F32)
    for k in range(2):
        for x in range(16):
            values = fields_ref[16 * k + x]
            at = 64 * k + 2 * x
            here = (lane >> 1) == at // 2
            right = jnp.where(here, pltpu.roll(values, (at + 2) % 128, 1), right)
            left = jnp.where(here, pltpu.roll(values, at, 1) if at else values, left)
    across_a[...] = jnp.where(even_col, right, left)
    across_b[...] = jnp.where(even_col, left, right)
    upward = fields_ref[16]
    for k, downward in enumerate([fields_ref[n] for n in (14, 15, 30, 31)]):
        along_a[k] = jnp.where(even_row, downward, upward)
        along_b[k] = jnp.where(even_row, upward, downward)


def pack_edges(elevation, velocity_pot, panel_slot, far_rows, far_cols, coef):
    side = jax.ShapeDtypeStruct((WAVES, 128), F32)
    rows = jax.ShapeDtypeStruct((4, WAVES, 128), F32)
    tracks = jax.ShapeDtypeStruct((32, WAVES, 128), F32)
    return call(
        pack_kernel,
        (tracks, jax.ShapeDtypeStruct((40, 128), F32), rows, rows, side, side),
        [HBM] * 6,
        (VMEM,) * 6,
        [
            pltpu.VMEM((24, 128), jnp.int32),
            pltpu.SemaphoreType.DMA((4,)),
            pltpu.SemaphoreType.DMA((32,)),
        ],
        limit=PACK,
    )(
        elevation,
        velocity_pot,
        panel_slot,
        far_rows.reshape(1, PAIRS),
        far_cols.reshape(1, PAIRS),
        coef,
    )


def order_kernel(plan_ref, hot_ref, place_ref, table_ref):
    up = iota((128, 128), 0) < iota((128, 128), 1)
    weights = jnp.concatenate([up.astype(F32), jnp.ones((128, 128), F32)], axis=1).astype(BF16)
    seen = jnp.zeros((128, 128), F32)
    for x in range(16):
        slot = plan_ref[x : x + 1, :].astype(jnp.int32)
        dest, local = slot >> 11, slot & (PANELS - 1)
        hits = iota((128, 128), 0) == dest
        sums = dot(hits.astype(F32).astype(BF16), weights)
        rank = jnp.sum(jnp.where(hits, sums[:, :128] + seen, 0.0), axis=0, keepdims=True)
        seen = seen + sums[:, 128:]
        rank = rank.astype(jnp.int32)
        row = dest * 8 + (rank & 7)
        lanes = pl.ds(x * 128, 128)
        hot_ref[:, lanes] = hot_block(ROWS, row)
        place_ref[0:1, lanes] = rank >> 3
        place_ref[1:2, lanes] = local >> 7
        place_ref[2:3, lanes] = local & 127
        place_ref[3:4, lanes] = row
        place_ref[4:8, lanes] = jnp.zeros((4, 128), jnp.int32)

    turned = [
        jnp.broadcast_to(plan_ref[k : k + 1, :], (128, 128)).T.astype(jnp.int32)
        for k in range(16, 18)
    ]
    hits = (turned[0] >> 3) == iota((128, 128), 1)
    down = (iota((128, 128), 0) > iota((128, 128), 1)).astype(F32).astype(BF16)
    rank = dot(down, hits.astype(F32).astype(BF16))
    values = (iota((128, 128), 0) - PAIRS, (turned[0] & 7) - 8, turned[1] & 7)
    for k, (value, base) in enumerate(zip(values, (PAIRS, 8, 0))):
        for s in range(2):
            chosen = hits & (rank == float(s))
            found = jnp.sum(jnp.where(chosen, value.astype(F32), 0.0), axis=0, keepdims=True)
            table_ref[2 * k + s : 2 * k + s + 1, :] = found.astype(jnp.int32) + base
    table_ref[6:8, :] = jnp.zeros((2, 128), jnp.int32)


def sender_order(plan):
    return call(
        order_kernel,
        (
            jax.ShapeDtypeStruct((ROWS, PANELS), BF16),
            jax.ShapeDtypeStruct((8, PANELS), jnp.int32),
            jax.ShapeDtypeStruct((8, 128), jnp.int32),
        ),
        [VMEM],
        (VMEM,) * 3,
        limit=8,
    )(plan)


def surface_kernel(
    plan_ref,
    fields,
    along_a,
    along_b,
    across_a,
    across_b,
    hot_ref,
    place_ref,
    table_ref,
    eta_hbm,
    out_hbm,
    eta_tracks,
    stack,
    out,
    eta_sems,
    out_sems,
):
    row, col = lax.axis_index("along"), lax.axis_index("across")
    first_row, last_row = row == 0, row == lax.axis_size("along") - 1
    first_col, last_col = col == 0, col == lax.axis_size("across") - 1
    lane = iota((WAVES, 128), 1)
    even_row, even_col = lax.rem(row, 2) == 0, lax.rem(col, 2) == 0
    west = jnp.where(even_col, across_b[...], across_a[...])
    east = jnp.where(even_col, across_a[...], across_b[...])
    west, east = jnp.where(first_col, 0.0, west), jnp.where(last_col, 0.0, east)
    above = [jnp.where(even_row, along_b[k], along_a[k]) for k in range(4)]
    above = [jnp.where(first_row, 0.0, values) for values in above]
    below = jnp.where(last_row, 0.0, jnp.where(even_row, along_a[0], along_b[0]))

    def views(f, x, k):
        x1 = fields[16 * k + x - 1] if x >= 1 else above[2 * k + 1]
        x2 = fields[16 * k + x - 2] if x >= 2 else above[2 * k + x]
        at = 64 * k + 2 * x
        left = pltpu.roll(west, 128 - at, 1) if at else west
        right = pltpu.roll(east, 126 - at, 1)
        w2 = jnp.where(lane < 2, left, pltpu.roll(f, 2, 1))
        w1 = jnp.where(lane < 1, pltpu.roll(left, 127, 1), pltpu.roll(f, 1, 1))
        e2 = jnp.where(lane >= 126, right, pltpu.roll(f, 126, 1))
        e1 = jnp.where(lane >= 127, pltpu.roll(right, 1, 1), pltpu.roll(f, 127, 1))
        up = 0.5 * (3.0 * f - 4.0 * x1 + x2)
        across = (w2 - 8.0 * w1 + 8.0 * e1 - e2) * (1.0 / 12.0)
        return x1, w1, e1, up, across

    stack[128:256, :] = jnp.zeros((128, PANELS + 128), BF16)
    stack[0:128, pl.ds(PANELS, 128)] = jnp.zeros((128, 128), BF16)
    stores = []
    for x in range(16):
        e, p = fields[x], fields[16 + x]
        _, _, _, up, across = views(e, x, 0)
        p1, pw, pe, phi_up, phi_across = views(p, x, 1)
        next_row = fields[17 + x] if x < 15 else below
        curvature = next_row + p1 + pe + pw - 4.0 * p
        eta = e - 0.4 * up + 0.3 * across + plan_ref[24 + x : 25 + x, :] * curvature
        eta_tracks[x] = eta
        stores.append(pltpu.make_async_copy(eta_tracks.at[x], eta_hbm.at[x], eta_sems.at[x]))
        stores[x].start()
        values = p - 0.4 * phi_up + 0.3 * phi_across - 0.5 * eta
        lanes = pl.ds(x * 128, 128)
        place = place_ref[:, lanes]
        second = place[0:1] == 1
        stack[0:64, lanes] = jnp.where(second, 0.0, values).astype(BF16)
        stack[64:128, lanes] = jnp.where(second, values, 0.0).astype(BF16)
        high, low = place[1:2].astype(F32), place[2:3].astype(F32)
        notes = [
            jnp.where(second, 0.0, high),
            jnp.where(second, 0.0, low),
            jnp.where(second, high, 0.0),
            jnp.where(second, low, 0.0),
            jnp.zeros((12, 128), F32),
        ]
        stack[128:144, lanes] = jnp.concatenate(notes, axis=0).astype(BF16)
    rows = table_ref[2:4, :].astype(F32)
    own = jnp.concatenate([jnp.zeros((4, 128), F32), rows, jnp.zeros((10, 128), F32)], axis=0)
    stack[128:144, pl.ds(PANELS, 128)] = own.astype(BF16)
    for m in range(0, ROWS, 256):
        at = pl.ds(m, 256)
        owner = ((iota((256, 128), 0) + m) >> 3) == iota((256, 128), 1)
        values = dot_nt(hot_ref[at, :], stack[:, pl.ds(0, PANELS)])
        values += dot_nt(owner.astype(F32).astype(BF16), stack[:, pl.ds(PANELS, 128)])
        out[at, :] = values.astype(BF16)
        stores.append(pltpu.make_async_copy(out.at[at], out_hbm.at[at], out_sems.at[m // 256]))
        stores[-1].start()
    for copy in stores:
        copy.wait()


def surface_payload(plan, fields, halo, hot, place, table):
    return call(
        surface_kernel,
        (
            jax.ShapeDtypeStruct((16, WAVES, 128), F32),
            jax.ShapeDtypeStruct((ROWS, 256), BF16),
        ),
        [VMEM] * 9,
        (HBM, HBM),
        [
            pltpu.VMEM((16, WAVES, 128), F32),
            pltpu.VMEM((256, PANELS + 128), BF16),
            pltpu.VMEM((ROWS, 256), BF16),
            pltpu.SemaphoreType.DMA((16,)),
            pltpu.SemaphoreType.DMA((4,)),
        ],
        limit=12,
    )(plan, fields, *halo, hot, place, table)


def cluster_kernel(arrived_ref, clustered_ref, info_ref, hot, right):
    lane = iota((128, 128), 1)
    for m in range(0, ROWS, 128):
        lanes = pl.ds(m, 128)
        values = arrived_ref[lanes, 0:128].astype(F32)
        tail = arrived_ref[lanes, 128:256].astype(F32)
        notes = tail.T
        swapped = pltpu.roll(values, 64, 1)
        for half in range(2):
            slot = notes[2 * half : 2 * half + 1] * 128.0 + notes[2 * half + 1 : 2 * half + 2]
            info_ref[half : half + 1, lanes] = slot
            at = half * ROWS + m
            place = slot.astype(jnp.int32) & 1023
            hot[:, pl.ds(at, 128)] = hot_block(1024, place)
            both = jnp.where((lane < 64) == (half == 0), values, swapped)
            upper = tail[:, 2 * half : 2 * half + 1] >= 8.0
            right[pl.ds(at, 128), :] = jnp.where(upper == (lane >= 64), both, 0.0).astype(BF16)
        info_ref[2:4, lanes] = notes[4:6]
        info_ref[4:8, lanes] = jnp.zeros((4, 128), F32)
    for m in range(0, 1024, 256):
        clustered_ref[pl.ds(m, 256), :] = dot(hot[pl.ds(m, 256), :], right[...]).astype(BF16)


def to_clusters(arrived):
    return call(
        cluster_kernel,
        (
            jax.ShapeDtypeStruct((1024, 128), BF16),
            jax.ShapeDtypeStruct((8, ROWS), F32),
        ),
        [VMEM],
        (VMEM,) * 2,
        [pltpu.VMEM((1024, PANELS), BF16), pltpu.VMEM((PANELS, 128), BF16)],
        limit=8,
    )(arrived)


def coeff_kernel(table_ref, clustered_ref, v_hbm, big_hbm, out_hbm, basis, coeff, packed, sems):
    del big_hbm
    parts = [
        pltpu.make_async_copy(v_hbm.at[pl.ds(m, 32)], basis.at[pl.ds(m, 32)], sems.at[m // 32])
        for m in range(0, PAIRS, 32)
    ]
    for copy in parts:
        copy.start()
    weights = [clustered_ref[pl.ds(q * 256, 256), :] for q in range(4)]
    weights = [jnp.concatenate(weights[q : q + 2], axis=1) for q in (0, 2)]
    for q in range(4):
        coeff[q, pl.ds(PAIRS * RANK, RANK), :] = jnp.zeros((RANK, 128), F32)
    for m in range(0, PAIRS, 16):
        if m % 32 == 0:
            parts[m // 32].wait()
        rows = basis[pl.ds(m, 16)].reshape(16 * RANK, CL)
        at = pl.ds(m * RANK, 16 * RANK)
        for q in range(2):
            got = dot(rows, weights[q])
            coeff[2 * q, at, :] = got[:, :128]
            coeff[2 * q + 1, at, :] = got[:, 128:]
    lane = iota((RANK, 128), 1)

    def put(t, c):
        both = []
        for s in range(2):
            p = table_ref[s * OWNERS + t]
            col = table_ref[(4 + s) * OWNERS + t]
            tile = coeff[col & 3, pl.ds(pl.multiple_of(p * RANK, RANK), RANK), :]
            both.append(pltpu.roll(tile, ((col >> 2) ^ s) * 64, 1))
        both = jnp.where(lane < 64, both[0], both[1])
        packed[t, :, 0:128] = both[0:16].astype(BF16)
        packed[t, :, 128:256] = both[16:32].astype(BF16)
        return c

    lax.fori_loop(0, OWNERS, put, 0, unroll=8)
    load([(packed, out_hbm.at[:, 64:80, :])], sems)


def add_coeff(table, clustered, far_v, big):
    return pl.pallas_call(
        coeff_kernel,
        out_shape=jax.ShapeDtypeStruct((OWNERS, 80, CL), BF16),
        in_specs=[SMEM, VMEM, HBM, HBM],
        out_specs=HBM,
        scratch_shapes=[
            pltpu.VMEM((PAIRS, RANK, CL), BF16),
            pltpu.VMEM((4, PAIRS * RANK + RANK, 128), F32),
            pltpu.VMEM((OWNERS, 16, CL), BF16),
            pltpu.SemaphoreType.DMA((4,)),
        ],
        input_output_aliases={3: 0},
        compiler_params=pltpu.CompilerParams(vmem_limit_bytes=TIGHT * 2**20),
        cost_estimate=pl.CostEstimate(flops=0, bytes_accessed=32 * 2**20, transcendentals=0),
    )(table, clustered, far_v, big)


def near_kernel(
    rel_ref,
    before_ref,
    own_ref,
    after_ref,
    place_ref,
    eta_tracks,
    blocks_ref,
    out_ref,
    hot_hbm,
    eta_hbm,
    wide,
    hot,
    sems,
):
    c = pl.program_id(0)

    @pl.when(c == 0)
    def _():
        for k, ref in enumerate((before_ref, own_ref, after_ref)):
            for q in range(4):
                turned = ref[pl.ds(q * 256, 256), :].astype(F32).T.astype(BF16)
                wide[8 * k + q] = turned[0:64]
                wide[8 * k + 4 + q] = turned[64:128]

    lanes = pl.ds(pl.multiple_of(c * 256, 256), 256)
    hot[:, lanes] = hot_block(ROWS, place_ref[3:4, lanes])
    total = jnp.zeros((WAVES, CL), F32)
    for k in range(9):
        total += dot_nt(wide[rel_ref[c * 9 + k]], blocks_ref[0, k])
    out_ref[0] = total

    @pl.when(c == 7)
    def _():
        tracks = [(eta_tracks.at[x], eta_hbm.at[:, x, :]) for x in range(16)]
        load([(hot, hot_hbm)] + tracks, sems)


def near_product(relative, before, own, after, place, eta, near_blocks):
    matrix = jax.ShapeDtypeStruct((1024, PANELS), BF16)
    return pl.pallas_call(
        near_kernel,
        out_shape=(
                jax.ShapeDtypeStruct((8, WAVES, CL), F32),
                matrix,
                jax.ShapeDtypeStruct((WAVES, 16, 128), F32),
        ),
        grid_spec=pltpu.PrefetchScalarGridSpec(
            num_scalar_prefetch=1,
            grid=(8,),
            in_specs=[VMEM] * 4 + [HBM, pl.BlockSpec((1, 9, CL, CL), lambda c, r: (c, 0, 0, 0))],
            out_specs=(pl.BlockSpec((1, WAVES, CL), lambda c, r: (c, 0, 0)), HBM, HBM),
            scratch_shapes=[
                pltpu.VMEM((24, WAVES, CL), BF16),
                pltpu.VMEM((1024, PANELS), BF16),
                pltpu.SemaphoreType.DMA((17,)),
            ],
        ),
        compiler_params=pltpu.CompilerParams(vmem_limit_bytes=TIGHT * 2**20),
        cost_estimate=pl.CostEstimate(flops=0, bytes_accessed=512 * 2**20, transcendentals=0),
    )(relative, before, own, after, place, eta, near_blocks)


def total_kernel(big_ref, near_ref, info_ref, out_hbm, hot, acc, masked, grid, out, out_sems):
    spread = ((iota((128, 256), 0) >> 3) == (iota((128, 256), 1) >> 4)) & (
        (iota((128, 256), 0) & 7) == 0
    )
    spread = spread.astype(F32).astype(BF16)
    for m in range(8):
        src = pl.ds(m * 16, 16)
        at = pl.ds(m * 256, 256)
        rows = dot(info_ref[:, pl.ds(m * 128, 128)].astype(BF16), spread)
        for part in range(2):
            mine = big_ref[src, 64:80, pl.ds(part * 128, 128)].reshape(256, 128)
            turned = mine.astype(F32).T.astype(BF16)
            for s in range(2):
                for cluster in range(8):
                    hit = (rows[2 + s : 3 + s] == float(cluster)).astype(F32).astype(BF16)
                    values = turned[s * 64 : s * 64 + 64] * hit
                    masked[2 * s + part, pl.ds(cluster * 64, 64), at] = values
    basis = [big_ref[:, pl.ds(16 * n, 16), :].reshape(2048, CL) for n in range(4)]
    for r in range(0, 512, 128):
        at = pl.ds(r, 128)
        product = dot(masked[0, at, :], basis[0])
        for n in range(1, 4):
            product += dot(masked[n, at, :], basis[n])
        acc[at, :] = product
    for half in range(2):
        for m in range(0, ROWS, 128):
            slot = info_ref[half : half + 1, pl.ds(m, 128)].astype(jnp.int32)
            hot[:, pl.ds(half * ROWS + m, 128)] = hot_block(1024, slot & 1023)
    for cluster in range(8):
        total = near_ref[cluster] + acc[pl.ds(cluster * 64, 64), :]
        grid[pl.ds((cluster >> 2) * 64, 64), pl.ds((cluster & 3) * 256, 256)] = total.astype(BF16)
    stores = []
    for m in range(0, ROWS, 256):
        at = pl.ds(m, 256)
        halves = []
        for half in range(2):
            got = dot(grid[...], hot[:, pl.ds(half * ROWS + m, 256)])
            upper = info_ref[half : half + 1, at] >= 1024.0
            halves.append(jnp.where(upper, got[64:128], got[0:64]))
        out[at, :] = jnp.concatenate(halves, axis=0).T.astype(BF16)
        stores.append(pltpu.make_async_copy(out.at[at], out_hbm.at[at], out_sems.at[m // 256]))
        stores[-1].start()
    for copy in stores:
        copy.wait()


def total_home(big, near, info):
    return call(
        total_kernel,
        jax.ShapeDtypeStruct((ROWS, 128), BF16),
        [VMEM, VMEM, VMEM],
        HBM,
        [
            pltpu.VMEM((1024, PANELS), BF16),
            pltpu.VMEM((512, CL), F32),
            pltpu.VMEM((4, 512, 2048), BF16),
            pltpu.VMEM((128, 1024), BF16),
            pltpu.VMEM((ROWS, 128), BF16),
            pltpu.SemaphoreType.DMA((4,)),
        ],
        limit=24,
    )(big, near, info)


def potential_kernel(returned_ref, hot_ref, place_ref, out_ref, turned, wide):
    for m in range(0, ROWS, 128):
        turned[:, pl.ds(m, 128)] = returned_ref[pl.ds(m, 128), :].astype(F32).T.astype(BF16)
    for x in range(0, 16, 2):
        lanes = pl.ds(x * 128, 256)
        got = dot(turned[...], hot_ref[:, lanes])
        got = jnp.where(place_ref[0:1, lanes] == 1, got[64:128], got[0:64])
        wide[:, x, :] = got[:, :128]
        wide[:, x + 1, :] = got[:, 128:]
    out_ref[...] = wide[...].astype(BF16)


def panel_potential(returned, hot, place):
    return call(
        potential_kernel,
        jax.ShapeDtypeStruct((WAVES, 16, 128), BF16),
        [VMEM] * 3,
        VMEM,
        [pltpu.VMEM((128, ROWS), BF16), pltpu.VMEM((WAVES, 16, 128), F32)],
    )(returned, hot, place)


def exchange(x):
    return lax.all_to_all(x, BOTH, split_axis=0, concat_axis=0, tiled=True)


def ring(axis, step):
    size = lax.axis_size(axis)
    return [(i, (i + step) % size) for i in range(size)]


def swap(axis, first):
    size = lax.axis_size(axis)
    pairs = [(i, (i + 1) % size) for i in range(first, size, 2)]
    return pairs + [(j, i) for i, j in pairs]


def body(
    elevation,
    velocity_pot,
    surface_coef,
    panel_slot,
    near_blocks,
    near_cols,
    far_v,
    far_u,
    far_rows,
    far_cols,
):
    per_owner, clusters = 8, 1024
    me = lax.axis_index(BOTH)
    fields, plan, along_a, along_b, across_a, across_b = pack_edges(
        elevation, velocity_pot, panel_slot, far_rows, far_cols, surface_coef
    )
    along_a = lax.ppermute(along_a, "along", swap("along", 0))
    along_b = lax.ppermute(along_b, "along", swap("along", 1))
    across_a = lax.ppermute(across_a, "across", swap("across", 0))
    across_b = lax.ppermute(across_b, "across", swap("across", 1))
    hot, place, table = sender_order(plan)
    halo = (along_a, along_b, across_a, across_b)
    eta, payload = surface_payload(plan, fields, halo, hot, place, table)
    table = table.reshape(8 * 128)
    arrived = exchange(payload.reshape(OWNERS, 8, 256)).reshape(ROWS, 256)
    big = far_bucket(table, far_u)
    arrived, big = lax.optimization_barrier((arrived, big))

    clustered, info = to_clusters(arrived)
    before = lax.ppermute(clustered, BOTH, ring(BOTH, 1))
    after = lax.ppermute(clustered, BOTH, ring(BOTH, -1))
    big = add_coeff(table, clustered, far_v, big)
    after, before, big = lax.optimization_barrier((after, before, big))
    big = exchange(big)

    relative = (near_cols - (me * per_owner - per_owner)) % clusters
    near, hot, eta = near_product(
        relative.reshape(72), before, clustered, after, place, eta, near_blocks
    )

    home = total_home(big, near, info).reshape(OWNERS, 8, 128)
    returned = exchange(home).reshape(ROWS, 128)
    potential = panel_potential(returned, hot, place)
    return (eta, potential)


def solution(mesh):
    in_specs = (
        P(None, "along", "across"),
        P(None, "along", "across"),
        P("along", "across"),
        P("along", "across"),
        P(BOTH, None, None, None),
        P(BOTH, None),
        P(BOTH, None, None),
        P(BOTH, None, None),
        P(BOTH),
        P(BOTH),
    )
    out_specs = (P(None, "along", "across"), P(None, "along", "across"))
    return jax.shard_map(body, mesh=mesh, in_specs=in_specs, out_specs=out_specs, check_vma=False)
```

```python
import jax
import jax.numpy as jnp
from jax import lax
from jax.experimental import pallas as pl
from jax.experimental.pallas import tpu as pltpu
from jax.sharding import PartitionSpec as P

CL = 256
BOTH = ("along", "across")
OWNERS = 128
PAIRS = 128
RANK = 32
WAVES = 64
ROWS = 1024
PANELS = 2048
BF16 = jnp.bfloat16
F32 = jnp.float32
WIDE = 56
PACK = 56
TIGHT = 52
VMEM = pl.BlockSpec(memory_space=pltpu.VMEM)
SMEM = pl.BlockSpec(memory_space=pltpu.SMEM)
HBM = pl.BlockSpec(memory_space=pltpu.HBM)


def call(kernel, out_shape, in_specs, out_specs, scratch=(), limit=4, cost=0):
    return pl.pallas_call(
        kernel,
        out_shape=out_shape,
        in_specs=in_specs,
        out_specs=out_specs,
        scratch_shapes=list(scratch),
        compiler_params=pltpu.CompilerParams(vmem_limit_bytes=limit * 2**20),
        cost_estimate=pl.CostEstimate(flops=0, bytes_accessed=cost, transcendentals=0),
    )


def hot_block(count, row):
    index = iota((count, row.shape[1]), 0).astype(jnp.int16)
    hit = index == row.astype(jnp.int16)
    return jnp.where(hit, jnp.ones((), BF16), jnp.zeros((), BF16))


def iota(shape, dim):
    return lax.broadcasted_iota(jnp.int32, shape, dim)


def dot(a, b):
    return jnp.dot(a, b, preferred_element_type=F32)


def dot_nt(a, b):
    return lax.dot_general(a, b, (((1,), (1,)), ((), ())), preferred_element_type=F32)


def bucket_kernel(table_ref, u_hbm, out_hbm, values, packed, sems):
    load([(u_hbm, values)], sems)

    def put(t, c):
        for s in range(2):
            p = table_ref[s * OWNERS + t]
            mine = values[jnp.minimum(p, PAIRS - 1)]
            packed[t, pl.ds(s * RANK, RANK), :] = jnp.where(p < PAIRS, mine, jnp.zeros_like(mine))
        return c

    lax.fori_loop(0, OWNERS, put, 0, unroll=4)
    load([(packed, out_hbm.at[:, 0:64, :])], sems)


def far_bucket(table, far_u):
    return call(
        bucket_kernel,
        jax.ShapeDtypeStruct((OWNERS, 80, CL), BF16),
        [SMEM, HBM],
        HBM,
        [
            pltpu.VMEM((PAIRS, RANK, CL), BF16),
            pltpu.VMEM((OWNERS, 2 * RANK, CL), BF16),
            pltpu.SemaphoreType.DMA((1,)),
        ],
        limit=TIGHT,
        cost=9 * 2**20,
    )(table, far_u)


def load(pairs, sems):
    copies = [pltpu.make_async_copy(a, b, sems.at[i]) for i, (a, b) in enumerate(pairs)]
    for copy in copies:
        copy.start()
    for copy in copies:
        copy.wait()


def pack_kernel(
    elevation_hbm,
    phi_hbm,
    slot_hbm,
    rows_hbm,
    cols_hbm,
    coef_hbm,
    fields_ref,
    plan_ref,
    along_a,
    along_b,
    across_a,
    across_b,
    ints,
    sems,
    field_sems,
):
    small = [
        (slot_hbm, ints.at[0:16]),
        (rows_hbm, ints.at[16:17]),
        (cols_hbm, ints.at[17:18]),
        (coef_hbm, plan_ref.at[24:40]),
    ]
    small = [pltpu.make_async_copy(a, b, sems.at[i]) for i, (a, b) in enumerate(small)]
    fields = []
    for x in range(16):
        fields.append((elevation_hbm.at[:, x, :], fields_ref.at[x]))
        fields.append((phi_hbm.at[:, x, :], fields_ref.at[16 + x]))
    fields = [pltpu.make_async_copy(a, b, field_sems.at[i]) for i, (a, b) in enumerate(fields)]
    for copy in fields + small:
        copy.start()
    for copy in small:
        copy.wait()
    plan_ref[0:24, :] = ints[...].astype(F32)
    even_row = lax.rem(lax.axis_index("along"), 2) == 0
    even_col = lax.rem(lax.axis_index("across"), 2) == 0
    for copy in fields:
        copy.wait()
    lane = iota((WAVES, 128), 1)
    right = jnp.zeros((WAVES, 128), F32)
    left = jnp.zeros((WAVES, 128), F32)
    for k in range(2):
        for x in range(16):
            values = fields_ref[16 * k + x]
            at = 64 * k + 2 * x
            here = (lane >> 1) == at // 2
            right = jnp.where(here, pltpu.roll(values, (at + 2) % 128, 1), right)
            left = jnp.where(here, pltpu.roll(values, at, 1) if at else values, left)
    across_a[...] = jnp.where(even_col, right, left)
    across_b[...] = jnp.where(even_col, left, right)
    upward = fields_ref[16]
    for k, downward in enumerate([fields_ref[n] for n in (14, 15, 30, 31)]):
        along_a[k] = jnp.where(even_row, downward, upward)
        along_b[k] = jnp.where(even_row, upward, downward)


def pack_edges(elevation, velocity_pot, panel_slot, far_rows, far_cols, coef):
    side = jax.ShapeDtypeStruct((WAVES, 128), F32)
    rows = jax.ShapeDtypeStruct((4, WAVES, 128), F32)
    tracks = jax.ShapeDtypeStruct((32, WAVES, 128), F32)
    return call(
        pack_kernel,
        (tracks, jax.ShapeDtypeStruct((40, 128), F32), rows, rows, side, side),
        [HBM] * 6,
        (VMEM,) * 6,
        [
            pltpu.VMEM((24, 128), jnp.int32),
            pltpu.SemaphoreType.DMA((4,)),
            pltpu.SemaphoreType.DMA((32,)),
        ],
        limit=PACK,
    )(
        elevation,
        velocity_pot,
        panel_slot,
        far_rows.reshape(1, PAIRS),
        far_cols.reshape(1, PAIRS),
        coef,
    )


def order_kernel(plan_ref, hot_ref, place_ref, table_ref):
    up = iota((128, 128), 0) < iota((128, 128), 1)
    weights = jnp.concatenate([up.astype(F32), jnp.ones((128, 128), F32)], axis=1).astype(BF16)
    seen = jnp.zeros((128, 128), F32)
    for x in range(16):
        slot = plan_ref[x : x + 1, :].astype(jnp.int32)
        dest, local = slot >> 11, slot & (PANELS - 1)
        hits = iota((128, 128), 0) == dest
        sums = dot(hits.astype(F32).astype(BF16), weights)
        rank = jnp.sum(jnp.where(hits, sums[:, :128] + seen, 0.0), axis=0, keepdims=True)
        seen = seen + sums[:, 128:]
        rank = rank.astype(jnp.int32)
        row = dest * 8 + (rank & 7)
        lanes = pl.ds(x * 128, 128)
        hot_ref[:, lanes] = hot_block(ROWS, row)
        place_ref[0:1, lanes] = rank >> 3
        place_ref[1:2, lanes] = local >> 7
        place_ref[2:3, lanes] = local & 127
        place_ref[3:4, lanes] = row
        place_ref[4:8, lanes] = jnp.zeros((4, 128), jnp.int32)

    turned = [
        jnp.broadcast_to(plan_ref[k : k + 1, :], (128, 128)).T.astype(jnp.int32)
        for k in range(16, 18)
    ]
    hits = (turned[0] >> 3) == iota((128, 128), 1)
    down = (iota((128, 128), 0) > iota((128, 128), 1)).astype(F32).astype(BF16)
    rank = dot(down, hits.astype(F32).astype(BF16))
    values = (iota((128, 128), 0) - PAIRS, (turned[0] & 7) - 8, turned[1] & 7)
    for k, (value, base) in enumerate(zip(values, (PAIRS, 8, 0))):
        for s in range(2):
            chosen = hits & (rank == float(s))
            found = jnp.sum(jnp.where(chosen, value.astype(F32), 0.0), axis=0, keepdims=True)
            table_ref[2 * k + s : 2 * k + s + 1, :] = found.astype(jnp.int32) + base
    table_ref[6:8, :] = jnp.zeros((2, 128), jnp.int32)


def sender_order(plan):
    return call(
        order_kernel,
        (
            jax.ShapeDtypeStruct((ROWS, PANELS), BF16),
            jax.ShapeDtypeStruct((8, PANELS), jnp.int32),
            jax.ShapeDtypeStruct((8, 128), jnp.int32),
        ),
        [VMEM],
        (VMEM,) * 3,
        limit=8,
    )(plan)


def surface_kernel(
    plan_ref,
    fields,
    along_a,
    along_b,
    across_a,
    across_b,
    hot_ref,
    place_ref,
    table_ref,
    eta_hbm,
    out_hbm,
    eta_tracks,
    stack,
    out,
    eta_sems,
    out_sems,
):
    row, col = lax.axis_index("along"), lax.axis_index("across")
    first_row, last_row = row == 0, row == lax.axis_size("along") - 1
    first_col, last_col = col == 0, col == lax.axis_size("across") - 1
    lane = iota((WAVES, 128), 1)
    even_row, even_col = lax.rem(row, 2) == 0, lax.rem(col, 2) == 0
    west = jnp.where(even_col, across_b[...], across_a[...])
    east = jnp.where(even_col, across_a[...], across_b[...])
    west, east = jnp.where(first_col, 0.0, west), jnp.where(last_col, 0.0, east)
    above = [jnp.where(even_row, along_b[k], along_a[k]) for k in range(4)]
    above = [jnp.where(first_row, 0.0, values) for values in above]
    below = jnp.where(last_row, 0.0, jnp.where(even_row, along_a[0], along_b[0]))

    def views(f, x, k):
        x1 = fields[16 * k + x - 1] if x >= 1 else above[2 * k + 1]
        x2 = fields[16 * k + x - 2] if x >= 2 else above[2 * k + x]
        at = 64 * k + 2 * x
        left = pltpu.roll(west, 128 - at, 1) if at else west
        right = pltpu.roll(east, 126 - at, 1)
        w2 = jnp.where(lane < 2, left, pltpu.roll(f, 2, 1))
        w1 = jnp.where(lane < 1, pltpu.roll(left, 127, 1), pltpu.roll(f, 1, 1))
        e2 = jnp.where(lane >= 126, right, pltpu.roll(f, 126, 1))
        e1 = jnp.where(lane >= 127, pltpu.roll(right, 1, 1), pltpu.roll(f, 127, 1))
        up = 0.5 * (3.0 * f - 4.0 * x1 + x2)
        across = (w2 - 8.0 * w1 + 8.0 * e1 - e2) * (1.0 / 12.0)
        return x1, w1, e1, up, across

    stack[128:256, :] = jnp.zeros((128, PANELS + 128), BF16)
    stack[0:128, pl.ds(PANELS, 128)] = jnp.zeros((128, 128), BF16)
    stores = []
    for x in range(16):
        e, p = fields[x], fields[16 + x]
        _, _, _, up, across = views(e, x, 0)
        p1, pw, pe, phi_up, phi_across = views(p, x, 1)
        next_row = fields[17 + x] if x < 15 else below
        curvature = next_row + p1 + pe + pw - 4.0 * p
        eta = e - 0.4 * up + 0.3 * across + plan_ref[24 + x : 25 + x, :] * curvature
        eta_tracks[x] = eta
        stores.append(pltpu.make_async_copy(eta_tracks.at[x], eta_hbm.at[:, x, :], eta_sems.at[x]))
        stores[x].start()
        values = p - 0.4 * phi_up + 0.3 * phi_across - 0.5 * eta
        lanes = pl.ds(x * 128, 128)
        place = place_ref[:, lanes]
        second = place[0:1] == 1
        stack[0:64, lanes] = jnp.where(second, 0.0, values).astype(BF16)
        stack[64:128, lanes] = jnp.where(second, values, 0.0).astype(BF16)
        high, low = place[1:2].astype(F32), place[2:3].astype(F32)
        notes = [
            jnp.where(second, 0.0, high),
            jnp.where(second, 0.0, low),
            jnp.where(second, high, 0.0),
            jnp.where(second, low, 0.0),
            jnp.zeros((12, 128), F32),
        ]
        stack[128:144, lanes] = jnp.concatenate(notes, axis=0).astype(BF16)
    rows = table_ref[2:4, :].astype(F32)
    own = jnp.concatenate([jnp.zeros((4, 128), F32), rows, jnp.zeros((10, 128), F32)], axis=0)
    stack[128:144, pl.ds(PANELS, 128)] = own.astype(BF16)
    for m in range(0, ROWS, 256):
        at = pl.ds(m, 256)
        owner = ((iota((256, 128), 0) + m) >> 3) == iota((256, 128), 1)
        values = dot_nt(hot_ref[at, :], stack[:, pl.ds(0, PANELS)])
        values += dot_nt(owner.astype(F32).astype(BF16), stack[:, pl.ds(PANELS, 128)])
        out[at, :] = values.astype(BF16)
        stores.append(pltpu.make_async_copy(out.at[at], out_hbm.at[at], out_sems.at[m // 256]))
        stores[-1].start()
    for copy in stores:
        copy.wait()


def surface_payload(plan, fields, halo, hot, place, table):
    return call(
        surface_kernel,
        (
            jax.ShapeDtypeStruct((WAVES, 16, 128), F32),
            jax.ShapeDtypeStruct((ROWS, 256), BF16),
        ),
        [VMEM] * 9,
        (HBM, HBM),
        [
            pltpu.VMEM((16, WAVES, 128), F32),
            pltpu.VMEM((256, PANELS + 128), BF16),
            pltpu.VMEM((ROWS, 256), BF16),
            pltpu.SemaphoreType.DMA((16,)),
            pltpu.SemaphoreType.DMA((4,)),
        ],
        limit=12,
    )(plan, fields, *halo, hot, place, table)


def cluster_kernel(arrived_ref, clustered_ref, info_ref, hot, right):
    lane = iota((128, 128), 1)
    for m in range(0, ROWS, 128):
        lanes = pl.ds(m, 128)
        values = arrived_ref[lanes, 0:128].astype(F32)
        tail = arrived_ref[lanes, 128:256].astype(F32)
        notes = tail.T
        swapped = pltpu.roll(values, 64, 1)
        for half in range(2):
            slot = notes[2 * half : 2 * half + 1] * 128.0 + notes[2 * half + 1 : 2 * half + 2]
            info_ref[half : half + 1, lanes] = slot
            at = half * ROWS + m
            place = slot.astype(jnp.int32) & 1023
            hot[:, pl.ds(at, 128)] = hot_block(1024, place)
            both = jnp.where((lane < 64) == (half == 0), values, swapped)
            upper = tail[:, 2 * half : 2 * half + 1] >= 8.0
            right[pl.ds(at, 128), :] = jnp.where(upper == (lane >= 64), both, 0.0).astype(BF16)
        info_ref[2:4, lanes] = notes[4:6]
        info_ref[4:8, lanes] = jnp.zeros((4, 128), F32)
    for m in range(0, 1024, 256):
        clustered_ref[pl.ds(m, 256), :] = dot(hot[pl.ds(m, 256), :], right[...]).astype(BF16)


def to_clusters(arrived):
    return call(
        cluster_kernel,
        (
            jax.ShapeDtypeStruct((1024, 128), BF16),
            jax.ShapeDtypeStruct((8, ROWS), F32),
        ),
        [VMEM],
        (VMEM,) * 2,
        [pltpu.VMEM((1024, PANELS), BF16), pltpu.VMEM((PANELS, 128), BF16)],
        limit=8,
    )(arrived)


def coeff_kernel(table_ref, clustered_ref, v_hbm, big_hbm, out_hbm, basis, coeff, packed, sems):
    del big_hbm
    parts = [
        pltpu.make_async_copy(v_hbm.at[pl.ds(m, 32)], basis.at[pl.ds(m, 32)], sems.at[m // 32])
        for m in range(0, PAIRS, 32)
    ]
    for copy in parts:
        copy.start()
    weights = [clustered_ref[pl.ds(q * 256, 256), :] for q in range(4)]
    weights = [jnp.concatenate(weights[q : q + 2], axis=1) for q in (0, 2)]
    for q in range(4):
        coeff[q, pl.ds(PAIRS * RANK, RANK), :] = jnp.zeros((RANK, 128), F32)
    for m in range(0, PAIRS, 16):
        if m % 32 == 0:
            parts[m // 32].wait()
        rows = basis[pl.ds(m, 16)].reshape(16 * RANK, CL)
        at = pl.ds(m * RANK, 16 * RANK)
        for q in range(2):
            got = dot(rows, weights[q])
            coeff[2 * q, at, :] = got[:, :128]
            coeff[2 * q + 1, at, :] = got[:, 128:]
    lane = iota((RANK, 128), 1)

    def put(t, c):
        both = []
        for s in range(2):
            p = table_ref[s * OWNERS + t]
            col = table_ref[(4 + s) * OWNERS + t]
            tile = coeff[col & 3, pl.ds(pl.multiple_of(p * RANK, RANK), RANK), :]
            both.append(pltpu.roll(tile, ((col >> 2) ^ s) * 64, 1))
        both = jnp.where(lane < 64, both[0], both[1])
        packed[t, :, 0:128] = both[0:16].astype(BF16)
        packed[t, :, 128:256] = both[16:32].astype(BF16)
        return c

    lax.fori_loop(0, OWNERS, put, 0, unroll=8)
    load([(packed, out_hbm.at[:, 64:80, :])], sems)


def add_coeff(table, clustered, far_v, big):
    return pl.pallas_call(
        coeff_kernel,
        out_shape=jax.ShapeDtypeStruct((OWNERS, 80, CL), BF16),
        in_specs=[SMEM, VMEM, HBM, HBM],
        out_specs=HBM,
        scratch_shapes=[
            pltpu.VMEM((PAIRS, RANK, CL), BF16),
            pltpu.VMEM((4, PAIRS * RANK + RANK, 128), F32),
            pltpu.VMEM((OWNERS, 16, CL), BF16),
            pltpu.SemaphoreType.DMA((4,)),
        ],
        input_output_aliases={3: 0},
        compiler_params=pltpu.CompilerParams(vmem_limit_bytes=TIGHT * 2**20),
        cost_estimate=pl.CostEstimate(flops=0, bytes_accessed=32 * 2**20, transcendentals=0),
    )(table, clustered, far_v, big)


def near_kernel(
    rel_ref,
    before_ref,
    own_ref,
    after_ref,
    place_ref,
    blocks_ref,
    out_ref,
    hot_hbm,
    wide,
    hot,
    sems,
):
    c = pl.program_id(0)

    @pl.when(c == 0)
    def _():
        for k, ref in enumerate((before_ref, own_ref, after_ref)):
            for q in range(4):
                turned = ref[pl.ds(q * 256, 256), :].astype(F32).T.astype(BF16)
                wide[8 * k + q] = turned[0:64]
                wide[8 * k + 4 + q] = turned[64:128]

    lanes = pl.ds(pl.multiple_of(c * 256, 256), 256)
    hot[:, lanes] = hot_block(ROWS, place_ref[3:4, lanes])
    total = jnp.zeros((WAVES, CL), F32)
    for k in range(9):
        total += dot_nt(wide[rel_ref[c * 9 + k]], blocks_ref[0, k])
    out_ref[0] = total

    @pl.when(c == 7)
    def _():
        load([(hot, hot_hbm)], sems)


def near_product(relative, before, own, after, place, near_blocks):
    matrix = jax.ShapeDtypeStruct((1024, PANELS), BF16)
    return pl.pallas_call(
        near_kernel,
        out_shape=(jax.ShapeDtypeStruct((8, WAVES, CL), F32), matrix),
        grid_spec=pltpu.PrefetchScalarGridSpec(
            num_scalar_prefetch=1,
            grid=(8,),
            in_specs=[VMEM] * 4 + [pl.BlockSpec((1, 9, CL, CL), lambda c, r: (c, 0, 0, 0))],
            out_specs=(pl.BlockSpec((1, WAVES, CL), lambda c, r: (c, 0, 0)), HBM),
            scratch_shapes=[
                pltpu.VMEM((24, WAVES, CL), BF16),
                pltpu.VMEM((1024, PANELS), BF16),
                pltpu.SemaphoreType.DMA((1,)),
            ],
        ),
        compiler_params=pltpu.CompilerParams(vmem_limit_bytes=TIGHT * 2**20),
        cost_estimate=pl.CostEstimate(flops=0, bytes_accessed=512 * 2**20, transcendentals=0),
    )(relative, before, own, after, place, near_blocks)


def total_kernel(big_ref, near_ref, info_ref, out_hbm, hot, acc, masked, grid, out, out_sems):
    spread = ((iota((128, 256), 0) >> 3) == (iota((128, 256), 1) >> 4)) & (
        (iota((128, 256), 0) & 7) == 0
    )
    spread = spread.astype(F32).astype(BF16)
    for m in range(8):
        src = pl.ds(m * 16, 16)
        at = pl.ds(m * 256, 256)
        rows = dot(info_ref[:, pl.ds(m * 128, 128)].astype(BF16), spread)
        for part in range(2):
            mine = big_ref[src, 64:80, pl.ds(part * 128, 128)].reshape(256, 128)
            turned = mine.astype(F32).T.astype(BF16)
            for s in range(2):
                for cluster in range(8):
                    hit = (rows[2 + s : 3 + s] == float(cluster)).astype(F32).astype(BF16)
                    values = turned[s * 64 : s * 64 + 64] * hit
                    masked[2 * s + part, pl.ds(cluster * 64, 64), at] = values
    basis = [big_ref[:, pl.ds(16 * n, 16), :].reshape(2048, CL) for n in range(4)]
    for r in range(0, 512, 256):
        at = pl.ds(r, 256)
        product = dot(masked[0, at, :], basis[0])
        for n in range(1, 4):
            product += dot(masked[n, at, :], basis[n])
        acc[at, :] = product
    for half in range(2):
        for m in range(0, ROWS, 128):
            slot = info_ref[half : half + 1, pl.ds(m, 128)].astype(jnp.int32)
            hot[:, pl.ds(half * ROWS + m, 128)] = hot_block(1024, slot & 1023)
    for cluster in range(8):
        total = near_ref[cluster] + acc[pl.ds(cluster * 64, 64), :]
        grid[pl.ds((cluster >> 2) * 64, 64), pl.ds((cluster & 3) * 256, 256)] = total.astype(BF16)
    stores = []
    for m in range(0, ROWS, 256):
        at = pl.ds(m, 256)
        halves = []
        for half in range(2):
            got = dot(grid[...], hot[:, pl.ds(half * ROWS + m, 256)])
            upper = info_ref[half : half + 1, at] >= 1024.0
            halves.append(jnp.where(upper, got[64:128], got[0:64]))
        out[at, :] = jnp.concatenate(halves, axis=0).T.astype(BF16)
        stores.append(pltpu.make_async_copy(out.at[at], out_hbm.at[at], out_sems.at[m // 256]))
        stores[-1].start()
    for copy in stores:
        copy.wait()


def total_home(big, near, info):
    return call(
        total_kernel,
        jax.ShapeDtypeStruct((ROWS, 128), BF16),
        [VMEM, VMEM, VMEM],
        HBM,
        [
            pltpu.VMEM((1024, PANELS), BF16),
            pltpu.VMEM((512, CL), F32),
            pltpu.VMEM((4, 512, 2048), BF16),
            pltpu.VMEM((128, 1024), BF16),
            pltpu.VMEM((ROWS, 128), BF16),
            pltpu.SemaphoreType.DMA((4,)),
        ],
        limit=24,
    )(big, near, info)


def potential_kernel(returned_ref, hot_ref, place_ref, out_ref, turned, wide):
    for m in range(0, ROWS, 128):
        turned[:, pl.ds(m, 128)] = returned_ref[pl.ds(m, 128), :].astype(F32).T.astype(BF16)
    for x in range(0, 16, 2):
        lanes = pl.ds(x * 128, 256)
        got = dot(turned[...], hot_ref[:, lanes])
        got = jnp.where(place_ref[0:1, lanes] == 1, got[64:128], got[0:64])
        wide[:, x, :] = got[:, :128]
        wide[:, x + 1, :] = got[:, 128:]
    out_ref[...] = wide[...].astype(BF16)


def panel_potential(returned, hot, place):
    return call(
        potential_kernel,
        jax.ShapeDtypeStruct((WAVES, 16, 128), BF16),
        [VMEM] * 3,
        VMEM,
        [pltpu.VMEM((128, ROWS), BF16), pltpu.VMEM((WAVES, 16, 128), F32)],
    )(returned, hot, place)


def exchange(x):
    return lax.all_to_all(x, BOTH, split_axis=0, concat_axis=0, tiled=True)


def ring(axis, step):
    size = lax.axis_size(axis)
    return [(i, (i + step) % size) for i in range(size)]


def swap(axis, first):
    size = lax.axis_size(axis)
    pairs = [(i, (i + 1) % size) for i in range(first, size, 2)]
    return pairs + [(j, i) for i, j in pairs]


def body(
    elevation,
    velocity_pot,
    surface_coef,
    panel_slot,
    near_blocks,
    near_cols,
    far_v,
    far_u,
    far_rows,
    far_cols,
):
    per_owner, clusters = 8, 1024
    me = lax.axis_index(BOTH)
    fields, plan, along_a, along_b, across_a, across_b = pack_edges(
        elevation, velocity_pot, panel_slot, far_rows, far_cols, surface_coef
    )
    along_a = lax.ppermute(along_a, "along", swap("along", 0))
    along_b = lax.ppermute(along_b, "along", swap("along", 1))
    across_a = lax.ppermute(across_a, "across", swap("across", 0))
    across_b = lax.ppermute(across_b, "across", swap("across", 1))
    hot, place, table = sender_order(plan)
    halo = (along_a, along_b, across_a, across_b)
    eta, payload = surface_payload(plan, fields, halo, hot, place, table)
    table = table.reshape(8 * 128)
    arrived = exchange(payload.reshape(OWNERS, 8, 256)).reshape(ROWS, 256)
    big = far_bucket(table, far_u)
    arrived, big = lax.optimization_barrier((arrived, big))

    clustered, info = to_clusters(arrived)
    before = lax.ppermute(clustered, BOTH, ring(BOTH, 1))
    after = lax.ppermute(clustered, BOTH, ring(BOTH, -1))
    big = add_coeff(table, clustered, far_v, big)
    after, before, big = lax.optimization_barrier((after, before, big))
    big = exchange(big)

    relative = (near_cols - (me * per_owner - per_owner)) % clusters
    near, hot = near_product(
        relative.reshape(72), before, clustered, after, place, near_blocks
    )

    home = total_home(big, near, info).reshape(OWNERS, 8, 128)
    returned = exchange(home).reshape(ROWS, 128)
    potential = panel_potential(returned, hot, place)
    return (eta, potential)


def solution(mesh):
    in_specs = (
        P(None, "along", "across"),
        P(None, "along", "across"),
        P("along", "across"),
        P("along", "across"),
        P(BOTH, None, None, None),
        P(BOTH, None),
        P(BOTH, None, None),
        P(BOTH, None, None),
        P(BOTH),
        P(BOTH),
    )
    out_specs = (P(None, "along", "across"), P(None, "along", "across"))
    return jax.shard_map(body, mesh=mesh, in_specs=in_specs, out_specs=out_specs, check_vma=False)
```
